256 devices in a mesh: ctx: 16 (over x, y_lo, core), tp: 16 (over z, y_hi).
Axes of the slice: x: 4, y: 4 (y_hi: 2, y_lo: 2; y = y_hi * 2 + y_lo), z: 8, core: 2. Of those that a mesh axis runs over, the one named last changes fastest.
Arguments:
- queries: bfloat16 [4096, 8192], P('ctx', 'tp'), may hold values from -5 to 5
- keys: bfloat16 [8, 4096, 128], P(None, 'ctx'), may hold values from -5 to 5
- values: bfloat16 [8, 4096, 128], P(None, 'ctx'), may hold values from -6 to 6
- d_out: bfloat16 [4096, 8192], P('ctx', 'tp'), may hold values from -6 to 6
- span_order: int32 [32], replicated, may hold values from 0 to 31, each once
- segments: int32 [4096], replicated, may hold values from 0 to 3, never falling along the last dimension, each value on 1 to 2048 neighbouring positions
Outputs:
- d_queries: bfloat16 [4096, 8192], P('ctx', 'tp')
- d_keys: float32 [8, 4096, 128], P(None, 'ctx')
- d_values: float32 [8, 4096, 128], P(None, 'ctx')
The draws below stay inside these ranges and needn't reach their ends.
Inputs may be any that keep to these rules, and one draw needn't show every extreme that they name: `span_order`: each number once. `segments`: never falling along positions.
All inputs are finite; a program needn't handle non-finite values.
Results may differ from the reference program's by a relative error of at most 0.015.
Values may be sent and summed in bfloat16 or wider, within the bound.
A program may use at most 64 MiB of HBM per device.

```python
import math
import jax
import jax.numpy as jnp
import numpy as np
from jax import lax

HD = 128
GROUP = 8
TOK_DEV = 256
HEADS = 64
KVH = 8
TOKENS = 4096
N_CTX = 16


def draw_queries(key, part):
    key = jax.random.fold_in(key, 1)
    base = jnp.clip(jax.random.normal(key, (TOKENS, HEADS * HD), jnp.float32), -5.0, 5.0)
    return base.astype(jnp.bfloat16)


def draw_keys(key, part):
    key = jax.random.fold_in(key, 2)
    base = jnp.clip(jax.random.normal(key, (KVH, TOKENS, HD), jnp.float32), -5.0, 5.0)
    return base.astype(jnp.bfloat16)


def level_of(key, extent, shards, smallest, high):
    factor_of, own = 1.0, jax.random.fold_in(key, 6)
    for axis_at, shards_of in shards:
        steps = jnp.exp(jax.random.uniform(jax.random.fold_in(own, axis_at), (shards_of,), jnp.float32, smallest / len(shards), high / len(shards)))
        factor_of = factor_of * jnp.repeat(steps, extent[axis_at] // shards_of).reshape([-1 if axis == axis_at else 1 for axis in range(len(extent))])
    return factor_of


def split_up(number_of, total, limit, skew):
    weights = [(1 << 20) // math.isqrt(rank ** skew) + 1 for rank in range(2, number_of + 1)]
    spare, given = total - limit - (number_of - 1), [1] * (number_of - 1)
    while spare > 0:
        free = [i for i in range(number_of - 1) if given[i] < limit]
        pool, remaining = sum([weights[i] for i in free]), spare
        for i in free:
            more = min(limit - given[i], max(1, remaining * weights[i] // pool), spare)
            given[i] = given[i] + more
            spare = spare - more
    return np.array([limit] + given)


def ragged(rng, number_of, total, reach, skew):
    if number_of == 2:
        one = jax.random.randint(rng, (), max(1, total - reach), min(reach, total - 1) + 1)
        return jnp.stack([one, total - one])
    tallies = jnp.asarray(split_up(number_of, total, reach, skew), jnp.int32)
    couples = (number_of - 1) // 2
    giver, receiver = tallies[1:1 + 2 * couples:2], tallies[2:2 + 2 * couples:2]
    room = jnp.minimum(giver - 1, reach - receiver)
    shifted = jax.random.randint(jax.random.fold_in(rng, 1), (couples,), 0, 1 << 20) % (room + 1)
    tallies = tallies.at[1:1 + 2 * couples:2].set(giver - shifted).at[2:2 + 2 * couples:2].set(receiver + shifted)
    return tallies[jax.random.permutation(jax.random.fold_in(rng, 2), number_of)]


def bell_draw(rng, dims, deviation, bound, pieces=(), held_as=jnp.bfloat16):
    result = jax.random.normal(rng, dims, jnp.float32) * deviation
    if len(pieces) > 0:
        result = level_of(rng, dims, pieces, -0.22, 0.18) * result
    return jnp.clip(result, min=-bound, max=bound).astype(held_as)


def setup_inputs(seed: int = 0) -> dict:
    key_list = jax.random.split(jax.random.key(seed), 7)
    return {
        "queries": draw_queries(jax.random.fold_in(key_list[6], 71), 0),
        "keys": draw_keys(jax.random.fold_in(key_list[6], 71), 0),
        "values": bell_draw(key_list[2], (KVH, TOKENS, HD), 1.0, 6.0, ((1, 16),)),
        "d_out": bell_draw(key_list[3], (TOKENS, HEADS * HD), 1.0, 6.0, ((0, 16), (1, 16))),
        "span_order": jax.random.permutation(key_list[4], 2 * N_CTX).astype(jnp.int32),
        "segments": jnp.searchsorted(jnp.cumsum(ragged(key_list[5], 4, TOKENS, TOKENS // 2, 0)), jnp.arange(TOKENS), side="right").astype(jnp.int32),
    }


def reference(queries, keys, values, d_out, span_order, segments):
    span = TOK_DEV // 2
    rows = jnp.arange(TOKENS, dtype=jnp.int32)
    pos = (span_order[rows // span] * span + rows % span).astype(jnp.int32)
    seg = segments[pos]
    allowed = (pos[None, :] <= pos[:, None]) & (seg[None, :] == seg[:, None])
    scale = HD ** -0.5
    query_heads = jnp.transpose(queries.reshape(TOKENS, HEADS, HD), (1, 0, 2))
    grad_heads = jnp.transpose(d_out.reshape(TOKENS, HEADS, HD), (1, 0, 2))
    head_ids = jnp.arange(HEADS, dtype=jnp.int32)

    def one_head(item):
        query_h, grad_h, head = item
        kv_index = head // GROUP
        key_h = keys[kv_index]
        value_h = values[kv_index]
        scores = jnp.dot(query_h, key_h.T, preferred_element_type=jnp.float32) * scale
        scores = jnp.where(allowed, scores, -1e30)
        top = jnp.max(scores, axis=1, keepdims=True)
        lse = top + jnp.log(jnp.sum(jnp.exp(scores - top), axis=1, keepdims=True))
        probs = jnp.exp(scores - lse)
        probs16 = probs.astype(jnp.bfloat16)
        output = jnp.dot(probs16, value_h, preferred_element_type=jnp.float32)
        delta = jnp.sum(grad_h.astype(jnp.float32) * output, axis=1, keepdims=True)
        dprobs = jnp.dot(grad_h, value_h.T, preferred_element_type=jnp.float32)
        dscores = (probs * (dprobs - delta)).astype(jnp.bfloat16)
        dquery = (jnp.dot(dscores, key_h, preferred_element_type=jnp.float32) * scale).astype(jnp.bfloat16)
        dkey = jnp.dot(dscores.T, query_h, preferred_element_type=jnp.float32) * scale
        dvalue = jnp.dot(probs16.T, grad_h, preferred_element_type=jnp.float32)
        return dquery, dkey, dvalue

    dquery, dkey, dvalue = lax.map(one_head, (query_heads, grad_heads, head_ids))
    d_queries = jnp.transpose(dquery, (1, 0, 2)).reshape(TOKENS, HEADS * HD)
    d_keys = jnp.sum(dkey.reshape(KVH, GROUP, TOKENS, HD), axis=1)
    d_values = jnp.sum(dvalue.reshape(KVH, GROUP, TOKENS, HD), axis=1)
    return d_queries, d_keys, d_values
```

```python
import functools

import jax
import jax.numpy as jnp
from jax import lax
from jax.experimental import pallas as pl
from jax.experimental.pallas import tpu as pltpu
from jax.sharding import PartitionSpec as P

HD = 128
BLK = 128
HEADS_DEV = 4
COLS = HEADS_DEV * BLK
WIN = 17
NEGATIVE = -1e30
SCALE = HD**-0.5
LOG2E = 1.4426950408889634
BF = jnp.bfloat16
F32 = jnp.float32


class Place:
    def __init__(self):
        self.ctx = lax.axis_index("ctx")
        self.tp = lax.axis_index("tp")
        self.x = self.ctx // 4
        self.ylo = (self.ctx // 2) % 2
        self.core = self.ctx % 2
        self.z = self.tp // 2
        self.yhi = self.tp % 2
        self.y = self.yhi * 2 + self.ylo

    def at(self, dx=0, dy=0, dc=0, dz=0):
        x = (self.x + dx + 4) % 4
        y = (self.y + dy + 4) % 4
        c = (self.core + dc) % 2
        z = (self.z + dz + 8) % 8
        return (x * 4 + (y % 2) * 2 + c, z * 2 + y // 2)

    def block(self, dx=0, dy=0, dc=0):
        return ((self.x + dx + 4) % 4) * 4 + ((self.ylo + dy) % 2) * 2 + (self.core + dc) % 2


class Mail:
    def __init__(self, send, recv):
        self.send, self.recv, self.used, self.out = send, recv, 0, []

    def post(self, src, dst, device):
        copy = pltpu.make_async_remote_copy(
            src_ref=src,
            dst_ref=dst,
            send_sem=self.send.at[self.used],
            recv_sem=self.recv.at[self.used],
            device_id=device,
            device_id_type=pl.DeviceIdType.MESH,
        )
        self.used += 1
        copy.start()
        self.out.append(copy)
        return copy

    def drain(self):
        for copy in self.out:
            copy.wait_send()
        self.out = []


def greet(devices):
    barrier = pltpu.get_barrier_semaphore()
    for device in devices:
        pl.semaphore_signal(
            barrier, inc=1, device_id=device, device_id_type=pl.DeviceIdType.MESH
        )
    pl.semaphore_wait(barrier, len(devices))


def gather_phase(me, mail, k_ref, v_ref, kbuf, vbuf, local_sem):
    own = me.block()
    src = (k_ref.at[me.z], v_ref.at[me.z])
    buf = (kbuf, vbuf)

    def at(kind, block):
        return buf[kind].at[pl.ds(2 * block, 2)]

    def forward(kind, block, device):
        return mail.post(at(kind, block), at(kind, block), device)

    local = []
    for kind in range(2):
        copy = pltpu.make_async_copy(src[kind], at(kind, own), local_sem.at[kind])
        copy.start()
        local.append(copy)
    ydir = (1, -1)
    xp, xm, y0, s0 = [], [], [], []
    for kind in range(2):
        xp.append(mail.post(src[kind], at(kind, own), me.at(dx=1)))
        xm.append(mail.post(src[kind], at(kind, own), me.at(dx=-1)))
        y0.append(mail.post(src[kind], at(kind, own), me.at(dy=ydir[kind])))
    for kind in range(2):
        s0.append(mail.post(src[kind], at(kind, own), me.at(dc=1)))
    x2, sib, yfar = [None, None], [], []
    for kind in range(2):
        xp[kind].wait_recv()
        block = me.block(dx=-1)
        if kind == 0:
            x2[0] = forward(0, block, me.at(dx=1))
        yfar.append((kind, -1, forward(kind, block, me.at(dy=ydir[kind]))))
        sib.append(forward(kind, block, me.at(dc=1)))
        xm[kind].wait_recv()
        block = me.block(dx=1)
        if kind == 1:
            x2[1] = forward(1, block, me.at(dx=-1))
        yfar.append((kind, 1, forward(kind, block, me.at(dy=ydir[kind]))))
        sib.append(forward(kind, block, me.at(dc=1)))
    for kind in range(2):
        y0[kind].wait_recv()
        sib.append(forward(kind, me.block(dy=1), me.at(dc=1)))
    for kind in range(2):
        x2[kind].wait_recv()
        block = me.block(dx=2)
        yfar.append((kind, 2, forward(kind, block, me.at(dy=ydir[kind]))))
        sib.append(forward(kind, block, me.at(dc=1)))
    for kind, dx, copy in yfar:
        copy.wait_recv()
        sib.append(forward(kind, me.block(dx=dx, dy=1), me.at(dc=1)))
    for copy in local:
        copy.wait()
    for copy in s0 + sib:
        copy.wait_recv()
    mail.drain()


CHUNKS = ((0, 6), (6, 12), (12, 17))


def compute_phase(
    ctx, q_ref, do_ref, kbuf, vbuf, span_ref, seg_ref, dq_ref, terms,
    inv, qs, ds_rows, kg, vg, s_scr, dp_scr, p_scr, ds_scr,
):
    for j in range(32):
        found = jnp.int32(0)
        for s in range(32):
            found = found + jnp.where(span_ref[s] == j, s, 0)
        inv[j] = found
    seg_all = seg_ref[...]
    counts = [jnp.sum(jnp.where(seg_all == v, 1.0, 0.0)) for v in range(3)]
    zero = jnp.zeros((BLK, COLS), BF)
    c2 = SCALE * LOG2E

    for u in range(2):
        p = span_ref[2 * ctx + u]
        p_scr[u, WIN] = zero
        ds_scr[u, WIN] = zero
        for h in range(HEADS_DEV):
            qs[u, pl.ds(h * BLK, BLK), :] = q_ref[pl.ds(u * BLK, BLK), pl.ds(h * HD, HD)]
            ds_rows[u, pl.ds(h * BLK, BLK), :] = do_ref[pl.ds(u * BLK, BLK), pl.ds(h * HD, HD)]
        for t in range(WIN):
            j = jnp.maximum(p - (WIN - 1) + t, 0)
            s = inv[j]
            kg[pl.ds(t * BLK, BLK), :] = kbuf[s]
            vg[pl.ds(t * BLK, BLK), :] = vbuf[s]
        seg_row = seg_ref[pl.ds(p, 1), :]
        start = jnp.zeros((1, BLK), F32)
        for v in range(3):
            start = start + jnp.where(seg_row > v, counts[v], 0.0)
        first = (p - (WIN - 1)) * BLK
        start = start - first.astype(F32)
        start2 = jnp.concatenate([start, start], axis=1)
        cols2 = lax.broadcasted_iota(jnp.int32, (BLK, 2 * BLK), 1) % BLK
        rows2 = lax.broadcasted_iota(jnp.int32, (BLK, 2 * BLK), 0)
        causal = rows2 <= cols2
        rows_f = rows2.astype(F32)

        for hp in range(2):
            wide = pl.ds(hp * 256, 256)
            q2 = qs[u, wide, :]
            do2 = ds_rows[u, wide, :]
            top = jnp.full((8, 256), NEGATIVE, F32)
            for t0, t1 in CHUNKS:
                rows = pl.ds(t0 * BLK, (t1 - t0) * BLK)
                sc = lax.dot_general(
                    kg[rows, :], q2, (((1,), (1,)), ((), ())), preferred_element_type=F32
                )
                for t in range(t0, t1):
                    tile = sc[(t - t0) * BLK : (t - t0 + 1) * BLK]
                    ok = rows_f >= start2 - float(t * BLK)
                    if t == WIN - 1:
                        ok = ok & causal
                    tile = jnp.where(ok, tile * c2, NEGATIVE)
                    s_scr[pl.ds(t * BLK, BLK), wide] = tile
                    top = jnp.maximum(top, jnp.max(tile.reshape(16, 8, 256), axis=0))
            top = jnp.max(top, axis=0, keepdims=True)
            norm = jnp.zeros((8, 256), F32)
            mixed = jnp.zeros((8, 256), F32)
            for t0, t1 in CHUNKS:
                rows = pl.ds(t0 * BLK, (t1 - t0) * BLK)
                dp = lax.dot_general(
                    vg[rows, :], do2, (((1,), (1,)), ((), ())), preferred_element_type=F32
                )
                for t in range(t0, t1):
                    tile = pl.ds(t * BLK, BLK)
                    dpt = dp[(t - t0) * BLK : (t - t0 + 1) * BLK]
                    pt = jnp.exp2(s_scr[tile, wide] - top)
                    s_scr[tile, wide] = pt
                    dp_scr[tile, wide] = dpt
                    norm = norm + jnp.sum(pt.reshape(16, 8, 256), axis=0)
                    mixed = mixed + jnp.sum((pt * dpt).reshape(16, 8, 256), axis=0)
            inv_norm = 1.0 / jnp.sum(norm, axis=0, keepdims=True)
            delta = jnp.sum(mixed, axis=0, keepdims=True) * inv_norm
            dqt = jnp.zeros((HD, 256), F32)
            for t0, t1 in CHUNKS:
                for t in range(t0, t1):
                    tile = pl.ds(t * BLK, BLK)
                    prob = s_scr[tile, wide] * inv_norm
                    p_scr[u, t, :, wide] = prob.astype(BF)
                    ds_scr[u, t, :, wide] = (prob * (dp_scr[tile, wide] - delta)).astype(BF)
                rows = pl.ds(t0 * BLK, (t1 - t0) * BLK)
                dsc = ds_scr[u, pl.ds(t0, t1 - t0), :, wide].reshape((t1 - t0) * BLK, 256)
                dqt = dqt + lax.dot_general(
                    kg[rows, :], dsc, (((0,), (0,)), ((), ())), preferred_element_type=F32
                )
            for i in range(2):
                piece = (dqt[:, i * BLK : (i + 1) * BLK] * SCALE).T
                dq_ref[pl.ds(u * BLK, BLK), pl.ds((2 * hp + i) * HD, HD)] = piece.astype(BF)

    base = [span_ref[2 * ctx + u] - (WIN - 1) for u in range(2)]

    @pl.loop(0, 4)
    def _(xx):
        picks = []
        for s in range(8):
            where = span_ref[xx * 8 + s]
            pick = []
            for u in range(2):
                t = where - base[u]
                pick.append(jnp.where((t >= 0) & (t < WIN), t, WIN))
            picks.append(pick)
        for kind, source, weights in ((0, ds_scr, qs), (1, p_scr, ds_rows)):
            total = None
            for u in range(2):
                left = jnp.concatenate([source[u, picks[s][u]] for s in range(8)], axis=0)
                part = jnp.dot(left, weights[u], preferred_element_type=F32)
                total = part if total is None else total + part
            if kind == 0:
                total = total * SCALE
            terms[kind, xx] = total.astype(BF).reshape(2, 2, 2, BLK, HD)


def add_into(dst, *srcs):
    total = dst[...].astype(F32)
    for src in srcs:
        total = total + src[...].astype(F32)
    dst[...] = total.astype(BF)


def reduce_phase(me, mail, terms, part, r0, ra1, ra2, rb1, rb2, rc1, rc2, rd1, rd2, result):
    half = mail.post(terms.at[:, :, :, 1 - me.core], r0, me.at(dc=1))
    half.wait_recv()
    for kind in range(2):
        for xx in range(4):
            part[kind, xx] = (
                terms[kind, xx, :, me.core].astype(F32) + r0[kind, xx].astype(F32)
            ).astype(BF)
    x, y, ylo, yhi = me.x, me.y, me.ylo, me.yhi
    xp, xm, xo = (x + 1) % 4, (x + 3) % 4, (x + 2) % 4
    yp, ym = (y + 1) % 4, (y + 3) % 4
    hp, hm, ho = yp // 2, ym // 2, 1 - yhi
    lo = 1 - ylo
    a1p = mail.post(part.at[0, xo, :, 0], ra1.at[0], me.at(dx=1))
    a1m = mail.post(part.at[1, xo, :, 0], ra1.at[1], me.at(dx=-1))
    b1p = mail.post(part.at[ho, pl.ds(0, 2), ylo, 1], rb1.at[0], me.at(dy=1))
    b1m = mail.post(part.at[ho, pl.ds(2, 2), ylo, 1], rb1.at[1], me.at(dy=-1))
    a1p.wait_recv()
    add_into(part.at[0, xp, :, 0], ra1.at[0])
    a2p = mail.post(part.at[:, xp, :, 0], ra2.at[0], me.at(dx=1))
    a1m.wait_recv()
    add_into(part.at[1, xm, :, 0], ra1.at[1])
    a2m = mail.post(part.at[:, xm, :, 0], ra2.at[1], me.at(dx=-1))
    b1p.wait_recv()
    add_into(part.at[hp, pl.ds(0, 2), lo, 1], rb1.at[0])
    b2p = mail.post(part.at[hp, :, lo, 1], rb2.at[0], me.at(dy=1))
    b1m.wait_recv()
    add_into(part.at[hm, pl.ds(2, 2), lo, 1], rb1.at[1])
    b2m = mail.post(part.at[hm, :, lo, 1], rb2.at[1], me.at(dy=-1))
    a2p.wait_recv()
    a2m.wait_recv()
    add_into(part.at[:, x, :, 0], ra2.at[0], ra2.at[1])
    c1p = mail.post(part.at[ho, x, ylo, 0, pl.ds(0, 64)], rc1.at[0], me.at(dy=1))
    c1m = mail.post(part.at[ho, x, ylo, 0, pl.ds(64, 64)], rc1.at[1], me.at(dy=-1))
    b2p.wait_recv()
    b2m.wait_recv()
    add_into(part.at[yhi, :, ylo, 1], rb2.at[0], rb2.at[1])
    d1p = mail.post(part.at[yhi, xo, ylo, 1, pl.ds(0, 64)], rd1.at[0], me.at(dx=1))
    d1m = mail.post(part.at[yhi, xo, ylo, 1, pl.ds(64, 64)], rd1.at[1], me.at(dx=-1))
    c1p.wait_recv()
    add_into(part.at[hp, x, lo, 0, pl.ds(0, 64)], rc1.at[0])
    c2p = mail.post(part.at[hp, x, lo, 0], rc2.at[0], me.at(dy=1))
    c1m.wait_recv()
    add_into(part.at[hm, x, lo, 0, pl.ds(64, 64)], rc1.at[1])
    c2m = mail.post(part.at[hm, x, lo, 0], rc2.at[1], me.at(dy=-1))
    d1p.wait_recv()
    add_into(part.at[yhi, xp, ylo, 1, pl.ds(0, 64)], rd1.at[0])
    d2p = mail.post(part.at[yhi, xp, ylo, 1], rd2.at[0], me.at(dx=1))
    d1m.wait_recv()
    add_into(part.at[yhi, xm, ylo, 1, pl.ds(64, 64)], rd1.at[1])
    d2m = mail.post(part.at[yhi, xm, ylo, 1], rd2.at[1], me.at(dx=-1))

    def owned(h, copies, parts):
        for copy in copies:
            copy.wait_recv()
        total = part[yhi, x, ylo, h].astype(F32)
        for piece in parts:
            total = total + piece[...].astype(F32)
        result[yhi, me.z, h] = total.astype(BF)

    owned(0, (c2p, c2m), (rc2.at[0], rc2.at[1]))
    owned(1, (d2p, d2m), (rd2.at[0], rd2.at[1]))

    z = me.z
    kinds = (yhi, 1 - yhi)

    def spot(k, dz):
        return result.at[kinds[k], (z + dz + 8) % 8]

    def pass_on(k, dz, step):
        return mail.post(spot(k, dz), spot(k, dz), me.at(dz=step))

    up, down = [None, None], [None, None]
    up[0], down[0] = pass_on(0, 0, 1), pass_on(0, 0, -1)
    swap = mail.post(spot(0, 0), spot(0, 0), me.at(dy=2))
    swap.wait_recv()
    up[1], down[1] = pass_on(1, 0, 1), pass_on(1, 0, -1)
    last = []
    for hop in range(1, 4):
        for k in range(2):
            up[k].wait_recv()
            if hop < 3 or k == 0:
                up[k] = pass_on(k, -hop, 1)
            down[k].wait_recv()
            if hop < 3 or k == 1:
                down[k] = pass_on(k, hop, -1)
    up[0].wait_recv()
    down[1].wait_recv()
    mail.drain()


VMEM = pl.BlockSpec(memory_space=pltpu.VMEM)
SMEM = pl.BlockSpec(memory_space=pltpu.SMEM)
ANY = pl.BlockSpec(memory_space=pl.ANY)
LIMIT = 56 * 2**20


def gather_kernel(k_ref, v_ref, kbuf, vbuf, send, recv, local_sem):
    me = Place()
    greet([me.at(dx=1), me.at(dx=-1), me.at(dy=1), me.at(dy=-1), me.at(dc=1)])
    gather_phase(me, Mail(send, recv), k_ref, v_ref, kbuf, vbuf, local_sem)


def compute_kernel(q, do, kb, vb, span, seg, dq, terms, *scratch):
    compute_phase(lax.axis_index("ctx"), q, do, kb, vb, span, seg, dq, terms, *scratch)


def reduce_kernel(terms, result, send, recv, *scratch):
    me = Place()
    greet(
        [me.at(dx=1), me.at(dx=-1), me.at(dy=1), me.at(dy=-1), me.at(dc=1)]
        + [me.at(dy=2), me.at(dz=1), me.at(dz=-1)]
    )
    reduce_phase(me, Mail(send, recv), terms, *scratch, result)


def per_device(queries, keys, values, d_out, span_order, segments):
    keys = keys.reshape(8, 2, BLK, HD)
    values = values.reshape(8, 2, BLK, HD)
    kb, vb = pl.pallas_call(
        gather_kernel,
        out_shape=[jax.ShapeDtypeStruct((32, BLK, HD), BF)] * 2,
        in_specs=[ANY, ANY],
        out_specs=[VMEM, VMEM],
        scratch_shapes=[
            pltpu.SemaphoreType.DMA((32,)),
            pltpu.SemaphoreType.DMA((32,)),
            pltpu.SemaphoreType.DMA((2,)),
        ],
        compiler_params=pltpu.CompilerParams(
            collective_id=0, has_side_effects=True, vmem_limit_bytes=LIMIT
        ),
        name="gather",
    )(keys, values)
    dq, terms = pl.pallas_call(
        compute_kernel,
        out_shape=[
            jax.ShapeDtypeStruct((256, 512), BF),
            jax.ShapeDtypeStruct((2, 4, 2, 2, 2, BLK, HD), BF),
        ],
        in_specs=[VMEM, VMEM, VMEM, VMEM, SMEM, VMEM],
        out_specs=[VMEM, VMEM],
        scratch_shapes=[
            pltpu.SMEM((32,), jnp.int32),
            pltpu.VMEM((2, COLS, HD), BF),
            pltpu.VMEM((2, COLS, HD), BF),
            pltpu.VMEM((WIN * BLK, HD), BF),
            pltpu.VMEM((WIN * BLK, HD), BF),
            pltpu.VMEM((WIN * BLK, COLS), F32),
            pltpu.VMEM((WIN * BLK, COLS), F32),
            pltpu.VMEM((2, WIN + 1, BLK, COLS), BF),
            pltpu.VMEM((2, WIN + 1, BLK, COLS), BF),
        ],
        compiler_params=pltpu.CompilerParams(vmem_limit_bytes=LIMIT),
        name="attend",
    )(queries, d_out, kb, vb, span_order, segments.reshape(32, BLK))
    result = pl.pallas_call(
        reduce_kernel,
        out_shape=jax.ShapeDtypeStruct((2, 8, 2, BLK, HD), BF),
        in_specs=[VMEM],
        out_specs=VMEM,
        scratch_shapes=[
            pltpu.SemaphoreType.DMA((40,)),
            pltpu.SemaphoreType.DMA((40,)),
            pltpu.VMEM((2, 4, 2, 2, BLK, HD), BF),
            pltpu.VMEM((2, 4, 2, 2, BLK, HD), BF),
            pltpu.VMEM((2, 2, BLK, HD), BF),
            pltpu.VMEM((2, 2, 2, BLK, HD), BF),
            pltpu.VMEM((2, 2, BLK, HD), BF),
            pltpu.VMEM((2, 4, BLK, HD), BF),
            pltpu.VMEM((2, 64, HD), BF),
            pltpu.VMEM((2, BLK, HD), BF),
            pltpu.VMEM((2, 64, HD), BF),
            pltpu.VMEM((2, BLK, HD), BF),
        ],
        compiler_params=pltpu.CompilerParams(
            collective_id=1, has_side_effects=True, vmem_limit_bytes=LIMIT
        ),
        name="reduce",
    )(terms)
    result = result.reshape(2, 8, 256, HD).astype(F32)
    return (dq, result[0], result[1])


def solution(mesh):
    return jax.shard_map(
        per_device,
        mesh=mesh,
        in_specs=(
            P("ctx", "tp"),
            P(None, "ctx", None),
            P(None, "ctx", None),
            P("ctx", "tp"),
            P(),
            P(),
        ),
        out_specs=(P("ctx", "tp"), P(None, "ctx", None), P(None, "ctx", None)),
        check_vma=False,
    )
```

```python
import functools

import jax
import jax.numpy as jnp
from jax import lax
from jax.experimental import pallas as pl
from jax.experimental.pallas import tpu as pltpu
from jax.sharding import PartitionSpec as P

HD = 128
BLK = 128
HEADS_DEV = 4
COLS = HEADS_DEV * BLK
WIN = 17
NEGATIVE = -1e30
SCALE = HD**-0.5
LOG2E = 1.4426950408889634
BF = jnp.bfloat16
F32 = jnp.float32


class Place:
    def __init__(self):
        self.ctx = lax.axis_index("ctx")
        self.tp = lax.axis_index("tp")
        self.x = self.ctx // 4
        self.ylo = (self.ctx // 2) % 2
        self.core = self.ctx % 2
        self.z = self.tp // 2
        self.yhi = self.tp % 2
        self.y = self.yhi * 2 + self.ylo

    def at(self, dx=0, dy=0, dc=0, dz=0):
        x = (self.x + dx + 4) % 4
        y = (self.y + dy + 4) % 4
        c = (self.core + dc) % 2
        z = (self.z + dz + 8) % 8
        return (x * 4 + (y % 2) * 2 + c, z * 2 + y // 2)

    def block(self, dx=0, dy=0, dc=0):
        return ((self.x + dx + 4) % 4) * 4 + ((self.ylo + dy) % 2) * 2 + (self.core + dc) % 2


class Mail:
    def __init__(self, send, recv):
        self.send, self.recv, self.used, self.out = send, recv, 0, []

    def post(self, src, dst, device):
        copy = pltpu.make_async_remote_copy(
            src_ref=src,
            dst_ref=dst,
            send_sem=self.send.at[self.used],
            recv_sem=self.recv.at[self.used],
            device_id=device,
            device_id_type=pl.DeviceIdType.MESH,
        )
        self.used += 1
        copy.start()
        self.out.append(copy)
        return copy

    def drain(self):
        for copy in self.out:
            copy.wait_send()
        self.out = []


def greet(devices):
    barrier = pltpu.get_barrier_semaphore()
    for device in devices:
        pl.semaphore_signal(
            barrier, inc=1, device_id=device, device_id_type=pl.DeviceIdType.MESH
        )
    pl.semaphore_wait(barrier, len(devices))


def gather_phase(me, mail, k_ref, v_ref, kbuf, vbuf, local_sem, meanwhile):
    own = me.block()
    src = (k_ref.at[me.z], v_ref.at[me.z])
    buf = (kbuf, vbuf)

    def at(kind, block):
        return buf[kind].at[pl.ds(2 * block, 2)]

    def forward(kind, block, device):
        return mail.post(at(kind, block), at(kind, block), device)

    local = []
    for kind in range(2):
        copy = pltpu.make_async_copy(src[kind], at(kind, own), local_sem.at[kind])
        copy.start()
        local.append(copy)
    ydir = (1, -1)
    xp, xm, y0, s0 = [], [], [], []
    for kind in range(2):
        xp.append(mail.post(src[kind], at(kind, own), me.at(dx=1)))
        xm.append(mail.post(src[kind], at(kind, own), me.at(dx=-1)))
        y0.append(mail.post(src[kind], at(kind, own), me.at(dy=ydir[kind])))
    for kind in range(2):
        s0.append(mail.post(src[kind], at(kind, own), me.at(dc=1)))
    meanwhile()
    x2, sib, yfar = [None, None], [], []
    for kind in range(2):
        xp[kind].wait_recv()
        block = me.block(dx=-1)
        if kind == 0:
            x2[0] = forward(0, block, me.at(dx=1))
        yfar.append((kind, -1, forward(kind, block, me.at(dy=ydir[kind]))))
        sib.append(forward(kind, block, me.at(dc=1)))
        xm[kind].wait_recv()
        block = me.block(dx=1)
        if kind == 1:
            x2[1] = forward(1, block, me.at(dx=-1))
        yfar.append((kind, 1, forward(kind, block, me.at(dy=ydir[kind]))))
        sib.append(forward(kind, block, me.at(dc=1)))
    for kind in range(2):
        y0[kind].wait_recv()
        sib.append(forward(kind, me.block(dy=1), me.at(dc=1)))
    for kind in range(2):
        x2[kind].wait_recv()
        block = me.block(dx=2)
        yfar.append((kind, 2, forward(kind, block, me.at(dy=ydir[kind]))))
        sib.append(forward(kind, block, me.at(dc=1)))
    for kind, dx, copy in yfar:
        copy.wait_recv()
        sib.append(forward(kind, me.block(dx=dx, dy=1), me.at(dc=1)))
    for copy in local:
        copy.wait()
    for copy in s0 + sib:
        copy.wait_recv()


CHUNKS = ((0, 6), (6, 12), (12, 17))


def prepare(span_ref, seg_ref, q_ref, do_ref, inv, qs, ds_rows, p_scr, ds_scr):
    for j in range(32):
        found = jnp.int32(0)
        for s in range(32):
            found = jnp.where(span_ref[s] == j, s, found)
        inv[j] = found
    zero = jnp.zeros((BLK, COLS), BF)
    for u in range(2):
        p_scr[u, WIN] = zero
        ds_scr[u, WIN] = zero
        for h in range(HEADS_DEV):
            qs[u, pl.ds(h * BLK, BLK), :] = q_ref[pl.ds(u * BLK, BLK), pl.ds(h * HD, HD)]
            ds_rows[u, pl.ds(h * BLK, BLK), :] = do_ref[pl.ds(u * BLK, BLK), pl.ds(h * HD, HD)]


def attend(
    ctx, kbuf, vbuf, span_ref, seg_ref, inv, qs, ds_rows, kg, vg, s_scr, dp_scr, p_scr, ds_scr
):
    seg_all = seg_ref[...]
    counts = [jnp.sum(jnp.where(seg_all == v, 1.0, 0.0)) for v in range(3)]
    c2 = SCALE * LOG2E
    cols2 = lax.broadcasted_iota(jnp.int32, (BLK, 2 * BLK), 1) % BLK
    rows2 = lax.broadcasted_iota(jnp.int32, (BLK, 2 * BLK), 0)
    causal = rows2 <= cols2
    rows_f = rows2.astype(F32)
    for u in range(2):
        p = span_ref[2 * ctx + u]
        for t in range(WIN):
            j = jnp.maximum(p - (WIN - 1) + t, 0)
            s = inv[j]
            kg[u, pl.ds(t * BLK, BLK), :] = kbuf[s]
            vg[pl.ds(t * BLK, BLK), :] = vbuf[s]
        seg_row = seg_ref[pl.ds(p, 1), :]
        start = jnp.zeros((1, BLK), F32)
        for v in range(3):
            start = start + jnp.where(seg_row > v, counts[v], 0.0)
        first = (p - (WIN - 1)) * BLK
        start = start - first.astype(F32)
        start2 = jnp.concatenate([start, start], axis=1)

        for hp in range(2):
            wide = pl.ds(hp * 256, 256)
            q2 = qs[u, wide, :]
            do2 = ds_rows[u, wide, :]
            top = jnp.full((8, 256), NEGATIVE, F32)
            for t0, t1 in CHUNKS:
                rows = pl.ds(t0 * BLK, (t1 - t0) * BLK)
                sc = lax.dot_general(
                    kg[u, rows, :], q2, (((1,), (1,)), ((), ())), preferred_element_type=F32
                )
                for t in range(t0, t1):
                    tile = sc[(t - t0) * BLK : (t - t0 + 1) * BLK]
                    ok = rows_f >= start2 - float(t * BLK)
                    if t == WIN - 1:
                        ok = ok & causal
                    tile = jnp.where(ok, tile * c2, NEGATIVE)
                    s_scr[pl.ds(t * BLK, BLK), wide] = tile
                    top = jnp.maximum(top, jnp.max(tile.reshape(16, 8, 256), axis=0))
            top = jnp.max(top, axis=0, keepdims=True)
            norm = jnp.zeros((8, 256), F32)
            mixed = jnp.zeros((8, 256), F32)
            for t0, t1 in CHUNKS:
                rows = pl.ds(t0 * BLK, (t1 - t0) * BLK)
                dp = lax.dot_general(
                    vg[rows, :], do2, (((1,), (1,)), ((), ())), preferred_element_type=F32
                )
                for t in range(t0, t1):
                    tile = pl.ds(t * BLK, BLK)
                    dpt = dp[(t - t0) * BLK : (t - t0 + 1) * BLK]
                    pt = jnp.exp2(s_scr[tile, wide] - top)
                    s_scr[tile, wide] = pt
                    dp_scr[tile, wide] = dpt
                    norm = norm + jnp.sum(pt.reshape(16, 8, 256), axis=0)
                    mixed = mixed + jnp.sum((pt * dpt).reshape(16, 8, 256), axis=0)
            inv_norm = 1.0 / jnp.sum(norm, axis=0, keepdims=True)
            delta = jnp.sum(mixed, axis=0, keepdims=True) * inv_norm
            for t in range(WIN):
                tile = pl.ds(t * BLK, BLK)
                prob = s_scr[tile, wide] * inv_norm
                p_scr[u, t, :, wide] = prob.astype(BF)
                ds_scr[u, t, :, wide] = (prob * (dp_scr[tile, wide] - delta)).astype(BF)


def query_grads(dq_ref, kg, ds_scr):
    for u in range(2):
        for hp in range(2):
            wide = pl.ds(hp * 256, 256)
            dqt = jnp.zeros((HD, 256), F32)
            for t0, t1 in CHUNKS:
                dsc = ds_scr[u, pl.ds(t0, t1 - t0), :, wide].reshape((t1 - t0) * BLK, 256)
                dqt = dqt + lax.dot_general(
                    kg[u, pl.ds(t0 * BLK, (t1 - t0) * BLK), :], dsc,
                    (((0,), (0,)), ((), ())), preferred_element_type=F32,
                )
            for i in range(2):
                piece = (dqt[:, i * BLK : (i + 1) * BLK] * SCALE).T
                dq_ref[pl.ds(u * BLK, BLK), pl.ds((2 * hp + i) * HD, HD)] = piece.astype(BF)


def key_terms(ctx, span_ref, kind, core, source, weights, terms):
    base = [span_ref[2 * ctx + u] - (WIN - 1) for u in range(2)]

    @pl.loop(0, 2)
    def _(xx):
        picks = []
        for i in range(8):
            x2, lo, h = i // 4, (i // 2) % 2, i % 2
            where = span_ref[(xx * 2 + x2) * 8 + lo * 4 + core * 2 + h]
            pick = []
            for u in range(2):
                t = where - base[u]
                pick.append(jnp.where((t >= 0) & (t < WIN), t, WIN))
            picks.append(pick)
        total = None
        for u in range(2):
            left = jnp.concatenate([source[u, picks[i][u]] for i in range(8)], axis=0)
            part = jnp.dot(left, weights[u], preferred_element_type=F32)
            total = part if total is None else total + part
        if kind == 0:
            total = total * SCALE
        terms[pl.ds(xx * 2, 2)] = total.astype(BF).reshape(2, 2, 2, BLK, HD)


class Stream:
    def __init__(self, me, mail, kind, theirs, mine, r0, a1, b1, a2, b2, result):
        self.me, self.mail, self.kind = me, mail, kind
        self.theirs, self.mine, self.r0 = theirs, mine, r0
        self.a1, self.b1, self.a2, self.b2 = a1, b1, a2, b2
        self.result = result

    def to_sibling(self):
        self.half = self.mail.post(self.theirs, self.r0, self.me.at(dc=1))

    def first_leg(self):
        me, mine = self.me, self.mine
        self.half.wait_recv()
        for xx in range(4):
            mine[xx] = (mine[xx].astype(F32) + self.r0[xx].astype(F32)).astype(BF)
        self.leg1 = []
        for i, d in enumerate((1, -1, 2)):
            x = (me.x + d + 4) % 4
            y = (me.y + d + 4) % 4
            self.leg1.append(
                self.mail.post(mine.at[x, :, :, pl.ds(0, 64)], self.a1.at[i], me.at(dx=d))
            )
            self.leg1.append(
                self.mail.post(mine.at[:, y % 2, y // 2, pl.ds(64, 64)], self.b1.at[i], me.at(dy=d))
            )

    def second_leg(self):
        me, mine = self.me, self.mine
        for copy in self.leg1:
            copy.wait_recv()
        own_a = mine.at[me.x, :, :, pl.ds(0, 64)]
        own_b = mine.at[:, me.ylo, me.yhi, pl.ds(64, 64)]
        for own, got in ((own_a, self.a1), (own_b, self.b1)):
            total = own[...].astype(F32)
            for i in range(3):
                total = total + got[i].astype(F32)
            own[...] = total.astype(BF)
        self.leg2 = []
        for i, d in enumerate((1, -1, 2)):
            x = (me.x + d + 4) % 4
            y = (me.y + d + 4) % 4
            self.leg2.append(
                self.mail.post(
                    mine.at[me.x, y % 2, y // 2, pl.ds(0, 64)], self.a2.at[i], me.at(dy=d)
                )
            )
            self.leg2.append(
                self.mail.post(
                    mine.at[x, me.ylo, me.yhi, pl.ds(64, 64)], self.b2.at[i], me.at(dx=d)
                )
            )

    def spot(self, k, dz):
        half = self.me.yhi if k == 0 else 1 - self.me.yhi
        return self.result.at[self.kind, (self.me.z + dz + 8) % 8, half]

    def pass_on(self, k, dz, step):
        return self.mail.post(self.spot(k, dz), self.spot(k, dz), self.me.at(dz=step))

    def finish(self):
        me, mine = self.me, self.mine
        for copy in self.leg2:
            copy.wait_recv()
        own = self.spot(0, 0)
        for rows, got in ((pl.ds(0, 64), self.a2), (pl.ds(64, 64), self.b2)):
            total = mine[me.x, me.ylo, me.yhi, rows].astype(F32)
            for i in range(3):
                total = total + got[i].astype(F32)
            self.result[self.kind, me.z, me.yhi, rows] = total.astype(BF)
        self.up, self.down = [None, None], [None, None]
        self.up[0], self.down[0] = self.pass_on(0, 0, 1), self.pass_on(0, 0, -1)
        self.swap = self.mail.post(own, own, me.at(dy=2))

    def swapped(self):
        self.swap.wait_recv()
        self.up[1], self.down[1] = self.pass_on(1, 0, 1), self.pass_on(1, 0, -1)

    def hop(self, hop, k):
        self.up[k].wait_recv()
        if hop < 3 or (hop == 3 and k == 0):
            self.up[k] = self.pass_on(k, -hop, 1)
        self.down[k].wait_recv()
        if hop < 3 or (hop == 3 and k == 1):
            self.down[k] = self.pass_on(k, hop, -1)

    def last(self):
        self.up[0].wait_recv()
        self.down[1].wait_recv()


VMEM = pl.BlockSpec(memory_space=pltpu.VMEM)
SMEM = pl.BlockSpec(memory_space=pltpu.SMEM)
ANY = pl.BlockSpec(memory_space=pl.ANY)
LIMIT = 56 * 2**20


def kernel(
    q_ref, k_ref, v_ref, do_ref, span_ref, seg_ref, dq_ref, result,
    send, recv, local_sem, kbuf, vbuf, inv, qs, ds_rows, kg, vg, s_scr, dp_scr, p_scr, ds_scr,
    theirs, mine, r0, a1, b1, a2, b2,
):
    me = Place()
    greet(
        [me.at(dx=1), me.at(dx=-1), me.at(dx=2), me.at(dy=1), me.at(dy=-1), me.at(dy=2)]
        + [me.at(dc=1), me.at(dz=1), me.at(dz=-1)]
    )
    mail = Mail(send, recv)
    gather_phase(
        me, mail, k_ref, v_ref, kbuf, vbuf, local_sem,
        lambda: prepare(span_ref, seg_ref, q_ref, do_ref, inv, qs, ds_rows, p_scr, ds_scr),
    )
    attend(
        me.ctx, kbuf, vbuf, span_ref, seg_ref, inv, qs, ds_rows, kg, vg, s_scr, dp_scr,
        p_scr, ds_scr,
    )
    dk, dv = (
        Stream(
            me, mail, kind, theirs.at[kind], mine.at[kind], r0.at[kind], a1.at[kind],
            b1.at[kind], a2.at[kind], b2.at[kind], result,
        )
        for kind in range(2)
    )
    work = {0: (ds_scr, qs), 1: (p_scr, ds_rows)}

    def terms(stream, core, out):
        key_terms(me.ctx, span_ref, stream.kind, core, *work[stream.kind], out)

    terms(dv, 1 - me.core, dv.theirs)
    dv.to_sibling()
    terms(dv, me.core, dv.mine)
    dv.first_leg()
    terms(dk, 1 - me.core, dk.theirs)
    dk.to_sibling()
    terms(dk, me.core, dk.mine)
    dk.first_leg()
    dv.second_leg()
    query_grads(dq_ref, kg, ds_scr)
    dv.finish()
    dk.second_leg()
    dv.swapped()
    dv.hop(1, 0)
    dk.finish()
    dv.hop(1, 1)
    dk.swapped()
    dv.hop(2, 0)
    dv.hop(2, 1)
    dk.hop(1, 0)
    dk.hop(1, 1)
    dv.hop(3, 0)
    dv.hop(3, 1)
    dk.hop(2, 0)
    dk.hop(2, 1)
    dv.last()
    dk.hop(3, 0)
    dk.hop(3, 1)
    dk.last()
    mail.drain()


def per_device(queries, keys, values, d_out, span_order, segments):
    keys = keys.reshape(8, 2, BLK, HD)
    values = values.reshape(8, 2, BLK, HD)
    dq, result = pl.pallas_call(
        kernel,
        out_shape=[
            jax.ShapeDtypeStruct((256, 512), BF),
            jax.ShapeDtypeStruct((2, 8, 2, BLK, HD), BF),
        ],
        in_specs=[VMEM, ANY, ANY, VMEM, SMEM, VMEM],
        out_specs=[VMEM, VMEM],
        scratch_shapes=[
            pltpu.SemaphoreType.DMA((96,)),
            pltpu.SemaphoreType.DMA((96,)),
            pltpu.SemaphoreType.DMA((2,)),
            pltpu.VMEM((32, BLK, HD), BF),
            pltpu.VMEM((32, BLK, HD), BF),
            pltpu.SMEM((32,), jnp.int32),
            pltpu.VMEM((2, COLS, HD), BF),
            pltpu.VMEM((2, COLS, HD), BF),
            pltpu.VMEM((2, WIN * BLK, HD), BF),
            pltpu.VMEM((WIN * BLK, HD), BF),
            pltpu.VMEM((WIN * BLK, COLS), F32),
            pltpu.VMEM((WIN * BLK, COLS), F32),
            pltpu.VMEM((2, WIN + 1, BLK, COLS), BF),
            pltpu.VMEM((2, WIN + 1, BLK, COLS), BF),
            pltpu.VMEM((2, 4, 2, 2, BLK, HD), BF),
            pltpu.VMEM((2, 4, 2, 2, BLK, HD), BF),
            pltpu.VMEM((2, 4, 2, 2, BLK, HD), BF),
            pltpu.VMEM((2, 3, 2, 2, 64, HD), BF),
            pltpu.VMEM((2, 3, 4, 64, HD), BF),
            pltpu.VMEM((2, 3, 64, HD), BF),
            pltpu.VMEM((2, 3, 64, HD), BF),
        ],
        compiler_params=pltpu.CompilerParams(
            collective_id=0, has_side_effects=True, vmem_limit_bytes=LIMIT
        ),
        name="backward",
    )(queries, keys, values, d_out, span_order, segments.reshape(32, BLK))
    result = result.reshape(2, 8, 256, HD).astype(F32)
    return (dq, result[0], result[1])


def solution(mesh):
    return jax.shard_map(
        per_device,
        mesh=mesh,
        in_specs=(
            P("ctx", "tp"),
            P(None, "ctx", None),
            P(None, "ctx", None),
            P("ctx", "tp"),
            P(),
            P(),
        ),
        out_specs=(P("ctx", "tp"), P(None, "ctx", None), P(None, "ctx", None)),
        check_vma=False,
    )
```

```python
import functools

import jax
import jax.numpy as jnp
from jax import lax
from jax.experimental import pallas as pl
from jax.experimental.pallas import tpu as pltpu
from jax.sharding import PartitionSpec as P

HD = 128
BLK = 128
HEADS_DEV = 4
COLS = HEADS_DEV * BLK
WIN = 17
NEGATIVE = -1e30
SCALE = HD**-0.5
LOG2E = 1.4426950408889634
BF = jnp.bfloat16
F32 = jnp.float32


class Place:
    def __init__(self):
        self.ctx = lax.axis_index("ctx")
        self.tp = lax.axis_index("tp")
        self.x = self.ctx // 4
        self.ylo = (self.ctx // 2) % 2
        self.core = self.ctx % 2
        self.z = self.tp // 2
        self.yhi = self.tp % 2
        self.y = self.yhi * 2 + self.ylo

    def at(self, dx=0, dy=0, dc=0, dz=0):
        x = (self.x + dx + 4) % 4
        y = (self.y + dy + 4) % 4
        c = (self.core + dc) % 2
        z = (self.z + dz + 8) % 8
        return (x * 4 + (y % 2) * 2 + c, z * 2 + y // 2)

    def block(self, dx=0, dy=0, dc=0):
        return ((self.x + dx + 4) % 4) * 4 + ((self.ylo + dy) % 2) * 2 + (self.core + dc) % 2


class Mail:
    def __init__(self, send, recv):
        self.send, self.recv, self.used, self.out = send, recv, 0, []

    def post(self, src, dst, device):
        copy = pltpu.make_async_remote_copy(
            src_ref=src,
            dst_ref=dst,
            send_sem=self.send.at[self.used],
            recv_sem=self.recv.at[self.used],
            device_id=device,
            device_id_type=pl.DeviceIdType.MESH,
        )
        self.used += 1
        copy.start()
        self.out.append(copy)
        return copy

    def drain(self):
        for copy in self.out:
            copy.wait_send()
        self.out = []


def greet(devices):
    barrier = pltpu.get_barrier_semaphore()
    for device in devices:
        pl.semaphore_signal(
            barrier, inc=1, device_id=device, device_id_type=pl.DeviceIdType.MESH
        )
    pl.semaphore_wait(barrier, len(devices))


class Gather:
    def __init__(self, me, mail, src, buf, local_sem):
        self.me, self.mail, self.src, self.buf, self.local_sem = me, mail, src, buf, local_sem
        self.sib, self.far = [], []

    def whole(self, block):
        return self.buf.at[pl.ds(2 * block, 2)]

    def half(self, block, h):
        return self.buf.at[2 * block + h]

    def share(self, block, h=None):
        ref = self.whole(block) if h is None else self.half(block, h)
        self.sib.append(self.mail.post(ref, ref, self.me.at(dc=1)))

    def along_y(self, dx, h):
        ref = self.half(self.me.block(dx=dx), h)
        copy = self.mail.post(ref, ref, self.me.at(dy=1 - 2 * h))
        self.far.append((dx, h, copy))

    def own_x(self):
        me, own = self.me, self.me.block()
        self.local = pltpu.make_async_copy(self.src, self.whole(own), self.local_sem)
        self.local.start()
        self.xs = [
            (-d, self.mail.post(self.src, self.whole(own), me.at(dx=d))) for d in (1, -1)
        ]

    def own_y(self):
        me, own = self.me, self.me.block()
        self.y0 = [
            self.mail.post(self.src.at[h], self.half(own, h), me.at(dy=1 - 2 * h))
            for h in range(2)
        ]
        self.sib.append(self.mail.post(self.src, self.whole(own), me.at(dc=1)))

    def from_x(self):
        self.x2 = []
        for h, (dx, copy) in enumerate(self.xs):
            copy.wait_recv()
            block = self.me.block(dx=dx)
            ref = self.half(block, h)
            self.x2.append(self.mail.post(ref, ref, self.me.at(dx=-dx)))
            for i in range(2):
                self.along_y(dx, i)
            self.share(block)

    def from_y(self):
        for h in range(2):
            self.y0[h].wait_recv()
        self.share(self.me.block(dy=1))

    def from_x2(self):
        for h in range(2):
            self.x2[h].wait_recv()
            self.along_y(2, h)
        self.share(self.me.block(dx=2))

    def from_far(self, first, last):
        for i in range(first, last):
            dx, h, copy = self.far[i]
            copy.wait_recv()
            if h == 1:
                self.share(self.me.block(dx=dx, dy=1))

    def complete(self):
        self.local.wait()
        for copy in self.sib:
            copy.wait_recv()


CHUNKS = ((0, 6), (6, 12), (12, 17))


def prepare(span_ref, q_ref, do_ref, inv, qs, ds_rows, w_scr):
    for j in range(32):
        found = jnp.int32(0)
        for s in range(32):
            found = jnp.where(span_ref[s] == j, s, found)
        inv[j] = found
    zero = jnp.zeros((BLK, HD), F32)
    for u in range(2):
        w_scr[u, WIN] = zero
        for h in range(HEADS_DEV):
            qs[u, pl.ds(h * BLK, BLK), :] = q_ref[pl.ds(u * BLK, BLK), pl.ds(h * HD, HD)]
            ds_rows[u, pl.ds(h * BLK, BLK), :] = do_ref[pl.ds(u * BLK, BLK), pl.ds(h * HD, HD)]


def window(ctx, u, span_ref, inv, buf, out):
    p = span_ref[2 * ctx + u]
    for t in range(WIN):
        out[u, pl.ds(t * BLK, BLK), :] = buf[inv[jnp.maximum(p - (WIN - 1) + t, 0)]]


def nt_dot(a, b):
    return lax.dot_general(a, b, (((1,), (1,)), ((), ())), preferred_element_type=F32)


def probs_of(ctx, u, span_ref, seg_ref, qs, kg, s_scr, p_scr):
    p = span_ref[2 * ctx + u]
    seg_all = seg_ref[...]
    counts = [jnp.sum(jnp.where(seg_all == v, 1.0, 0.0)) for v in range(3)]
    cols2 = lax.broadcasted_iota(jnp.int32, (BLK, 2 * BLK), 1) % BLK
    rows2 = lax.broadcasted_iota(jnp.int32, (BLK, 2 * BLK), 0)
    causal = rows2 <= cols2
    rows_f = rows2.astype(F32)
    seg_row = seg_ref[pl.ds(p, 1), :]
    start = jnp.zeros((1, BLK), F32)
    for v in range(3):
        start = start + jnp.where(seg_row > v, counts[v], 0.0)
    first = (p - (WIN - 1)) * BLK
    start = start - first.astype(F32)
    start2 = jnp.concatenate([start, start], axis=1)
    inv_norms = []
    for hp in range(2):
        wide = pl.ds(hp * 256, 256)
        q2 = qs[u, wide, :]
        top = jnp.full((8, 256), NEGATIVE, F32)
        for t0, t1 in CHUNKS:
            sc = nt_dot(kg[u, pl.ds(t0 * BLK, (t1 - t0) * BLK), :], q2)
            for t in range(t0, t1):
                tile = sc[(t - t0) * BLK : (t - t0 + 1) * BLK]
                ok = rows_f >= start2 - float(t * BLK)
                if t == WIN - 1:
                    ok = ok & causal
                tile = jnp.where(ok, tile * (SCALE * LOG2E), NEGATIVE)
                s_scr[u, pl.ds(t * BLK, BLK), wide] = tile
                top = jnp.maximum(top, jnp.max(tile.reshape(16, 8, 256), axis=0))
        top = jnp.max(top, axis=0, keepdims=True)
        norm = jnp.zeros((8, 256), F32)
        for t in range(WIN):
            tile = pl.ds(t * BLK, BLK)
            pt = jnp.exp2(s_scr[u, tile, wide] - top)
            s_scr[u, tile, wide] = pt
            norm = norm + jnp.sum(pt.reshape(16, 8, 256), axis=0)
        inv_norm = 1.0 / jnp.sum(norm, axis=0, keepdims=True)
        for t in range(WIN):
            tile = pl.ds(t * BLK, BLK)
            p_scr[u, tile, wide] = (s_scr[u, tile, wide] * inv_norm).astype(BF)
        inv_norms.append(inv_norm)
    return inv_norms


def dscores_of(u, inv_norms, ds_rows, vg, s_scr, dp_scr, ds_scr):
    for hp in range(2):
        wide = pl.ds(hp * 256, 256)
        do2 = ds_rows[u, wide, :]
        mixed = jnp.zeros((8, 256), F32)
        for t0, t1 in CHUNKS:
            dp = nt_dot(vg[u, pl.ds(t0 * BLK, (t1 - t0) * BLK), :], do2)
            for t in range(t0, t1):
                tile = pl.ds(t * BLK, BLK)
                dpt = dp[(t - t0) * BLK : (t - t0 + 1) * BLK]
                dp_scr[tile, wide] = dpt
                mixed = mixed + jnp.sum(
                    (s_scr[u, tile, wide] * dpt).reshape(16, 8, 256), axis=0
                )
        inv_norm = inv_norms[hp]
        delta = jnp.sum(mixed, axis=0, keepdims=True) * inv_norm
        for t in range(WIN):
            tile = pl.ds(t * BLK, BLK)
            prob = s_scr[u, tile, wide] * inv_norm
            ds_scr[u, tile, wide] = (prob * (dp_scr[tile, wide] - delta)).astype(BF)


def query_grads(dq_ref, kg, ds_scr):
    for u in range(2):
        for hp in range(2):
            dqt = lax.dot_general(
                kg[u], ds_scr[u, :, pl.ds(hp * 256, 256)],
                (((0,), (0,)), ((), ())), preferred_element_type=F32,
            )
            for i in range(2):
                piece = (dqt[:, i * BLK : (i + 1) * BLK] * SCALE).T
                dq_ref[pl.ds(u * BLK, BLK), pl.ds((2 * hp + i) * HD, HD)] = piece.astype(BF)


def window_terms(u, source, weights, w_scr):
    for t0, t1 in CHUNKS:
        part = jnp.dot(
            source[u, pl.ds(t0 * BLK, (t1 - t0) * BLK), :], weights[u], preferred_element_type=F32
        )
        w_scr[u, pl.ds(t0, t1 - t0)] = part.reshape(t1 - t0, BLK, HD)


def assemble(ctx, span_ref, kind, core, w_scr, terms):
    base = [span_ref[2 * ctx + u] - (WIN - 1) for u in range(2)]
    for i in range(16):
        xx, lo, h = i // 4, (i // 2) % 2, i % 2
        where = span_ref[xx * 8 + lo * 4 + core * 2 + h]
        total = None
        for u in range(2):
            t = where - base[u]
            piece = w_scr[u, jnp.where((t >= 0) & (t < WIN), t, WIN)]
            total = piece if total is None else total + piece
        if kind == 0:
            total = total * SCALE
        terms[xx, lo, h] = total.astype(BF)


class Stream:
    def __init__(self, me, mail, kind, theirs, mine, r0, a1, b1, a2, b2, result):
        self.me, self.mail, self.kind = me, mail, kind
        self.theirs, self.mine, self.r0 = theirs, mine, r0
        self.a1, self.b1, self.a2, self.b2 = a1, b1, a2, b2
        self.result = result

    def to_sibling(self):
        self.half = self.mail.post(self.theirs, self.r0, self.me.at(dc=1))

    def first_leg(self):
        me, mine = self.me, self.mine
        self.half.wait_recv()
        for xx in range(4):
            mine[xx] = (mine[xx].astype(F32) + self.r0[xx].astype(F32)).astype(BF)
        self.leg1 = []
        for i, d in enumerate((1, -1, 2)):
            x = (me.x + d + 4) % 4
            y = (me.y + d + 4) % 4
            self.leg1.append(
                self.mail.post(mine.at[x, :, :, pl.ds(0, 64)], self.a1.at[i], me.at(dx=d))
            )
            self.leg1.append(
                self.mail.post(mine.at[:, y % 2, y // 2, pl.ds(64, 64)], self.b1.at[i], me.at(dy=d))
            )

    def second_leg(self):
        me, mine = self.me, self.mine
        for copy in self.leg1:
            copy.wait_recv()
        own_a = mine.at[me.x, :, :, pl.ds(0, 64)]
        own_b = mine.at[:, me.ylo, me.yhi, pl.ds(64, 64)]
        for own, got in ((own_a, self.a1), (own_b, self.b1)):
            total = own[...].astype(F32)
            for i in range(3):
                total = total + got[i].astype(F32)
            own[...] = total.astype(BF)
        self.leg2 = []
        for i, d in enumerate((1, -1, 2)):
            x = (me.x + d + 4) % 4
            y = (me.y + d + 4) % 4
            self.leg2.append(
                self.mail.post(
                    mine.at[me.x, y % 2, y // 2, pl.ds(0, 64)], self.a2.at[i], me.at(dy=d)
                )
            )
            self.leg2.append(
                self.mail.post(
                    mine.at[x, me.ylo, me.yhi, pl.ds(64, 64)], self.b2.at[i], me.at(dx=d)
                )
            )

    def spot(self, k, dz):
        half = self.me.yhi if k == 0 else 1 - self.me.yhi
        return self.result.at[self.kind, (self.me.z + dz + 8) % 8, half]

    def pass_on(self, k, dz, step):
        return self.mail.post(self.spot(k, dz), self.spot(k, dz), self.me.at(dz=step))

    def over(self, dz):
        return self.mail.post(self.spot(0, dz), self.spot(0, dz), self.me.at(dy=2))

    def finish(self):
        me, mine = self.me, self.mine
        for copy in self.leg2:
            copy.wait_recv()
        for rows, got in ((pl.ds(0, 64), self.a2), (pl.ds(64, 64), self.b2)):
            total = mine[me.x, me.ylo, me.yhi, rows].astype(F32)
            for i in range(3):
                total = total + got[i].astype(F32)
            self.result[self.kind, me.z, me.yhi, rows] = total.astype(BF)
        self.up, self.down = [None, None], [None, None]
        self.up[0], self.down[0] = self.pass_on(0, 0, 1), self.pass_on(0, 0, -1)
        self.swaps = [self.over(0)]

    def swapped(self):
        self.swaps[0].wait_recv()
        self.up[1], self.down[1] = self.pass_on(1, 0, 1), self.pass_on(1, 0, -1)

    def hop(self, hop, k):
        self.up[k].wait_recv()
        if hop < (3, 2)[k] or (hop == 3 and self.kind == 0):
            self.up[k] = self.pass_on(k, -hop, 1)
        if hop == 3:
            self.swaps.append(self.over(-hop))
        self.down[k].wait_recv()
        if hop < (3, 2)[k] or (hop == 3 and self.kind == 1):
            self.down[k] = self.pass_on(k, hop, -1)
        if hop == 3:
            self.swaps.append(self.over(hop))

    def farthest(self):
        (self.up[0] if self.kind == 0 else self.down[0]).wait_recv()
        self.swaps.append(self.over(4))

    def last(self):
        for copy in self.swaps[1:]:
            copy.wait_recv()


VMEM = pl.BlockSpec(memory_space=pltpu.VMEM)
SMEM = pl.BlockSpec(memory_space=pltpu.SMEM)
ANY = pl.BlockSpec(memory_space=pl.ANY)
LIMIT = 56 * 2**20


def kernel(
    q_ref, k_ref, v_ref, do_ref, span_ref, seg_ref, dq_ref, result,
    send, recv, local_sem, kbuf, vbuf, inv, qs, ds_rows, kg, vg, s_scr, dp_scr, p_scr, ds_scr,
    w_scr, theirs, mine, r0, a1, b1, a2, b2,
):
    me = Place()
    greet(
        [me.at(dx=1), me.at(dx=-1), me.at(dx=2), me.at(dy=1), me.at(dy=-1), me.at(dy=2)]
        + [me.at(dc=1), me.at(dz=1), me.at(dz=-1)]
    )
    mail = Mail(send, recv)
    gk = Gather(me, mail, k_ref.at[me.z], kbuf, local_sem.at[0])
    gv = Gather(me, mail, v_ref.at[me.z], vbuf, local_sem.at[1])
    gk.own_x()
    gk.own_y()
    gv.own_x()
    prepare(span_ref, q_ref, do_ref, inv, qs, ds_rows, w_scr)
    gk.from_x()
    gv.own_y()
    gk.from_y()
    gv.from_x()
    gk.from_x2()
    gk.from_far(0, 4)
    gv.from_y()
    gv.from_x2()
    gk.from_far(4, 6)
    gk.complete()
    ctx = me.ctx
    window(ctx, 0, span_ref, inv, kbuf, kg)
    norms = [probs_of(ctx, 0, span_ref, seg_ref, qs, kg, s_scr, p_scr)]
    gv.from_far(0, 6)
    window_terms(0, p_scr, ds_rows, w_scr)
    window(ctx, 1, span_ref, inv, kbuf, kg)
    norms.append(probs_of(ctx, 1, span_ref, seg_ref, qs, kg, s_scr, p_scr))
    window_terms(1, p_scr, ds_rows, w_scr)
    dk, dv = (
        Stream(
            me, mail, kind, theirs.at[kind], mine.at[kind], r0.at[kind], a1.at[kind],
            b1.at[kind], a2.at[kind], b2.at[kind], result,
        )
        for kind in range(2)
    )
    assemble(ctx, span_ref, 1, 1 - me.core, w_scr, dv.theirs)
    dv.to_sibling()
    assemble(ctx, span_ref, 1, me.core, w_scr, dv.mine)
    gv.complete()
    window(ctx, 0, span_ref, inv, vbuf, vg)
    dscores_of(0, norms[0], ds_rows, vg, s_scr, dp_scr, ds_scr)
    dv.first_leg()
    window_terms(0, ds_scr, qs, w_scr)
    window(ctx, 1, span_ref, inv, vbuf, vg)
    dscores_of(1, norms[1], ds_rows, vg, s_scr, dp_scr, ds_scr)
    window_terms(1, ds_scr, qs, w_scr)
    assemble(ctx, span_ref, 0, 1 - me.core, w_scr, dk.theirs)
    dk.to_sibling()
    dv.second_leg()
    assemble(ctx, span_ref, 0, me.core, w_scr, dk.mine)
    query_grads(dq_ref, kg, ds_scr)
    dk.first_leg()
    dv.finish()
    dv.swapped()
    dk.second_leg()
    dv.hop(1, 0)
    dv.hop(1, 1)
    dk.finish()
    dv.hop(2, 0)
    dk.swapped()
    dv.hop(2, 1)
    dk.hop(1, 0)
    dv.hop(3, 0)
    dk.hop(1, 1)
    dk.hop(2, 0)
    dv.farthest()
    dk.hop(2, 1)
    dk.hop(3, 0)
    dk.farthest()
    dv.last()
    dk.last()
    mail.drain()


def per_device(queries, keys, values, d_out, span_order, segments):
    keys = keys.reshape(8, 2, BLK, HD)
    values = values.reshape(8, 2, BLK, HD)
    dq, result = pl.pallas_call(
        kernel,
        out_shape=[
            jax.ShapeDtypeStruct((256, 512), BF),
            jax.ShapeDtypeStruct((2, 8, 2, BLK, HD), BF),
        ],
        in_specs=[VMEM, ANY, ANY, VMEM, SMEM, VMEM],
        out_specs=[VMEM, VMEM],
        scratch_shapes=[
            pltpu.SemaphoreType.DMA((112,)),
            pltpu.SemaphoreType.DMA((112,)),
            pltpu.SemaphoreType.DMA((2,)),
            pltpu.VMEM((32, BLK, HD), BF),
            pltpu.VMEM((32, BLK, HD), BF),
            pltpu.SMEM((32,), jnp.int32),
            pltpu.VMEM((2, COLS, HD), BF),
            pltpu.VMEM((2, COLS, HD), BF),
            pltpu.VMEM((2, WIN * BLK, HD), BF),
            pltpu.VMEM((2, WIN * BLK, HD), BF),
            pltpu.VMEM((2, WIN * BLK, COLS), F32),
            pltpu.VMEM((WIN * BLK, COLS), F32),
            pltpu.VMEM((2, WIN * BLK, COLS), BF),
            pltpu.VMEM((2, WIN * BLK, COLS), BF),
            pltpu.VMEM((2, WIN + 1, BLK, HD), F32),
            pltpu.VMEM((2, 4, 2, 2, BLK, HD), BF),
            pltpu.VMEM((2, 4, 2, 2, BLK, HD), BF),
            pltpu.VMEM((2, 4, 2, 2, BLK, HD), BF),
            pltpu.VMEM((2, 3, 2, 2, 64, HD), BF),
            pltpu.VMEM((2, 3, 4, 64, HD), BF),
            pltpu.VMEM((2, 3, 64, HD), BF),
            pltpu.VMEM((2, 3, 64, HD), BF),
        ],
        compiler_params=pltpu.CompilerParams(
            collective_id=0, has_side_effects=True, vmem_limit_bytes=LIMIT
        ),
        name="backward",
    )(queries, keys, values, d_out, span_order, segments.reshape(32, BLK))
    result = result.reshape(2, 8, 256, HD).astype(F32)
    return (dq, result[0], result[1])


def solution(mesh):
    return jax.shard_map(
        per_device,
        mesh=mesh,
        in_specs=(
            P("ctx", "tp"),
            P(None, "ctx", None),
            P(None, "ctx", None),
            P("ctx", "tp"),
            P(),
            P(),
        ),
        out_specs=(P("ctx", "tp"), P(None, "ctx", None), P(None, "ctx", None)),
        check_vma=False,
    )
```

```python
import functools

import jax
import jax.numpy as jnp
from jax import lax
from jax.experimental import pallas as pl
from jax.experimental.pallas import tpu as pltpu
from jax.sharding import PartitionSpec as P

HD = 128
BLK = 128
HEADS_DEV = 4
COLS = HEADS_DEV * BLK
WIN = 17
NEGATIVE = -1e30
SCALE = HD**-0.5
LOG2E = 1.4426950408889634
BF = jnp.bfloat16
F32 = jnp.float32


class Place:
    def __init__(self):
        self.ctx = lax.axis_index("ctx")
        self.tp = lax.axis_index("tp")
        self.x = self.ctx // 4
        self.ylo = (self.ctx // 2) % 2
        self.core = self.ctx % 2
        self.z = self.tp // 2
        self.yhi = self.tp % 2
        self.y = self.yhi * 2 + self.ylo

    def at(self, dx=0, dy=0, dc=0, dz=0):
        x = (self.x + dx + 4) % 4
        y = (self.y + dy + 4) % 4
        c = (self.core + dc) % 2
        z = (self.z + dz + 8) % 8
        return (x * 4 + (y % 2) * 2 + c, z * 2 + y // 2)

    def block(self, dx=0, dy=0, dc=0):
        return ((self.x + dx + 4) % 4) * 4 + ((self.ylo + dy) % 2) * 2 + (self.core + dc) % 2


class Mail:
    def __init__(self, send, recv):
        self.send, self.recv, self.used, self.out = send, recv, 0, []

    def post(self, src, dst, device):
        copy = pltpu.make_async_remote_copy(
            src_ref=src,
            dst_ref=dst,
            send_sem=self.send.at[self.used],
            recv_sem=self.recv.at[self.used],
            device_id=device,
            device_id_type=pl.DeviceIdType.MESH,
        )
        self.used += 1
        copy.start()
        self.out.append(copy)
        return copy

    def drain(self):
        for copy in self.out:
            copy.wait_send()
        self.out = []


def greet(devices):
    barrier = pltpu.get_barrier_semaphore()
    for device in devices:
        pl.semaphore_signal(
            barrier, inc=1, device_id=device, device_id_type=pl.DeviceIdType.MESH
        )
    pl.semaphore_wait(barrier, len(devices))


class Gather:
    def __init__(self, me, mail, src, buf, local_sem):
        self.me, self.mail, self.src, self.buf, self.local_sem = me, mail, src, buf, local_sem
        self.sib, self.far = [], []

    def whole(self, block):
        return self.buf.at[pl.ds(2 * block, 2)]

    def half(self, block, h):
        return self.buf.at[2 * block + h]

    def share(self, block, h=None):
        ref = self.whole(block) if h is None else self.half(block, h)
        self.sib.append(self.mail.post(ref, ref, self.me.at(dc=1)))

    def along_y(self, dx, h):
        ref = self.half(self.me.block(dx=dx), h)
        copy = self.mail.post(ref, ref, self.me.at(dy=1 - 2 * h))
        self.far.append((dx, h, copy))

    def own_x(self):
        me, own = self.me, self.me.block()
        self.local = pltpu.make_async_copy(self.src, self.whole(own), self.local_sem)
        self.local.start()
        self.xs = [
            (-d, self.mail.post(self.src, self.whole(own), me.at(dx=d))) for d in (1, -1, 2)
        ]

    def own_y(self):
        me, own = self.me, self.me.block()
        self.y0 = [
            self.mail.post(self.src.at[h], self.half(own, h), me.at(dy=1 - 2 * h))
            for h in range(2)
        ]
        self.sib.append(self.mail.post(self.src, self.whole(own), me.at(dc=1)))

    def from_x(self, i):
        dx, copy = self.xs[i]
        copy.wait_recv()
        for h in range(2):
            self.along_y(dx, h)
        self.share(self.me.block(dx=dx))

    def from_y(self):
        for h in range(2):
            self.y0[h].wait_recv()
        self.share(self.me.block(dy=1))

    def from_far(self, first, last):
        for i in range(first, last):
            dx, h, copy = self.far[i]
            copy.wait_recv()
            if h == 1:
                self.share(self.me.block(dx=dx, dy=1))

    def complete(self):
        self.local.wait()
        for copy in self.sib:
            copy.wait_recv()


CHUNKS = ((0, 6), (6, 12), (12, 17))


def prepare(span_ref, q_ref, do_ref, inv, qs, ds_rows, w_scr):
    for j in range(32):
        found = jnp.int32(0)
        for s in range(32):
            found = jnp.where(span_ref[s] == j, s, found)
        inv[j] = found
    zero = jnp.zeros((BLK, HD), F32)
    for u in range(2):
        w_scr[u, WIN] = zero
        for h in range(HEADS_DEV):
            qs[u, pl.ds(h * BLK, BLK), :] = q_ref[pl.ds(u * BLK, BLK), pl.ds(h * HD, HD)]
            ds_rows[u, pl.ds(h * BLK, BLK), :] = do_ref[pl.ds(u * BLK, BLK), pl.ds(h * HD, HD)]


def window(ctx, u, span_ref, inv, buf, out):
    p = span_ref[2 * ctx + u]
    for t in range(WIN):
        out[u, pl.ds(t * BLK, BLK), :] = buf[inv[jnp.maximum(p - (WIN - 1) + t, 0)]]


def nt_dot(a, b):
    return lax.dot_general(a, b, (((1,), (1,)), ((), ())), preferred_element_type=F32)


def probs_of(ctx, u, span_ref, seg_ref, qs, kg, s_scr, p_scr):
    p = span_ref[2 * ctx + u]
    seg_all = seg_ref[...]
    counts = [jnp.sum(jnp.where(seg_all == v, 1.0, 0.0)) for v in range(3)]
    cols2 = lax.broadcasted_iota(jnp.int32, (BLK, 2 * BLK), 1) % BLK
    rows2 = lax.broadcasted_iota(jnp.int32, (BLK, 2 * BLK), 0)
    causal = rows2 <= cols2
    rows_f = rows2.astype(F32)
    seg_row = seg_ref[pl.ds(p, 1), :]
    start = jnp.zeros((1, BLK), F32)
    for v in range(3):
        start = start + jnp.where(seg_row > v, counts[v], 0.0)
    first = (p - (WIN - 1)) * BLK
    start = start - first.astype(F32)
    start2 = jnp.concatenate([start, start], axis=1)
    inv_norms = []
    for hp in range(2):
        wide = pl.ds(hp * 256, 256)
        q2 = qs[u, wide, :]
        top = jnp.full((8, 256), NEGATIVE, F32)
        for t0, t1 in CHUNKS:
            sc = nt_dot(kg[u, pl.ds(t0 * BLK, (t1 - t0) * BLK), :], q2)
            for t in range(t0, t1):
                tile = sc[(t - t0) * BLK : (t - t0 + 1) * BLK]
                ok = rows_f >= start2 - float(t * BLK)
                if t == WIN - 1:
                    ok = ok & causal
                tile = jnp.where(ok, tile * (SCALE * LOG2E), NEGATIVE)
                s_scr[u, pl.ds(t * BLK, BLK), wide] = tile
                top = jnp.maximum(top, jnp.max(tile.reshape(16, 8, 256), axis=0))
        top = jnp.max(top, axis=0, keepdims=True)
        norm = jnp.zeros((8, 256), F32)
        for t in range(WIN):
            tile = pl.ds(t * BLK, BLK)
            pt = jnp.exp2(s_scr[u, tile, wide] - top)
            s_scr[u, tile, wide] = pt
            norm = norm + jnp.sum(pt.reshape(16, 8, 256), axis=0)
        inv_norm = 1.0 / jnp.sum(norm, axis=0, keepdims=True)
        for t in range(WIN):
            tile = pl.ds(t * BLK, BLK)
            p_scr[u, tile, wide] = (s_scr[u, tile, wide] * inv_norm).astype(BF)
        inv_norms.append(inv_norm)
    return inv_norms


def dscores_of(u, inv_norms, ds_rows, vg, s_scr, dp_scr, ds_scr):
    for hp in range(2):
        wide = pl.ds(hp * 256, 256)
        do2 = ds_rows[u, wide, :]
        mixed = jnp.zeros((8, 256), F32)
        for t0, t1 in CHUNKS:
            dp = nt_dot(vg[u, pl.ds(t0 * BLK, (t1 - t0) * BLK), :], do2)
            for t in range(t0, t1):
                tile = pl.ds(t * BLK, BLK)
                dpt = dp[(t - t0) * BLK : (t - t0 + 1) * BLK]
                dp_scr[tile, wide] = dpt
                mixed = mixed + jnp.sum(
                    (s_scr[u, tile, wide] * dpt).reshape(16, 8, 256), axis=0
                )
        inv_norm = inv_norms[hp]
        delta = jnp.sum(mixed, axis=0, keepdims=True) * inv_norm
        for t in range(WIN):
            tile = pl.ds(t * BLK, BLK)
            prob = s_scr[u, tile, wide] * inv_norm
            ds_scr[u, tile, wide] = (prob * (dp_scr[tile, wide] - delta)).astype(BF)


def query_grads(dq_ref, kg, ds_scr):
    for u in range(2):
        for hp in range(2):
            dqt = lax.dot_general(
                kg[u], ds_scr[u, :, pl.ds(hp * 256, 256)],
                (((0,), (0,)), ((), ())), preferred_element_type=F32,
            )
            for i in range(2):
                piece = (dqt[:, i * BLK : (i + 1) * BLK] * SCALE).T
                dq_ref[pl.ds(u * BLK, BLK), pl.ds((2 * hp + i) * HD, HD)] = piece.astype(BF)


def window_terms(u, source, weights, w_scr):
    for t0, t1 in CHUNKS:
        part = jnp.dot(
            source[u, pl.ds(t0 * BLK, (t1 - t0) * BLK), :], weights[u], preferred_element_type=F32
        )
        w_scr[u, pl.ds(t0, t1 - t0)] = part.reshape(t1 - t0, BLK, HD)


def assemble(ctx, span_ref, kind, core, w_scr, terms):
    base = [span_ref[2 * ctx + u] - (WIN - 1) for u in range(2)]
    for i in range(16):
        xx, lo, h = i // 4, (i // 2) % 2, i % 2
        where = span_ref[xx * 8 + lo * 4 + core * 2 + h]
        total = None
        for u in range(2):
            t = where - base[u]
            piece = w_scr[u, jnp.where((t >= 0) & (t < WIN), t, WIN)]
            total = piece if total is None else total + piece
        if kind == 0:
            total = total * SCALE
        terms[xx, lo, h] = total.astype(BF)


class Stream:
    def __init__(self, me, mail, kind, theirs, mine, r0, a1, b1, a2, b2, result):
        self.me, self.mail, self.kind = me, mail, kind
        self.theirs, self.mine, self.r0 = theirs, mine, r0
        self.a1, self.b1, self.a2, self.b2 = a1, b1, a2, b2
        self.result = result

    def to_sibling(self):
        self.half = self.mail.post(self.theirs, self.r0, self.me.at(dc=1))

    def first_leg(self):
        me, mine = self.me, self.mine
        self.half.wait_recv()
        for xx in range(4):
            mine[xx] = (mine[xx].astype(F32) + self.r0[xx].astype(F32)).astype(BF)
        self.leg1 = []
        for i, d in enumerate((1, -1, 2)):
            x = (me.x + d + 4) % 4
            y = (me.y + d + 4) % 4
            self.leg1.append(
                self.mail.post(mine.at[x, :, :, pl.ds(0, 64)], self.a1.at[i], me.at(dx=d))
            )
            self.leg1.append(
                self.mail.post(mine.at[:, y % 2, y // 2, pl.ds(64, 64)], self.b1.at[i], me.at(dy=d))
            )

    def second_leg(self):
        me, mine = self.me, self.mine
        for copy in self.leg1:
            copy.wait_recv()
        own_a = mine.at[me.x, :, :, pl.ds(0, 64)]
        own_b = mine.at[:, me.ylo, me.yhi, pl.ds(64, 64)]
        for own, got in ((own_a, self.a1), (own_b, self.b1)):
            total = own[...].astype(F32)
            for i in range(3):
                total = total + got[i].astype(F32)
            own[...] = total.astype(BF)
        self.leg2 = []
        for i, d in enumerate((1, -1, 2)):
            x = (me.x + d + 4) % 4
            y = (me.y + d + 4) % 4
            self.leg2.append(
                self.mail.post(
                    mine.at[me.x, y % 2, y // 2, pl.ds(0, 64)], self.a2.at[i], me.at(dy=d)
                )
            )
            self.leg2.append(
                self.mail.post(
                    mine.at[x, me.ylo, me.yhi, pl.ds(64, 64)], self.b2.at[i], me.at(dx=d)
                )
            )

    def spot(self, k, dz):
        half = self.me.yhi if k == 0 else 1 - self.me.yhi
        return self.result.at[self.kind, (self.me.z + dz + 8) % 8, half]

    def over(self, dz):
        return self.mail.post(self.spot(0, dz), self.spot(0, dz), self.me.at(dy=2))

    def finish(self):
        me, mine = self.me, self.mine
        for copy in self.leg2:
            copy.wait_recv()
        for rows, got in ((pl.ds(0, 64), self.a2), (pl.ds(64, 64), self.b2)):
            total = mine[me.x, me.ylo, me.yhi, rows].astype(F32)
            for i in range(3):
                total = total + got[i].astype(F32)
            self.result[self.kind, me.z, me.yhi, rows] = total.astype(BF)
        self.swaps = [self.over(0)]
        self.direct = [
            (-dz, self.mail.post(self.spot(0, 0), self.spot(0, 0), me.at(dz=dz)))
            for dz in (1, -1, 2, -2, 3, -3, 4)
        ]

    def spread(self):
        for dz, copy in self.direct:
            copy.wait_recv()
            self.swaps.append(self.over(dz))

    def last(self):
        for copy in self.swaps:
            copy.wait_recv()


VMEM = pl.BlockSpec(memory_space=pltpu.VMEM)
SMEM = pl.BlockSpec(memory_space=pltpu.SMEM)
ANY = pl.BlockSpec(memory_space=pl.ANY)
LIMIT = 56 * 2**20


def kernel(
    q_ref, k_ref, v_ref, do_ref, span_ref, seg_ref, dq_ref, result,
    send, recv, local_sem, kbuf, vbuf, inv, qs, ds_rows, kg, vg, s_scr, dp_scr, p_scr, ds_scr,
    w_scr, theirs, mine, r0, a1, b1, a2, b2,
):
    me = Place()
    greet(
        [me.at(dx=1), me.at(dx=-1), me.at(dx=2), me.at(dy=1), me.at(dy=-1), me.at(dy=2)]
        + [me.at(dc=1)]
        + [me.at(dz=dz) for dz in (1, -1, 2, -2, 3, -3, 4)]
    )
    mail = Mail(send, recv)
    gk = Gather(me, mail, k_ref.at[me.z], kbuf, local_sem.at[0])
    gv = Gather(me, mail, v_ref.at[me.z], vbuf, local_sem.at[1])
    gk.own_x()
    gk.own_y()
    gv.own_x()
    prepare(span_ref, q_ref, do_ref, inv, qs, ds_rows, w_scr)
    gk.from_x(0)
    gk.from_x(1)
    gv.own_y()
    gk.from_y()
    gk.from_x(2)
    gv.from_x(0)
    gv.from_x(1)
    gk.from_far(0, 4)
    gv.from_y()
    gv.from_x(2)
    gk.from_far(4, 6)
    gk.complete()
    ctx = me.ctx
    window(ctx, 0, span_ref, inv, kbuf, kg)
    norms = [probs_of(ctx, 0, span_ref, seg_ref, qs, kg, s_scr, p_scr)]
    gv.from_far(0, 6)
    window_terms(0, p_scr, ds_rows, w_scr)
    window(ctx, 1, span_ref, inv, kbuf, kg)
    norms.append(probs_of(ctx, 1, span_ref, seg_ref, qs, kg, s_scr, p_scr))
    window_terms(1, p_scr, ds_rows, w_scr)
    dk, dv = (
        Stream(
            me, mail, kind, theirs.at[kind], mine.at[kind], r0.at[kind], a1.at[kind],
            b1.at[kind], a2.at[kind], b2.at[kind], result,
        )
        for kind in range(2)
    )
    assemble(ctx, span_ref, 1, 1 - me.core, w_scr, dv.theirs)
    dv.to_sibling()
    assemble(ctx, span_ref, 1, me.core, w_scr, dv.mine)
    gv.complete()
    window(ctx, 0, span_ref, inv, vbuf, vg)
    dscores_of(0, norms[0], ds_rows, vg, s_scr, dp_scr, ds_scr)
    dv.first_leg()
    window_terms(0, ds_scr, qs, w_scr)
    window(ctx, 1, span_ref, inv, vbuf, vg)
    dscores_of(1, norms[1], ds_rows, vg, s_scr, dp_scr, ds_scr)
    window_terms(1, ds_scr, qs, w_scr)
    assemble(ctx, span_ref, 0, 1 - me.core, w_scr, dk.theirs)
    dk.to_sibling()
    assemble(ctx, span_ref, 0, me.core, w_scr, dk.mine)
    dv.second_leg()
    dk.first_leg()
    query_grads(dq_ref, kg, ds_scr)
    dv.finish()
    dk.second_leg()
    dv.spread()
    dk.finish()
    dk.spread()
    dv.last()
    dk.last()
    mail.drain()


def per_device(queries, keys, values, d_out, span_order, segments):
    keys = keys.reshape(8, 2, BLK, HD)
    values = values.reshape(8, 2, BLK, HD)
    dq, result = pl.pallas_call(
        kernel,
        out_shape=[
            jax.ShapeDtypeStruct((256, 512), BF),
            jax.ShapeDtypeStruct((2, 8, 2, BLK, HD), BF),
        ],
        in_specs=[VMEM, ANY, ANY, VMEM, SMEM, VMEM],
        out_specs=[VMEM, VMEM],
        scratch_shapes=[
            pltpu.SemaphoreType.DMA((112,)),
            pltpu.SemaphoreType.DMA((112,)),
            pltpu.SemaphoreType.DMA((2,)),
            pltpu.VMEM((32, BLK, HD), BF),
            pltpu.VMEM((32, BLK, HD), BF),
            pltpu.SMEM((32,), jnp.int32),
            pltpu.VMEM((2, COLS, HD), BF),
            pltpu.VMEM((2, COLS, HD), BF),
            pltpu.VMEM((2, WIN * BLK, HD), BF),
            pltpu.VMEM((2, WIN * BLK, HD), BF),
            pltpu.VMEM((2, WIN * BLK, COLS), F32),
            pltpu.VMEM((WIN * BLK, COLS), F32),
            pltpu.VMEM((2, WIN * BLK, COLS), BF),
            pltpu.VMEM((2, WIN * BLK, COLS), BF),
            pltpu.VMEM((2, WIN + 1, BLK, HD), F32),
            pltpu.VMEM((2, 4, 2, 2, BLK, HD), BF),
            pltpu.VMEM((2, 4, 2, 2, BLK, HD), BF),
            pltpu.VMEM((2, 4, 2, 2, BLK, HD), BF),
            pltpu.VMEM((2, 3, 2, 2, 64, HD), BF),
            pltpu.VMEM((2, 3, 4, 64, HD), BF),
            pltpu.VMEM((2, 3, 64, HD), BF),
            pltpu.VMEM((2, 3, 64, HD), BF),
        ],
        compiler_params=pltpu.CompilerParams(
            collective_id=0, has_side_effects=True, vmem_limit_bytes=LIMIT
        ),
        name="backward",
    )(queries, keys, values, d_out, span_order, segments.reshape(32, BLK))
    result = result.reshape(2, 8, 256, HD).astype(F32)
    return (dq, result[0], result[1])


def solution(mesh):
    return jax.shard_map(
        per_device,
        mesh=mesh,
        in_specs=(
            P("ctx", "tp"),
            P(None, "ctx", None),
            P(None, "ctx", None),
            P("ctx", "tp"),
            P(),
            P(),
        ),
        out_specs=(P("ctx", "tp"), P(None, "ctx", None), P(None, "ctx", None)),
        check_vma=False,
    )
```

```python
import functools

import jax
import jax.numpy as jnp
from jax import lax
from jax.experimental import pallas as pl
from jax.experimental.pallas import tpu as pltpu
from jax.sharding import PartitionSpec as P

HD = 128
BLK = 128
HEADS_DEV = 4
COLS = HEADS_DEV * BLK
WIN = 17
NEGATIVE = -1e30
SCALE = HD**-0.5
LOG2E = 1.4426950408889634
BF = jnp.bfloat16
F32 = jnp.float32


class Place:
    def __init__(self):
        self.ctx = lax.axis_index("ctx")
        self.tp = lax.axis_index("tp")
        self.x = self.ctx // 4
        self.ylo = (self.ctx // 2) % 2
        self.core = self.ctx % 2
        self.z = self.tp // 2
        self.yhi = self.tp % 2
        self.y = self.yhi * 2 + self.ylo

    def at(self, dx=0, dy=0, dc=0, dz=0):
        x = (self.x + dx + 4) % 4
        y = (self.y + dy + 4) % 4
        c = (self.core + dc) % 2
        z = (self.z + dz + 8) % 8
        return (x * 4 + (y % 2) * 2 + c, z * 2 + y // 2)

    def block(self, dx=0, dy=0, dc=0):
        return ((self.x + dx + 4) % 4) * 4 + ((self.ylo + dy) % 2) * 2 + (self.core + dc) % 2


class Mail:
    def __init__(self, send, recv):
        self.send, self.recv, self.used, self.out = send, recv, 0, []

    def post(self, src, dst, device):
        copy = pltpu.make_async_remote_copy(
            src_ref=src,
            dst_ref=dst,
            send_sem=self.send.at[self.used],
            recv_sem=self.recv.at[self.used],
            device_id=device,
            device_id_type=pl.DeviceIdType.MESH,
        )
        self.used += 1
        copy.start()
        self.out.append(copy)
        return copy

    def drain(self):
        for copy in self.out:
            copy.wait_send()
        self.out = []


def greet(devices):
    barrier = pltpu.get_barrier_semaphore()
    for device in devices:
        pl.semaphore_signal(
            barrier, inc=1, device_id=device, device_id_type=pl.DeviceIdType.MESH
        )
    pl.semaphore_wait(barrier, len(devices))


class Gather:
    def __init__(self, me, mail, src, buf, local_sem):
        self.me, self.mail, self.src, self.buf, self.local_sem = me, mail, src, buf, local_sem
        self.sib, self.far = [], []

    def whole(self, block):
        return self.buf.at[pl.ds(2 * block, 2)]

    def half(self, block, h):
        return self.buf.at[2 * block + h]

    def share(self, block, h=None):
        ref = self.whole(block) if h is None else self.half(block, h)
        self.sib.append(self.mail.post(ref, ref, self.me.at(dc=1)))

    def along_y(self, dx, h):
        ref = self.half(self.me.block(dx=dx), h)
        copy = self.mail.post(ref, ref, self.me.at(dy=1 - 2 * h))
        self.far.append((dx, h, copy))

    def own_x(self):
        me, own = self.me, self.me.block()
        self.local = pltpu.make_async_copy(self.src, self.whole(own), self.local_sem)
        self.local.start()
        self.xs = [
            (-d, self.mail.post(self.src, self.whole(own), me.at(dx=d))) for d in (1, -1, 2)
        ]

    def own_y(self):
        me, own = self.me, self.me.block()
        self.y0 = [
            self.mail.post(self.src.at[h], self.half(own, h), me.at(dy=1 - 2 * h))
            for h in range(2)
        ]
        self.sib.append(self.mail.post(self.src, self.whole(own), me.at(dc=1)))

    def from_x(self, i):
        dx, copy = self.xs[i]
        copy.wait_recv()
        for h in range(2):
            self.along_y(dx, h)
        self.share(self.me.block(dx=dx))

    def from_y(self):
        for h in range(2):
            self.y0[h].wait_recv()
        self.share(self.me.block(dy=1))

    def from_far(self, first, last):
        for i in range(first, last):
            dx, h, copy = self.far[i]
            copy.wait_recv()
            if h == 1:
                self.share(self.me.block(dx=dx, dy=1))

    def complete(self):
        self.local.wait()
        for copy in self.sib:
            copy.wait_recv()


CHUNKS = ((0, 6), (6, 12), (12, 17))


def prepare(span_ref, inv, w_scr):
    for j in range(32):
        found = jnp.int32(0)
        for s in range(32):
            found = jnp.where(span_ref[s] == j, s, found)
        inv[j] = found
    zero = jnp.zeros((BLK, HD), F32)
    for u in range(2):
        w_scr[u, WIN] = zero


def stack_heads(q_ref, do_ref, qs, ds_rows):
    for u in range(2):
        for h in range(HEADS_DEV):
            qs[u, pl.ds(h * BLK, BLK), :] = q_ref[pl.ds(u * BLK, BLK), pl.ds(h * HD, HD)]
            ds_rows[u, pl.ds(h * BLK, BLK), :] = do_ref[pl.ds(u * BLK, BLK), pl.ds(h * HD, HD)]


def window(ctx, u, span_ref, inv, buf, out):
    p = span_ref[2 * ctx + u]
    for t in range(WIN):
        out[u, pl.ds(t * BLK, BLK), :] = buf[inv[jnp.maximum(p - (WIN - 1) + t, 0)]]


def nt_dot(a, b):
    return lax.dot_general(a, b, (((1,), (1,)), ((), ())), preferred_element_type=F32)


def probs_of(ctx, u, span_ref, seg_ref, qs, ds_rows, qn, dn, kg, s_scr, p_scr):
    p = span_ref[2 * ctx + u]
    seg_all = seg_ref[...]
    counts = [jnp.sum(jnp.where(seg_all == v, 1.0, 0.0)) for v in range(3)]
    cols2 = lax.broadcasted_iota(jnp.int32, (BLK, 2 * BLK), 1) % BLK
    rows2 = lax.broadcasted_iota(jnp.int32, (BLK, 2 * BLK), 0)
    causal = rows2 <= cols2
    rows_f = rows2.astype(F32)
    seg_row = seg_ref[pl.ds(p, 1), :]
    start = jnp.zeros((1, BLK), F32)
    for v in range(3):
        start = start + jnp.where(seg_row > v, counts[v], 0.0)
    first = (p - (WIN - 1)) * BLK
    start = start - first.astype(F32)
    start2 = jnp.concatenate([start, start], axis=1)
    inv_norms = []
    for hp in range(2):
        wide = pl.ds(hp * 256, 256)
        q2 = qs[u, wide, :]
        top = jnp.full((8, 256), NEGATIVE, F32)
        for t0, t1 in CHUNKS:
            sc = nt_dot(kg[u, pl.ds(t0 * BLK, (t1 - t0) * BLK), :], q2)
            for t in range(t0, t1):
                tile = sc[(t - t0) * BLK : (t - t0 + 1) * BLK]
                ok = rows_f >= start2 - float(t * BLK)
                if t == WIN - 1:
                    ok = ok & causal
                tile = jnp.where(ok, tile * (SCALE * LOG2E), NEGATIVE)
                s_scr[u, pl.ds(t * BLK, BLK), wide] = tile
                top = jnp.maximum(top, jnp.max(tile.reshape(16, 8, 256), axis=0))
        top = jnp.max(top, axis=0, keepdims=True)
        norm = jnp.zeros((8, 256), F32)
        for t in range(WIN):
            tile = pl.ds(t * BLK, BLK)
            pt = jnp.exp2(s_scr[u, tile, wide] - top)
            s_scr[u, tile, wide] = pt
            p_scr[u, tile, wide] = pt.astype(BF)
            norm = norm + jnp.sum(pt.reshape(16, 8, 256), axis=0)
        inv_norm = 1.0 / jnp.sum(norm, axis=0, keepdims=True)
        for i in range(2):
            row = inv_norm[:, i * BLK : (i + 1) * BLK]
            by_row = jnp.broadcast_to(row, (BLK, BLK)).T
            part = pl.ds((2 * hp + i) * BLK, BLK)
            qn[u, part, :] = (qs[u, part, :].astype(F32) * by_row).astype(BF)
            dn[u, part, :] = (ds_rows[u, part, :].astype(F32) * by_row).astype(BF)
        inv_norms.append(inv_norm)
    return inv_norms


def dscores_of(u, inv_norms, ds_rows, vg, s_scr, dp_scr, ds_scr):
    for hp in range(2):
        wide = pl.ds(hp * 256, 256)
        do2 = ds_rows[u, wide, :]
        mixed = jnp.zeros((8, 256), F32)
        for t0, t1 in CHUNKS:
            dp = nt_dot(vg[u, pl.ds(t0 * BLK, (t1 - t0) * BLK), :], do2)
            for t in range(t0, t1):
                tile = pl.ds(t * BLK, BLK)
                dpt = dp[(t - t0) * BLK : (t - t0 + 1) * BLK]
                dp_scr[tile, wide] = dpt
                mixed = mixed + jnp.sum(
                    (s_scr[u, tile, wide] * dpt).reshape(16, 8, 256), axis=0
                )
        delta = jnp.sum(mixed, axis=0, keepdims=True) * inv_norms[hp]
        for t in range(WIN):
            tile = pl.ds(t * BLK, BLK)
            ds_scr[u, tile, wide] = (s_scr[u, tile, wide] * (dp_scr[tile, wide] - delta)).astype(BF)


def query_grads(dq_ref, kg, ds_scr, norms):
    for u in range(2):
        for hp in range(2):
            dqt = lax.dot_general(
                kg[u], ds_scr[u, :, pl.ds(hp * 256, 256)],
                (((0,), (0,)), ((), ())), preferred_element_type=F32,
            ) * (norms[u][hp] * SCALE)
            for i in range(2):
                piece = dqt[:, i * BLK : (i + 1) * BLK].T
                dq_ref[pl.ds(u * BLK, BLK), pl.ds((2 * hp + i) * HD, HD)] = piece.astype(BF)


def window_terms(u, source, weights, w_scr):
    for t0, t1 in CHUNKS:
        part = jnp.dot(
            source[u, pl.ds(t0 * BLK, (t1 - t0) * BLK), :], weights[u], preferred_element_type=F32
        )
        w_scr[u, pl.ds(t0, t1 - t0)] = part.reshape(t1 - t0, BLK, HD)


def assemble(ctx, span_ref, kind, core, w_scr, terms):
    base = [span_ref[2 * ctx + u] - (WIN - 1) for u in range(2)]
    for i in range(16):
        xx, lo, h = i // 4, (i // 2) % 2, i % 2
        where = span_ref[xx * 8 + lo * 4 + core * 2 + h]
        total = None
        for u in range(2):
            t = where - base[u]
            piece = w_scr[u, jnp.where((t >= 0) & (t < WIN), t, WIN)]
            total = piece if total is None else total + piece
        if kind == 0:
            total = total * SCALE
        terms[xx, lo, h] = total.astype(BF)


class Stream:
    def __init__(self, me, mail, kind, theirs, mine, r0, a1, b1, a2, b2, own, sem, result):
        self.me, self.mail, self.kind = me, mail, kind
        self.theirs, self.mine, self.r0 = theirs, mine, r0
        self.a1, self.b1, self.a2, self.b2 = a1, b1, a2, b2
        self.own, self.sem, self.result = own, sem, result

    def to_sibling(self):
        self.half = self.mail.post(self.theirs, self.r0, self.me.at(dc=1))

    def first_leg(self):
        me, mine = self.me, self.mine
        self.half.wait_recv()
        for xx in range(4):
            mine[xx] = (mine[xx].astype(F32) + self.r0[xx].astype(F32)).astype(BF)
        self.leg1 = []
        for i, d in enumerate((1, -1, 2)):
            x = (me.x + d + 4) % 4
            y = (me.y + d + 4) % 4
            self.leg1.append(
                self.mail.post(mine.at[x, :, :, pl.ds(0, 64)], self.a1.at[i], me.at(dx=d))
            )
            self.leg1.append(
                self.mail.post(mine.at[:, y % 2, y // 2, pl.ds(64, 64)], self.b1.at[i], me.at(dy=d))
            )

    def second_leg(self):
        me, mine = self.me, self.mine
        for copy in self.leg1:
            copy.wait_recv()
        own_a = mine.at[me.x, :, :, pl.ds(0, 64)]
        own_b = mine.at[:, me.ylo, me.yhi, pl.ds(64, 64)]
        for own, got in ((own_a, self.a1), (own_b, self.b1)):
            total = own[...].astype(F32)
            for i in range(3):
                total = total + got[i].astype(F32)
            own[...] = total.astype(BF)
        self.leg2 = []
        for i, d in enumerate((1, -1, 2)):
            x = (me.x + d + 4) % 4
            y = (me.y + d + 4) % 4
            self.leg2.append(
                self.mail.post(
                    mine.at[me.x, y % 2, y // 2, pl.ds(0, 64)], self.a2.at[i], me.at(dy=d)
                )
            )
            self.leg2.append(
                self.mail.post(
                    mine.at[x, me.ylo, me.yhi, pl.ds(64, 64)], self.b2.at[i], me.at(dx=d)
                )
            )

    def spot(self, k, dz):
        half = self.me.yhi if k == 0 else 1 - self.me.yhi
        return self.result.at[self.kind, (self.me.z + dz + 8) % 8, half]

    def over(self, dz):
        return self.mail.post(self.spot(0, dz), self.spot(0, dz), self.me.at(dy=2))

    def finish(self):
        me, mine = self.me, self.mine
        for copy in self.leg2:
            copy.wait_recv()
        for rows, got in ((pl.ds(0, 64), self.a2), (pl.ds(64, 64), self.b2)):
            total = mine[me.x, me.ylo, me.yhi, rows].astype(F32)
            for i in range(3):
                total = total + got[i].astype(F32)
            self.own[rows] = total.astype(BF)
        self.kept = pltpu.make_async_copy(self.own, self.spot(0, 0), self.sem)
        self.kept.start()
        self.swaps = [self.mail.post(self.own, self.spot(0, 0), me.at(dy=2))]
        self.direct = [
            (-dz, self.mail.post(self.own, self.spot(0, 0), me.at(dz=dz)))
            for dz in (1, -1, 2, -2, 3, -3, 4)
        ]

    def spread(self):
        for dz, copy in self.direct:
            copy.wait_recv()
            self.swaps.append(self.over(dz))

    def last(self):
        self.kept.wait()
        for copy in self.swaps:
            copy.wait_recv()


VMEM = pl.BlockSpec(memory_space=pltpu.VMEM)
SMEM = pl.BlockSpec(memory_space=pltpu.SMEM)
ANY = pl.BlockSpec(memory_space=pl.ANY)
LIMIT = 56 * 2**20


def kernel(
    q_ref, k_ref, v_ref, do_ref, span_ref, seg_ref, dq_ref, result,
    send, recv, local_sem, q_rows, do_rows, dq_rows, kbuf, vbuf, inv, qs, ds_rows, qn, dn, kg, vg,
    s_scr, dp_scr, p_scr, ds_scr, w_scr, theirs, mine, r0, a1, b1, a2, b2, own,
):
    me = Place()
    greet(
        [me.at(dx=1), me.at(dx=-1), me.at(dx=2), me.at(dy=1), me.at(dy=-1), me.at(dy=2)]
        + [me.at(dc=1)]
        + [me.at(dz=dz) for dz in (1, -1, 2, -2, 3, -3, 4)]
    )
    mail = Mail(send, recv)
    gk = Gather(me, mail, k_ref.at[me.z], kbuf, local_sem.at[0])
    gv = Gather(me, mail, v_ref.at[me.z], vbuf, local_sem.at[1])
    gk.own_x()
    gk.own_y()
    gv.own_x()
    loads = [
        pltpu.make_async_copy(q_ref, q_rows, local_sem.at[2]),
        pltpu.make_async_copy(do_ref, do_rows, local_sem.at[3]),
    ]
    for load in loads:
        load.start()
    prepare(span_ref, inv, w_scr)
    for load in loads:
        load.wait()
    stack_heads(q_rows, do_rows, qs, ds_rows)
    gk.from_x(0)
    gk.from_x(1)
    gv.own_y()
    gk.from_y()
    gk.from_x(2)
    gv.from_x(0)
    gv.from_x(1)
    gk.from_far(0, 4)
    gv.from_y()
    gv.from_x(2)
    gk.from_far(4, 6)
    gk.complete()
    ctx = me.ctx
    window(ctx, 0, span_ref, inv, kbuf, kg)
    norms = [probs_of(ctx, 0, span_ref, seg_ref, qs, ds_rows, qn, dn, kg, s_scr, p_scr)]
    gv.from_far(0, 6)
    window_terms(0, p_scr, dn, w_scr)
    window(ctx, 1, span_ref, inv, kbuf, kg)
    norms.append(probs_of(ctx, 1, span_ref, seg_ref, qs, ds_rows, qn, dn, kg, s_scr, p_scr))
    window_terms(1, p_scr, dn, w_scr)
    dk, dv = (
        Stream(
            me, mail, kind, theirs.at[kind], mine.at[kind], r0.at[kind], a1.at[kind],
            b1.at[kind], a2.at[kind], b2.at[kind], own.at[kind], local_sem.at[4 + kind], result,
        )
        for kind in range(2)
    )
    assemble(ctx, span_ref, 1, 1 - me.core, w_scr, dv.theirs)
    dv.to_sibling()
    assemble(ctx, span_ref, 1, me.core, w_scr, dv.mine)
    gv.complete()
    window(ctx, 0, span_ref, inv, vbuf, vg)
    dscores_of(0, norms[0], ds_rows, vg, s_scr, dp_scr, ds_scr)
    dv.first_leg()
    window_terms(0, ds_scr, qn, w_scr)
    window(ctx, 1, span_ref, inv, vbuf, vg)
    dscores_of(1, norms[1], ds_rows, vg, s_scr, dp_scr, ds_scr)
    window_terms(1, ds_scr, qn, w_scr)
    assemble(ctx, span_ref, 0, 1 - me.core, w_scr, dk.theirs)
    dk.to_sibling()
    assemble(ctx, span_ref, 0, me.core, w_scr, dk.mine)
    dv.second_leg()
    dk.first_leg()
    query_grads(dq_rows, kg, ds_scr, norms)
    leave = pltpu.make_async_copy(dq_rows, dq_ref, local_sem.at[6])
    leave.start()
    dv.finish()
    dk.second_leg()
    dv.spread()
    dk.finish()
    dk.spread()
    dv.last()
    dk.last()
    leave.wait()
    mail.drain()


def cast_kernel(result, dq_in, dk, dv, dq_out, narrow, wide, sem_in, sem_out):
    through = pltpu.make_async_copy(dq_in, dq_out, sem_out.at[8])
    through.start()
    outs = (dk, dv)
    loads, stores = [], []
    for i in range(8):
        part = pl.ds(2 * (i % 4), 2)
        copy = pltpu.make_async_copy(
            result.at[i // 4, part], narrow.at[i // 4, part], sem_in.at[i]
        )
        copy.start()
        loads.append(copy)
    for i in range(8):
        part = pl.ds(2 * (i % 4), 2)
        loads[i].wait()
        wide[i // 4, part] = narrow[i // 4, part].astype(F32)
        copy = pltpu.make_async_copy(wide.at[i // 4, part], outs[i // 4].at[part], sem_out.at[i])
        copy.start()
        stores.append(copy)
    for copy in stores:
        copy.wait()
    through.wait()


def per_device(queries, keys, values, d_out, span_order, segments):
    keys = keys.reshape(8, 2, BLK, HD)
    values = values.reshape(8, 2, BLK, HD)
    dq, result = pl.pallas_call(
        kernel,
        out_shape=[
            jax.ShapeDtypeStruct((256, 512), BF),
            jax.ShapeDtypeStruct((2, 8, 2, BLK, HD), BF),
        ],
        in_specs=[ANY, ANY, ANY, ANY, SMEM, VMEM],
        out_specs=[ANY, ANY],
        scratch_shapes=[
            pltpu.SemaphoreType.DMA((112,)),
            pltpu.SemaphoreType.DMA((112,)),
            pltpu.SemaphoreType.DMA((7,)),
            pltpu.VMEM((256, 512), BF),
            pltpu.VMEM((256, 512), BF),
            pltpu.VMEM((256, 512), BF),
            pltpu.VMEM((32, BLK, HD), BF),
            pltpu.VMEM((32, BLK, HD), BF),
            pltpu.SMEM((32,), jnp.int32),
            pltpu.VMEM((2, COLS, HD), BF),
            pltpu.VMEM((2, COLS, HD), BF),
            pltpu.VMEM((2, COLS, HD), BF),
            pltpu.VMEM((2, COLS, HD), BF),
            pltpu.VMEM((2, WIN * BLK, HD), BF),
            pltpu.VMEM((2, WIN * BLK, HD), BF),
            pltpu.VMEM((2, WIN * BLK, COLS), F32),
            pltpu.VMEM((WIN * BLK, COLS), F32),
            pltpu.VMEM((2, WIN * BLK, COLS), BF),
            pltpu.VMEM((2, WIN * BLK, COLS), BF),
            pltpu.VMEM((2, WIN + 1, BLK, HD), F32),
            pltpu.VMEM((2, 4, 2, 2, BLK, HD), BF),
            pltpu.VMEM((2, 4, 2, 2, BLK, HD), BF),
            pltpu.VMEM((2, 4, 2, 2, BLK, HD), BF),
            pltpu.VMEM((2, 3, 2, 2, 64, HD), BF),
            pltpu.VMEM((2, 3, 4, 64, HD), BF),
            pltpu.VMEM((2, 3, 64, HD), BF),
            pltpu.VMEM((2, 3, 64, HD), BF),
            pltpu.VMEM((2, BLK, HD), BF),
        ],
        compiler_params=pltpu.CompilerParams(
            collective_id=0, has_side_effects=True, vmem_limit_bytes=LIMIT
        ),
        name="backward",
    )(queries, keys, values, d_out, span_order, segments.reshape(32, BLK))
    dk, dv, dq = pl.pallas_call(
        cast_kernel,
        out_shape=[
            jax.ShapeDtypeStruct((8, 2, BLK, HD), F32),
            jax.ShapeDtypeStruct((8, 2, BLK, HD), F32),
            jax.ShapeDtypeStruct((256, 512), BF),
        ],
        in_specs=[ANY, ANY],
        out_specs=[ANY, ANY, ANY],
        scratch_shapes=[
            pltpu.VMEM((2, 8, 2, BLK, HD), BF),
            pltpu.VMEM((2, 8, 2, BLK, HD), F32),
            pltpu.SemaphoreType.DMA((8,)),
            pltpu.SemaphoreType.DMA((9,)),
        ],
        compiler_params=pltpu.CompilerParams(vmem_limit_bytes=LIMIT),
        name="widen",
    )(result, dq)
    return (dq, dk.reshape(8, 256, HD), dv.reshape(8, 256, HD))


def solution(mesh):
    return jax.shard_map(
        per_device,
        mesh=mesh,
        in_specs=(
            P("ctx", "tp"),
            P(None, "ctx", None),
            P(None, "ctx", None),
            P("ctx", "tp"),
            P(),
            P(),
        ),
        out_specs=(P("ctx", "tp"), P(None, "ctx", None), P(None, "ctx", None)),
        check_vma=False,
    )
```

```python
import functools

import jax
import jax.numpy as jnp
from jax import lax
from jax.experimental import pallas as pl
from jax.experimental.pallas import tpu as pltpu
from jax.sharding import PartitionSpec as P

HD = 128
BLK = 128
HEADS_DEV = 4
COLS = HEADS_DEV * BLK
WIN = 17
NEGATIVE = -1e30
SCALE = HD**-0.5
LOG2E = 1.4426950408889634
BF = jnp.bfloat16
F32 = jnp.float32


class Place:
    def __init__(self):
        self.ctx = lax.axis_index("ctx")
        self.tp = lax.axis_index("tp")
        self.x = self.ctx // 4
        self.ylo = (self.ctx // 2) % 2
        self.core = self.ctx % 2
        self.z = self.tp // 2
        self.yhi = self.tp % 2
        self.y = self.yhi * 2 + self.ylo

    def at(self, dx=0, dy=0, dc=0, dz=0):
        x = (self.x + dx + 4) % 4
        y = (self.y + dy + 4) % 4
        c = (self.core + dc) % 2
        z = (self.z + dz + 8) % 8
        return (x * 4 + (y % 2) * 2 + c, z * 2 + y // 2)

    def block(self, dx=0, dy=0, dc=0):
        return ((self.x + dx + 4) % 4) * 4 + ((self.ylo + dy) % 2) * 2 + (self.core + dc) % 2


class Mail:
    def __init__(self, send, recv):
        self.send, self.recv, self.used, self.out = send, recv, 0, []

    def post(self, src, dst, device):
        copy = pltpu.make_async_remote_copy(
            src_ref=src,
            dst_ref=dst,
            send_sem=self.send.at[self.used],
            recv_sem=self.recv.at[self.used],
            device_id=device,
            device_id_type=pl.DeviceIdType.MESH,
        )
        self.used += 1
        copy.start()
        self.out.append(copy)
        return copy

    def drain(self):
        for copy in self.out:
            copy.wait_send()
        self.out = []


def greet(devices):
    barrier = pltpu.get_barrier_semaphore()
    for device in devices:
        pl.semaphore_signal(
            barrier, inc=1, device_id=device, device_id_type=pl.DeviceIdType.MESH
        )
    pl.semaphore_wait(barrier, len(devices))


class Gather:
    def __init__(self, me, mail, src, buf, local_sem):
        self.me, self.mail, self.src, self.buf, self.local_sem = me, mail, src, buf, local_sem
        self.sib, self.far = [], []

    def whole(self, block):
        return self.buf.at[pl.ds(2 * block, 2)]

    def half(self, block, h):
        return self.buf.at[2 * block + h]

    def share(self, block, h=None):
        ref = self.whole(block) if h is None else self.half(block, h)
        self.sib.append(self.mail.post(ref, ref, self.me.at(dc=1)))

    def along_y(self, dx, h):
        ref = self.half(self.me.block(dx=dx), h)
        copy = self.mail.post(ref, ref, self.me.at(dy=1 - 2 * h))
        self.far.append((dx, h, copy))

    def own_x(self):
        me, own = self.me, self.me.block()
        self.local = pltpu.make_async_copy(self.src, self.whole(own), self.local_sem)
        self.local.start()
        self.xs = [
            (-d, self.mail.post(self.src, self.whole(own), me.at(dx=d))) for d in (1, -1, 2)
        ]

    def own_y(self):
        me, own = self.me, self.me.block()
        self.y0 = [
            self.mail.post(self.src.at[h], self.half(own, h), me.at(dy=1 - 2 * h))
            for h in range(2)
        ]
        self.sib.append(self.mail.post(self.src, self.whole(own), me.at(dc=1)))

    def from_x(self, i):
        dx, copy = self.xs[i]
        copy.wait_recv()
        for h in range(2):
            self.along_y(dx, h)
        self.share(self.me.block(dx=dx))

    def from_y(self):
        for h in range(2):
            self.y0[h].wait_recv()
        self.share(self.me.block(dy=1))

    def from_far(self, first, last):
        for i in range(first, last):
            dx, h, copy = self.far[i]
            copy.wait_recv()
            if h == 1:
                self.share(self.me.block(dx=dx, dy=1))

    def complete(self):
        self.local.wait()
        for copy in self.sib:
            copy.wait_recv()


CHUNKS = ((0, 6), (6, 12), (12, 17))


def prepare(span_ref, inv, w_scr):
    for j in range(32):
        found = jnp.int32(0)
        for s in range(32):
            found = jnp.where(span_ref[s] == j, s, found)
        inv[j] = found
    zero = jnp.zeros((BLK, HD), F32)
    for u in range(2):
        w_scr[u, WIN] = zero


def stack_heads(q_ref, do_ref, qs, ds_rows):
    for u in range(2):
        for h in range(HEADS_DEV):
            qs[u, pl.ds(h * BLK, BLK), :] = q_ref[pl.ds(u * BLK, BLK), pl.ds(h * HD, HD)]
            ds_rows[u, pl.ds(h * BLK, BLK), :] = do_ref[pl.ds(u * BLK, BLK), pl.ds(h * HD, HD)]


def window(ctx, u, span_ref, inv, buf, out):
    p = span_ref[2 * ctx + u]
    for t in range(WIN):
        out[u, pl.ds(t * BLK, BLK), :] = buf[inv[jnp.maximum(p - (WIN - 1) + t, 0)]]


def nt_dot(a, b):
    return lax.dot_general(a, b, (((1,), (1,)), ((), ())), preferred_element_type=F32)


def probs_of(ctx, u, span_ref, seg_ref, qs, ds_rows, qn, dn, kg, s_scr, p_scr):
    p = span_ref[2 * ctx + u]
    seg_all = seg_ref[...]
    counts = [jnp.sum(jnp.where(seg_all == v, 1.0, 0.0)) for v in range(3)]
    cols2 = lax.broadcasted_iota(jnp.int32, (BLK, 2 * BLK), 1) % BLK
    rows2 = lax.broadcasted_iota(jnp.int32, (BLK, 2 * BLK), 0)
    causal = rows2 <= cols2
    rows_f = rows2.astype(F32)
    seg_row = seg_ref[pl.ds(p, 1), :]
    start = jnp.zeros((1, BLK), F32)
    for v in range(3):
        start = start + jnp.where(seg_row > v, counts[v], 0.0)
    first = (p - (WIN - 1)) * BLK
    start = start - first.astype(F32)
    start2 = jnp.concatenate([start, start], axis=1)
    inv_norms = []
    for hp in range(2):
        wide = pl.ds(hp * 256, 256)
        q2 = qs[u, wide, :]
        top = jnp.full((8, 256), NEGATIVE, F32)
        for t0, t1 in CHUNKS:
            sc = nt_dot(kg[u, pl.ds(t0 * BLK, (t1 - t0) * BLK), :], q2)
            for t in range(t0, t1):
                tile = sc[(t - t0) * BLK : (t - t0 + 1) * BLK]
                ok = rows_f >= start2 - float(t * BLK)
                if t == WIN - 1:
                    ok = ok & causal
                tile = jnp.where(ok, tile * (SCALE * LOG2E), NEGATIVE)
                s_scr[u, pl.ds(t * BLK, BLK), wide] = tile
                top = jnp.maximum(top, jnp.max(tile.reshape(16, 8, 256), axis=0))
        top = jnp.max(top, axis=0, keepdims=True)
        norm = jnp.zeros((8, 256), F32)
        for t in range(WIN):
            tile = pl.ds(t * BLK, BLK)
            pt = jnp.exp2(s_scr[u, tile, wide] - top)
            s_scr[u, tile, wide] = pt
            p_scr[u, tile, wide] = pt.astype(BF)
            norm = norm + jnp.sum(pt.reshape(16, 8, 256), axis=0)
        inv_norm = 1.0 / jnp.sum(norm, axis=0, keepdims=True)
        for i in range(2):
            row = inv_norm[:, i * BLK : (i + 1) * BLK]
            by_row = jnp.broadcast_to(row, (BLK, BLK)).T
            part = pl.ds((2 * hp + i) * BLK, BLK)
            qn[u, part, :] = (qs[u, part, :].astype(F32) * by_row).astype(BF)
            dn[u, part, :] = (ds_rows[u, part, :].astype(F32) * by_row).astype(BF)
        inv_norms.append(inv_norm)
    return inv_norms


def dscores_of(u, inv_norms, ds_rows, vg, s_scr, dp_scr, ds_scr):
    for hp in range(2):
        wide = pl.ds(hp * 256, 256)
        do2 = ds_rows[u, wide, :]
        mixed = jnp.zeros((8, 256), F32)
        for t0, t1 in CHUNKS:
            dp = nt_dot(vg[u, pl.ds(t0 * BLK, (t1 - t0) * BLK), :], do2)
            for t in range(t0, t1):
                tile = pl.ds(t * BLK, BLK)
                dpt = dp[(t - t0) * BLK : (t - t0 + 1) * BLK]
                dp_scr[tile, wide] = dpt
                mixed = mixed + jnp.sum(
                    (s_scr[u, tile, wide] * dpt).reshape(16, 8, 256), axis=0
                )
        delta = jnp.sum(mixed, axis=0, keepdims=True) * inv_norms[hp]
        for t in range(WIN):
            tile = pl.ds(t * BLK, BLK)
            ds_scr[u, tile, wide] = (s_scr[u, tile, wide] * (dp_scr[tile, wide] - delta)).astype(BF)


def query_grads(dq_ref, kg, ds_scr, norms):
    for u in range(2):
        for hp in range(2):
            dqt = lax.dot_general(
                kg[u], ds_scr[u, :, pl.ds(hp * 256, 256)],
                (((0,), (0,)), ((), ())), preferred_element_type=F32,
            ) * (norms[u][hp] * SCALE)
            for i in range(2):
                piece = dqt[:, i * BLK : (i + 1) * BLK].T
                dq_ref[pl.ds(u * BLK, BLK), pl.ds((2 * hp + i) * HD, HD)] = piece.astype(BF)


def window_terms(u, source, weights, w_scr):
    for t0, t1 in CHUNKS:
        part = jnp.dot(
            source[u, pl.ds(t0 * BLK, (t1 - t0) * BLK), :], weights[u], preferred_element_type=F32
        )
        w_scr[u, pl.ds(t0, t1 - t0)] = part.reshape(t1 - t0, BLK, HD)


def assemble(ctx, span_ref, kind, core, w_scr, terms):
    base = [span_ref[2 * ctx + u] - (WIN - 1) for u in range(2)]
    for i in range(16):
        xx, lo, h = i // 4, (i // 2) % 2, i % 2
        where = span_ref[xx * 8 + lo * 4 + core * 2 + h]
        total = None
        for u in range(2):
            t = where - base[u]
            piece = w_scr[u, jnp.where((t >= 0) & (t < WIN), t, WIN)]
            total = piece if total is None else total + piece
        if kind == 0:
            total = total * SCALE
        terms[xx, lo, h] = total.astype(BF)


class Stream:
    def __init__(self, me, mail, kind, theirs, mine, r0, a1, b1, a2, b2, own, sem, result):
        self.me, self.mail, self.kind = me, mail, kind
        self.theirs, self.mine, self.r0 = theirs, mine, r0
        self.a1, self.b1, self.a2, self.b2 = a1, b1, a2, b2
        self.own, self.sem, self.result = own, sem, result

    def to_sibling(self):
        self.half = self.mail.post(self.theirs, self.r0, self.me.at(dc=1))

    def first_leg(self):
        me, mine = self.me, self.mine
        self.half.wait_recv()
        for xx in range(4):
            mine[xx] = (mine[xx].astype(F32) + self.r0[xx].astype(F32)).astype(BF)
        self.leg1 = []
        for i, d in enumerate((1, -1, 2)):
            x = (me.x + d + 4) % 4
            y = (me.y + d + 4) % 4
            self.leg1.append(
                self.mail.post(mine.at[x, :, :, pl.ds(0, 64)], self.a1.at[i], me.at(dx=d))
            )
            self.leg1.append(
                self.mail.post(mine.at[:, y % 2, y // 2, pl.ds(64, 64)], self.b1.at[i], me.at(dy=d))
            )

    def second_leg(self):
        me, mine = self.me, self.mine
        for copy in self.leg1:
            copy.wait_recv()
        own_a = mine.at[me.x, :, :, pl.ds(0, 64)]
        own_b = mine.at[:, me.ylo, me.yhi, pl.ds(64, 64)]
        for own, got in ((own_a, self.a1), (own_b, self.b1)):
            total = own[...].astype(F32)
            for i in range(3):
                total = total + got[i].astype(F32)
            own[...] = total.astype(BF)
        self.leg2 = []
        for i, d in enumerate((1, -1, 2)):
            x = (me.x + d + 4) % 4
            y = (me.y + d + 4) % 4
            self.leg2.append(
                self.mail.post(
                    mine.at[me.x, y % 2, y // 2, pl.ds(0, 64)], self.a2.at[i], me.at(dy=d)
                )
            )
            self.leg2.append(
                self.mail.post(
                    mine.at[x, me.ylo, me.yhi, pl.ds(64, 64)], self.b2.at[i], me.at(dx=d)
                )
            )

    def spot(self, k, dz):
        half = self.me.yhi if k == 0 else 1 - self.me.yhi
        return self.result.at[self.kind, (self.me.z + dz + 8) % 8, half]

    def over(self, dz):
        return self.mail.post(self.spot(0, dz), self.spot(0, dz), self.me.at(dy=2))

    def finish(self):
        me, mine = self.me, self.mine
        for copy in self.leg2:
            copy.wait_recv()
        for rows, got in ((pl.ds(0, 64), self.a2), (pl.ds(64, 64), self.b2)):
            total = mine[me.x, me.ylo, me.yhi, rows].astype(F32)
            for i in range(3):
                total = total + got[i].astype(F32)
            self.own[rows] = total.astype(BF)
        self.kept = pltpu.make_async_copy(self.own, self.spot(0, 0), self.sem)
        self.kept.start()
        self.swaps = [self.mail.post(self.own, self.spot(0, 0), me.at(dy=2))]
        self.direct = [
            (-dz, self.mail.post(self.own, self.spot(0, 0), me.at(dz=dz)))
            for dz in (1, -1, 2, -2, 3, -3, 4)
        ]

    def spread(self):
        for dz, copy in self.direct:
            copy.wait_recv()
            self.swaps.append(self.over(dz))

    def last(self):
        self.kept.wait()
        for copy in self.swaps:
            copy.wait_recv()


VMEM = pl.BlockSpec(memory_space=pltpu.VMEM)
SMEM = pl.BlockSpec(memory_space=pltpu.SMEM)
ANY = pl.BlockSpec(memory_space=pl.ANY)
LIMIT = 56 * 2**20


def kernel(
    q_ref, k_ref, v_ref, do_ref, span_ref, seg_ref, dq_ref, result,
    send, recv, local_sem, q_rows, do_rows, dq_rows, kbuf, vbuf, inv, qs, ds_rows, qn, dn, kg, vg,
    s_scr, dp_scr, p_scr, ds_scr, w_scr, theirs, mine, r0, a1, b1, a2, b2, own,
):
    me = Place()
    greet(
        [me.at(dx=1), me.at(dx=-1), me.at(dx=2), me.at(dy=1), me.at(dy=-1), me.at(dy=2)]
        + [me.at(dc=1)]
        + [me.at(dz=dz) for dz in (1, -1, 2, -2, 3, -3, 4)]
    )
    mail = Mail(send, recv)
    gk = Gather(me, mail, k_ref.at[me.z], kbuf, local_sem.at[0])
    gv = Gather(me, mail, v_ref.at[me.z], vbuf, local_sem.at[1])
    gk.own_x()
    gk.own_y()
    gv.own_x()
    loads = [
        pltpu.make_async_copy(q_ref, q_rows, local_sem.at[2]),
        pltpu.make_async_copy(do_ref, do_rows, local_sem.at[3]),
    ]
    for load in loads:
        load.start()
    prepare(span_ref, inv, w_scr)
    for load in loads:
        load.wait()
    stack_heads(q_rows, do_rows, qs, ds_rows)
    gk.from_x(0)
    gk.from_x(1)
    gv.own_y()
    gk.from_y()
    gk.from_x(2)
    gv.from_x(0)
    gv.from_x(1)
    gk.from_far(0, 4)
    gv.from_y()
    gv.from_x(2)
    gk.from_far(4, 6)
    gk.complete()
    ctx = me.ctx
    window(ctx, 0, span_ref, inv, kbuf, kg)
    norms = [probs_of(ctx, 0, span_ref, seg_ref, qs, ds_rows, qn, dn, kg, s_scr, p_scr)]
    gv.from_far(0, 6)
    window_terms(0, p_scr, dn, w_scr)
    window(ctx, 1, span_ref, inv, kbuf, kg)
    norms.append(probs_of(ctx, 1, span_ref, seg_ref, qs, ds_rows, qn, dn, kg, s_scr, p_scr))
    window_terms(1, p_scr, dn, w_scr)
    dk, dv = (
        Stream(
            me, mail, kind, theirs.at[kind], mine.at[kind], r0.at[kind], a1.at[kind],
            b1.at[kind], a2.at[kind], b2.at[kind], own.at[kind], local_sem.at[4 + kind], result,
        )
        for kind in range(2)
    )
    assemble(ctx, span_ref, 1, 1 - me.core, w_scr, dv.theirs)
    dv.to_sibling()
    assemble(ctx, span_ref, 1, me.core, w_scr, dv.mine)
    gv.complete()
    window(ctx, 0, span_ref, inv, vbuf, vg)
    dscores_of(0, norms[0], ds_rows, vg, s_scr, dp_scr, ds_scr)
    dv.first_leg()
    window_terms(0, ds_scr, qn, w_scr)
    window(ctx, 1, span_ref, inv, vbuf, vg)
    dscores_of(1, norms[1], ds_rows, vg, s_scr, dp_scr, ds_scr)
    window_terms(1, ds_scr, qn, w_scr)
    assemble(ctx, span_ref, 0, 1 - me.core, w_scr, dk.theirs)
    dk.to_sibling()
    assemble(ctx, span_ref, 0, me.core, w_scr, dk.mine)
    dv.second_leg()
    dk.first_leg()
    query_grads(dq_rows, kg, ds_scr, norms)
    leave = pltpu.make_async_copy(dq_rows, dq_ref, local_sem.at[6])
    leave.start()
    dv.finish()
    dk.second_leg()
    dv.spread()
    dk.finish()
    dk.spread()
    dv.last()
    dk.last()
    leave.wait()
    mail.drain()


def cast_kernel(result, dq_in, dk, dv, dq_out, narrow, wide, passing, sem_in, sem_out):
    outs = (dk, dv)
    loads, stores = [], []
    for i in range(8):
        part = pl.ds(2 * (i % 4), 2)
        copy = pltpu.make_async_copy(
            result.at[i // 4, part], narrow.at[i // 4, part], sem_in.at[i]
        )
        copy.start()
        loads.append(copy)
    inward = pltpu.make_async_copy(dq_in, passing, sem_in.at[8])
    inward.start()
    for i in range(8):
        part = pl.ds(2 * (i % 4), 2)
        loads[i].wait()
        wide[i // 4, part] = narrow[i // 4, part].astype(F32)
        copy = pltpu.make_async_copy(wide.at[i // 4, part], outs[i // 4].at[part], sem_out.at[i])
        copy.start()
        stores.append(copy)
    inward.wait()
    outward = pltpu.make_async_copy(passing, dq_out, sem_out.at[8])
    outward.start()
    for copy in stores:
        copy.wait()
    outward.wait()


def per_device(queries, keys, values, d_out, span_order, segments):
    keys = keys.reshape(8, 2, BLK, HD)
    values = values.reshape(8, 2, BLK, HD)
    dq, result = pl.pallas_call(
        kernel,
        out_shape=[
            jax.ShapeDtypeStruct((256, 512), BF),
            jax.ShapeDtypeStruct((2, 8, 2, BLK, HD), BF),
        ],
        in_specs=[ANY, ANY, ANY, ANY, SMEM, VMEM],
        out_specs=[ANY, ANY],
        scratch_shapes=[
            pltpu.SemaphoreType.DMA((112,)),
            pltpu.SemaphoreType.DMA((112,)),
            pltpu.SemaphoreType.DMA((7,)),
            pltpu.VMEM((256, 512), BF),
            pltpu.VMEM((256, 512), BF),
            pltpu.VMEM((256, 512), BF),
            pltpu.VMEM((32, BLK, HD), BF),
            pltpu.VMEM((32, BLK, HD), BF),
            pltpu.SMEM((32,), jnp.int32),
            pltpu.VMEM((2, COLS, HD), BF),
            pltpu.VMEM((2, COLS, HD), BF),
            pltpu.VMEM((2, COLS, HD), BF),
            pltpu.VMEM((2, COLS, HD), BF),
            pltpu.VMEM((2, WIN * BLK, HD), BF),
            pltpu.VMEM((2, WIN * BLK, HD), BF),
            pltpu.VMEM((2, WIN * BLK, COLS), F32),
            pltpu.VMEM((WIN * BLK, COLS), F32),
            pltpu.VMEM((2, WIN * BLK, COLS), BF),
            pltpu.VMEM((2, WIN * BLK, COLS), BF),
            pltpu.VMEM((2, WIN + 1, BLK, HD), F32),
            pltpu.VMEM((2, 4, 2, 2, BLK, HD), BF),
            pltpu.VMEM((2, 4, 2, 2, BLK, HD), BF),
            pltpu.VMEM((2, 4, 2, 2, BLK, HD), BF),
            pltpu.VMEM((2, 3, 2, 2, 64, HD), BF),
            pltpu.VMEM((2, 3, 4, 64, HD), BF),
            pltpu.VMEM((2, 3, 64, HD), BF),
            pltpu.VMEM((2, 3, 64, HD), BF),
            pltpu.VMEM((2, BLK, HD), BF),
        ],
        compiler_params=pltpu.CompilerParams(
            collective_id=0, has_side_effects=True, vmem_limit_bytes=LIMIT
        ),
        name="backward",
    )(queries, keys, values, d_out, span_order, segments.reshape(32, BLK))
    dk, dv, dq = pl.pallas_call(
        cast_kernel,
        out_shape=[
            jax.ShapeDtypeStruct((8, 2, BLK, HD), F32),
            jax.ShapeDtypeStruct((8, 2, BLK, HD), F32),
            jax.ShapeDtypeStruct((256, 512), BF),
        ],
        in_specs=[ANY, ANY],
        out_specs=[ANY, ANY, ANY],
        scratch_shapes=[
            pltpu.VMEM((2, 8, 2, BLK, HD), BF),
            pltpu.VMEM((2, 8, 2, BLK, HD), F32),
            pltpu.VMEM((256, 512), BF),
            pltpu.SemaphoreType.DMA((9,)),
            pltpu.SemaphoreType.DMA((9,)),
        ],
        compiler_params=pltpu.CompilerParams(vmem_limit_bytes=LIMIT),
        name="widen",
    )(result, dq)
    return (dq, dk.reshape(8, 256, HD), dv.reshape(8, 256, HD))


def solution(mesh):
    return jax.shard_map(
        per_device,
        mesh=mesh,
        in_specs=(
            P("ctx", "tp"),
            P(None, "ctx", None),
            P(None, "ctx", None),
            P("ctx", "tp"),
            P(),
            P(),
        ),
        out_specs=(P("ctx", "tp"), P(None, "ctx", None), P(None, "ctx", None)),
        check_vma=False,
    )
```

```python
import functools

import jax
import jax.numpy as jnp
from jax import lax
from jax.experimental import pallas as pl
from jax.experimental.pallas import tpu as pltpu
from jax.sharding import PartitionSpec as P

HD = 128
BLK = 128
HEADS_DEV = 4
COLS = HEADS_DEV * BLK
WIN = 17
NEGATIVE = -1e30
SCALE = HD**-0.5
LOG2E = 1.4426950408889634
BF = jnp.bfloat16
F32 = jnp.float32


class Place:
    def __init__(self):
        self.ctx = lax.axis_index("ctx")
        self.tp = lax.axis_index("tp")
        self.x = self.ctx // 4
        self.ylo = (self.ctx // 2) % 2
        self.core = self.ctx % 2
        self.z = self.tp // 2
        self.yhi = self.tp % 2
        self.y = self.yhi * 2 + self.ylo

    def at(self, dx=0, dy=0, dc=0, dz=0):
        x = (self.x + dx + 4) % 4
        y = (self.y + dy + 4) % 4
        c = (self.core + dc) % 2
        z = (self.z + dz + 8) % 8
        return (x * 4 + (y % 2) * 2 + c, z * 2 + y // 2)

    def block(self, dx=0, dy=0, dc=0):
        return ((self.x + dx + 4) % 4) * 4 + ((self.ylo + dy) % 2) * 2 + (self.core + dc) % 2


class Mail:
    def __init__(self, send, recv):
        self.send, self.recv, self.used, self.out = send, recv, 0, []

    def post(self, src, dst, device):
        copy = pltpu.make_async_remote_copy(
            src_ref=src,
            dst_ref=dst,
            send_sem=self.send.at[self.used],
            recv_sem=self.recv.at[self.used],
            device_id=device,
            device_id_type=pl.DeviceIdType.MESH,
        )
        self.used += 1
        copy.start()
        self.out.append(copy)
        return copy

    def drain(self):
        for copy in self.out:
            copy.wait_send()
        self.out = []


def greet(devices):
    barrier = pltpu.get_barrier_semaphore()
    for device in devices:
        pl.semaphore_signal(
            barrier, inc=1, device_id=device, device_id_type=pl.DeviceIdType.MESH
        )
    pl.semaphore_wait(barrier, len(devices))


class Gather:
    def __init__(self, me, mail, src, buf, local_sem):
        self.me, self.mail, self.src, self.buf, self.local_sem = me, mail, src, buf, local_sem
        self.sib, self.far = [], []

    def whole(self, block):
        return self.buf.at[pl.ds(2 * block, 2)]

    def half(self, block, h):
        return self.buf.at[2 * block + h]

    def share(self, block, h=None):
        ref = self.whole(block) if h is None else self.half(block, h)
        self.sib.append(self.mail.post(ref, ref, self.me.at(dc=1)))

    def along_y(self, dx, h):
        ref = self.half(self.me.block(dx=dx), h)
        copy = self.mail.post(ref, ref, self.me.at(dy=1 - 2 * h))
        self.far.append((dx, h, copy))

    def own_x(self):
        me, own = self.me, self.me.block()
        self.local = pltpu.make_async_copy(self.src, self.whole(own), self.local_sem)
        self.local.start()
        self.xs = [
            (-d, self.mail.post(self.src, self.whole(own), me.at(dx=d))) for d in (1, -1, 2)
        ]

    def own_y(self):
        me, own = self.me, self.me.block()
        self.y0 = [
            self.mail.post(self.src.at[h], self.half(own, h), me.at(dy=1 - 2 * h))
            for h in range(2)
        ]
        self.sib.append(self.mail.post(self.src, self.whole(own), me.at(dc=1)))

    def from_x(self, i):
        dx, copy = self.xs[i]
        copy.wait_recv()
        for h in range(2):
            self.along_y(dx, h)
        self.share(self.me.block(dx=dx))

    def from_y(self):
        for h in range(2):
            self.y0[h].wait_recv()
        self.share(self.me.block(dy=1))

    def from_far(self, first, last):
        for i in range(first, last):
            dx, h, copy = self.far[i]
            copy.wait_recv()
            if h == 1:
                self.share(self.me.block(dx=dx, dy=1))

    def complete(self):
        self.local.wait()
        for copy in self.sib:
            copy.wait_recv()


CHUNKS = ((0, 6), (6, 12), (12, 17))


def prepare(span_ref, inv, w_scr):
    for j in range(32):
        found = jnp.int32(0)
        for s in range(32):
            found = jnp.where(span_ref[s] == j, s, found)
        inv[j] = found
    zero = jnp.zeros((BLK, HD), F32)
    for u in range(2):
        w_scr[u, WIN] = zero


def stack_heads(q_ref, do_ref, qs, ds_rows):
    for u in range(2):
        for h in range(HEADS_DEV):
            qs[u, pl.ds(h * BLK, BLK), :] = q_ref[pl.ds(u * BLK, BLK), pl.ds(h * HD, HD)]
            ds_rows[u, pl.ds(h * BLK, BLK), :] = do_ref[pl.ds(u * BLK, BLK), pl.ds(h * HD, HD)]


def window(ctx, u, span_ref, inv, buf, out):
    p = span_ref[2 * ctx + u]
    for t in range(WIN):
        out[u, pl.ds(t * BLK, BLK), :] = buf[inv[jnp.maximum(p - (WIN - 1) + t, 0)]]


def nt_dot(a, b):
    return lax.dot_general(a, b, (((1,), (1,)), ((), ())), preferred_element_type=F32)


def probs_of(ctx, u, span_ref, seg_ref, qs, ds_rows, qn, dn, kg, s_scr, p_scr):
    p = span_ref[2 * ctx + u]
    seg_all = seg_ref[...]
    counts = [jnp.sum(jnp.where(seg_all == v, 1.0, 0.0)) for v in range(3)]
    cols2 = lax.broadcasted_iota(jnp.int32, (BLK, 2 * BLK), 1) % BLK
    rows2 = lax.broadcasted_iota(jnp.int32, (BLK, 2 * BLK), 0)
    causal = rows2 <= cols2
    rows_f = rows2.astype(F32)
    seg_row = seg_ref[pl.ds(p, 1), :]
    start = jnp.zeros((1, BLK), F32)
    for v in range(3):
        start = start + jnp.where(seg_row > v, counts[v], 0.0)
    first = (p - (WIN - 1)) * BLK
    start = start - first.astype(F32)
    start2 = jnp.concatenate([start, start], axis=1)
    inv_norms = []
    for hp in range(2):
        wide = pl.ds(hp * 256, 256)
        q2 = qs[u, wide, :]
        top = jnp.full((8, 256), NEGATIVE, F32)
        for t0, t1 in CHUNKS:
            sc = nt_dot(kg[u, pl.ds(t0 * BLK, (t1 - t0) * BLK), :], q2)
            for t in range(t0, t1):
                tile = sc[(t - t0) * BLK : (t - t0 + 1) * BLK]
                ok = rows_f >= start2 - float(t * BLK)
                if t == WIN - 1:
                    ok = ok & causal
                tile = jnp.where(ok, tile * (SCALE * LOG2E), NEGATIVE)
                s_scr[u, pl.ds(t * BLK, BLK), wide] = tile
                top = jnp.maximum(top, jnp.max(tile.reshape(16, 8, 256), axis=0))
        top = jnp.max(top, axis=0, keepdims=True)
        norm = jnp.zeros((8, 256), F32)
        for t in range(WIN):
            tile = pl.ds(t * BLK, BLK)
            pt = jnp.exp2(s_scr[u, tile, wide] - top)
            s_scr[u, tile, wide] = pt
            p_scr[u, tile, wide] = pt.astype(BF)
            norm = norm + jnp.sum(pt.reshape(16, 8, 256), axis=0)
        inv_norm = 1.0 / jnp.sum(norm, axis=0, keepdims=True)
        for i in range(2):
            row = inv_norm[:, i * BLK : (i + 1) * BLK]
            by_row = jnp.broadcast_to(row, (BLK, BLK)).T
            part = pl.ds((2 * hp + i) * BLK, BLK)
            qn[u, part, :] = (qs[u, part, :].astype(F32) * by_row).astype(BF)
            dn[u, part, :] = (ds_rows[u, part, :].astype(F32) * by_row).astype(BF)
        inv_norms.append(inv_norm)
    return inv_norms


def dscores_of(u, inv_norms, ds_rows, vg, s_scr, dp_scr, ds_scr):
    for hp in range(2):
        wide = pl.ds(hp * 256, 256)
        do2 = ds_rows[u, wide, :]
        mixed = jnp.zeros((8, 256), F32)
        for t0, t1 in CHUNKS:
            dp = nt_dot(vg[u, pl.ds(t0 * BLK, (t1 - t0) * BLK), :], do2)
            for t in range(t0, t1):
                tile = pl.ds(t * BLK, BLK)
                dpt = dp[(t - t0) * BLK : (t - t0 + 1) * BLK]
                dp_scr[tile, wide] = dpt
                mixed = mixed + jnp.sum(
                    (s_scr[u, tile, wide] * dpt).reshape(16, 8, 256), axis=0
                )
        delta = jnp.sum(mixed, axis=0, keepdims=True) * inv_norms[hp]
        for t in range(WIN):
            tile = pl.ds(t * BLK, BLK)
            ds_scr[u, tile, wide] = (s_scr[u, tile, wide] * (dp_scr[tile, wide] - delta)).astype(BF)


def query_grads(dq_ref, kg, ds_scr, norms):
    for u in range(2):
        for hp in range(2):
            dqt = lax.dot_general(
                kg[u], ds_scr[u, :, pl.ds(hp * 256, 256)],
                (((0,), (0,)), ((), ())), preferred_element_type=F32,
            ) * (norms[u][hp] * SCALE)
            for i in range(2):
                piece = dqt[:, i * BLK : (i + 1) * BLK].T
                dq_ref[pl.ds(u * BLK, BLK), pl.ds((2 * hp + i) * HD, HD)] = piece.astype(BF)


def window_terms(u, source, weights, w_scr):
    for t0, t1 in CHUNKS:
        part = jnp.dot(
            source[u, pl.ds(t0 * BLK, (t1 - t0) * BLK), :], weights[u], preferred_element_type=F32
        )
        w_scr[u, pl.ds(t0, t1 - t0)] = part.reshape(t1 - t0, BLK, HD)


def assemble(ctx, span_ref, kind, core, w_scr, terms):
    base = [span_ref[2 * ctx + u] - (WIN - 1) for u in range(2)]
    for i in range(16):
        xx, lo, h = i // 4, (i // 2) % 2, i % 2
        where = span_ref[xx * 8 + lo * 4 + core * 2 + h]
        total = None
        for u in range(2):
            t = where - base[u]
            piece = w_scr[u, jnp.where((t >= 0) & (t < WIN), t, WIN)]
            total = piece if total is None else total + piece
        if kind == 0:
            total = total * SCALE
        terms[xx, lo, h] = total.astype(BF)


class Stream:
    def __init__(self, me, mail, kind, theirs, mine, r0, a1, b1, a2, b2, own, sem, result):
        self.me, self.mail, self.kind = me, mail, kind
        self.theirs, self.mine, self.r0 = theirs, mine, r0
        self.a1, self.b1, self.a2, self.b2 = a1, b1, a2, b2
        self.own, self.sem, self.result = own, sem, result

    def to_sibling(self):
        self.half = self.mail.post(self.theirs, self.r0, self.me.at(dc=1))

    def first_leg(self):
        me, mine = self.me, self.mine
        self.half.wait_recv()
        for xx in range(4):
            mine[xx] = (mine[xx].astype(F32) + self.r0[xx].astype(F32)).astype(BF)
        self.leg1 = []
        for i, d in enumerate((1, -1, 2)):
            x = (me.x + d + 4) % 4
            y = (me.y + d + 4) % 4
            self.leg1.append(
                self.mail.post(mine.at[x, :, :, pl.ds(0, 64)], self.a1.at[i], me.at(dx=d))
            )
            self.leg1.append(
                self.mail.post(mine.at[:, y % 2, y // 2, pl.ds(64, 64)], self.b1.at[i], me.at(dy=d))
            )

    def second_leg(self):
        me, mine = self.me, self.mine
        for copy in self.leg1:
            copy.wait_recv()
        own_a = mine.at[me.x, :, :, pl.ds(0, 64)]
        own_b = mine.at[:, me.ylo, me.yhi, pl.ds(64, 64)]
        for own, got in ((own_a, self.a1), (own_b, self.b1)):
            total = own[...].astype(F32)
            for i in range(3):
                total = total + got[i].astype(F32)
            own[...] = total.astype(BF)
        self.leg2 = []
        for i, d in enumerate((1, -1, 2)):
            x = (me.x + d + 4) % 4
            y = (me.y + d + 4) % 4
            self.leg2.append(
                self.mail.post(
                    mine.at[me.x, y % 2, y // 2, pl.ds(0, 64)], self.a2.at[i], me.at(dy=d)
                )
            )
            self.leg2.append(
                self.mail.post(
                    mine.at[x, me.ylo, me.yhi, pl.ds(64, 64)], self.b2.at[i], me.at(dx=d)
                )
            )

    def spot(self, k, dz):
        half = self.me.yhi if k == 0 else 1 - self.me.yhi
        return self.result.at[self.kind, (self.me.z + dz + 8) % 8, half]

    def over(self, dz):
        return self.mail.post(self.spot(0, dz), self.spot(0, dz), self.me.at(dy=2))

    def finish(self):
        me, mine = self.me, self.mine
        for copy in self.leg2:
            copy.wait_recv()
        for rows, got in ((pl.ds(0, 64), self.a2), (pl.ds(64, 64), self.b2)):
            total = mine[me.x, me.ylo, me.yhi, rows].astype(F32)
            for i in range(3):
                total = total + got[i].astype(F32)
            self.own[rows] = total.astype(BF)
        self.kept = pltpu.make_async_copy(self.own, self.spot(0, 0), self.sem)
        self.kept.start()
        self.swaps = [self.mail.post(self.own, self.spot(0, 0), me.at(dy=2))]
        self.direct = [
            (-dz, self.mail.post(self.own, self.spot(0, 0), me.at(dz=dz)))
            for dz in (4, 3, -3, 2, -2, 1, -1)
        ]

    def swapped(self):
        self.swaps[0].wait_recv()
        self.near = [
            self.mail.post(self.spot(1, 0), self.spot(1, 0), self.me.at(dz=dz)) for dz in (1, -1)
        ]

    def spread(self):
        for dz, copy in self.direct:
            copy.wait_recv()
            if abs(dz) != 1:
                self.swaps.append(self.over(dz))

    def last(self):
        self.kept.wait()
        for copy in self.swaps[1:] + self.near:
            copy.wait_recv()


VMEM = pl.BlockSpec(memory_space=pltpu.VMEM)
SMEM = pl.BlockSpec(memory_space=pltpu.SMEM)
ANY = pl.BlockSpec(memory_space=pl.ANY)
LIMIT = 56 * 2**20


def kernel(
    q_ref, k_ref, v_ref, do_ref, span_ref, seg_ref, dq_ref, result,
    send, recv, local_sem, q_rows, do_rows, dq_rows, kbuf, vbuf, inv, qs, ds_rows, qn, dn, kg, vg,
    s_scr, dp_scr, p_scr, ds_scr, w_scr, theirs, mine, r0, a1, b1, a2, b2, own,
):
    me = Place()
    greet(
        [me.at(dx=1), me.at(dx=-1), me.at(dx=2), me.at(dy=1), me.at(dy=-1), me.at(dy=2)]
        + [me.at(dc=1)]
        + [me.at(dz=dz) for dz in (1, -1, 2, -2, 3, -3, 4)]
    )
    mail = Mail(send, recv)
    gk = Gather(me, mail, k_ref.at[me.z], kbuf, local_sem.at[0])
    gv = Gather(me, mail, v_ref.at[me.z], vbuf, local_sem.at[1])
    gk.own_x()
    gk.own_y()
    gv.own_x()
    loads = [
        pltpu.make_async_copy(q_ref, q_rows, local_sem.at[2]),
        pltpu.make_async_copy(do_ref, do_rows, local_sem.at[3]),
    ]
    for load in loads:
        load.start()
    prepare(span_ref, inv, w_scr)
    for load in loads:
        load.wait()
    stack_heads(q_rows, do_rows, qs, ds_rows)
    gk.from_x(0)
    gk.from_x(1)
    gv.own_y()
    gk.from_y()
    gk.from_x(2)
    gv.from_x(0)
    gv.from_x(1)
    gk.from_far(0, 4)
    gv.from_y()
    gv.from_x(2)
    gk.from_far(4, 6)
    gk.complete()
    ctx = me.ctx
    window(ctx, 0, span_ref, inv, kbuf, kg)
    norms = [probs_of(ctx, 0, span_ref, seg_ref, qs, ds_rows, qn, dn, kg, s_scr, p_scr)]
    gv.from_far(0, 6)
    window_terms(0, p_scr, dn, w_scr)
    window(ctx, 1, span_ref, inv, kbuf, kg)
    norms.append(probs_of(ctx, 1, span_ref, seg_ref, qs, ds_rows, qn, dn, kg, s_scr, p_scr))
    window_terms(1, p_scr, dn, w_scr)
    dk, dv = (
        Stream(
            me, mail, kind, theirs.at[kind], mine.at[kind], r0.at[kind], a1.at[kind],
            b1.at[kind], a2.at[kind], b2.at[kind], own.at[kind], local_sem.at[4 + kind], result,
        )
        for kind in range(2)
    )
    assemble(ctx, span_ref, 1, 1 - me.core, w_scr, dv.theirs)
    dv.to_sibling()
    assemble(ctx, span_ref, 1, me.core, w_scr, dv.mine)
    gv.complete()
    window(ctx, 0, span_ref, inv, vbuf, vg)
    dscores_of(0, norms[0], ds_rows, vg, s_scr, dp_scr, ds_scr)
    dv.first_leg()
    window_terms(0, ds_scr, qn, w_scr)
    window(ctx, 1, span_ref, inv, vbuf, vg)
    dscores_of(1, norms[1], ds_rows, vg, s_scr, dp_scr, ds_scr)
    window_terms(1, ds_scr, qn, w_scr)
    assemble(ctx, span_ref, 0, 1 - me.core, w_scr, dk.theirs)
    dk.to_sibling()
    assemble(ctx, span_ref, 0, me.core, w_scr, dk.mine)
    dv.second_leg()
    dk.first_leg()
    query_grads(dq_rows, kg, ds_scr, norms)
    leave = pltpu.make_async_copy(dq_rows, dq_ref, local_sem.at[6])
    leave.start()
    dv.finish()
    dk.second_leg()
    dv.swapped()
    dk.finish()
    dv.spread()
    dk.swapped()
    dk.spread()
    dv.last()
    dk.last()
    leave.wait()
    mail.drain()


def cast_kernel(result, dq_in, dk, dv, dq_out, narrow, wide, passing, sem_in, sem_out):
    outs = (dk, dv)
    loads, stores = [], []
    for i in range(8):
        part = pl.ds(2 * (i % 4), 2)
        copy = pltpu.make_async_copy(
            result.at[i // 4, part], narrow.at[i // 4, part], sem_in.at[i]
        )
        copy.start()
        loads.append(copy)
    inward = pltpu.make_async_copy(dq_in, passing, sem_in.at[8])
    inward.start()
    for i in range(8):
        part = pl.ds(2 * (i % 4), 2)
        loads[i].wait()
        wide[i // 4, part] = narrow[i // 4, part].astype(F32)
        copy = pltpu.make_async_copy(wide.at[i // 4, part], outs[i // 4].at[part], sem_out.at[i])
        copy.start()
        stores.append(copy)
    inward.wait()
    outward = pltpu.make_async_copy(passing, dq_out, sem_out.at[8])
    outward.start()
    for copy in stores:
        copy.wait()
    outward.wait()


def per_device(queries, keys, values, d_out, span_order, segments):
    keys = keys.reshape(8, 2, BLK, HD)
    values = values.reshape(8, 2, BLK, HD)
    dq, result = pl.pallas_call(
        kernel,
        out_shape=[
            jax.ShapeDtypeStruct((256, 512), BF),
            jax.ShapeDtypeStruct((2, 8, 2, BLK, HD), BF),
        ],
        in_specs=[ANY, ANY, ANY, ANY, SMEM, VMEM],
        out_specs=[ANY, ANY],
        scratch_shapes=[
            pltpu.SemaphoreType.DMA((112,)),
            pltpu.SemaphoreType.DMA((112,)),
            pltpu.SemaphoreType.DMA((7,)),
            pltpu.VMEM((256, 512), BF),
            pltpu.VMEM((256, 512), BF),
            pltpu.VMEM((256, 512), BF),
            pltpu.VMEM((32, BLK, HD), BF),
            pltpu.VMEM((32, BLK, HD), BF),
            pltpu.SMEM((32,), jnp.int32),
            pltpu.VMEM((2, COLS, HD), BF),
            pltpu.VMEM((2, COLS, HD), BF),
            pltpu.VMEM((2, COLS, HD), BF),
            pltpu.VMEM((2, COLS, HD), BF),
            pltpu.VMEM((2, WIN * BLK, HD), BF),
            pltpu.VMEM((2, WIN * BLK, HD), BF),
            pltpu.VMEM((2, WIN * BLK, COLS), F32),
            pltpu.VMEM((WIN * BLK, COLS), F32),
            pltpu.VMEM((2, WIN * BLK, COLS), BF),
            pltpu.VMEM((2, WIN * BLK, COLS), BF),
            pltpu.VMEM((2, WIN + 1, BLK, HD), F32),
            pltpu.VMEM((2, 4, 2, 2, BLK, HD), BF),
            pltpu.VMEM((2, 4, 2, 2, BLK, HD), BF),
            pltpu.VMEM((2, 4, 2, 2, BLK, HD), BF),
            pltpu.VMEM((2, 3, 2, 2, 64, HD), BF),
            pltpu.VMEM((2, 3, 4, 64, HD), BF),
            pltpu.VMEM((2, 3, 64, HD), BF),
            pltpu.VMEM((2, 3, 64, HD), BF),
            pltpu.VMEM((2, BLK, HD), BF),
        ],
        compiler_params=pltpu.CompilerParams(
            collective_id=0, has_side_effects=True, vmem_limit_bytes=LIMIT
        ),
        name="backward",
    )(queries, keys, values, d_out, span_order, segments.reshape(32, BLK))
    dk, dv, dq = pl.pallas_call(
        cast_kernel,
        out_shape=[
            jax.ShapeDtypeStruct((8, 2, BLK, HD), F32),
            jax.ShapeDtypeStruct((8, 2, BLK, HD), F32),
            jax.ShapeDtypeStruct((256, 512), BF),
        ],
        in_specs=[ANY, ANY],
        out_specs=[ANY, ANY, ANY],
        scratch_shapes=[
            pltpu.VMEM((2, 8, 2, BLK, HD), BF),
            pltpu.VMEM((2, 8, 2, BLK, HD), F32),
            pltpu.VMEM((256, 512), BF),
            pltpu.SemaphoreType.DMA((9,)),
            pltpu.SemaphoreType.DMA((9,)),
        ],
        compiler_params=pltpu.CompilerParams(vmem_limit_bytes=LIMIT),
        name="widen",
    )(result, dq)
    return (dq, dk.reshape(8, 256, HD), dv.reshape(8, 256, HD))


def solution(mesh):
    return jax.shard_map(
        per_device,
        mesh=mesh,
        in_specs=(
            P("ctx", "tp"),
            P(None, "ctx", None),
            P(None, "ctx", None),
            P("ctx", "tp"),
            P(),
            P(),
        ),
        out_specs=(P("ctx", "tp"), P(None, "ctx", None), P(None, "ctx", None)),
        check_vma=False,
    )
```

```python
import functools

import jax
import jax.numpy as jnp
from jax import lax
from jax.experimental import pallas as pl
from jax.experimental.pallas import tpu as pltpu
from jax.sharding import PartitionSpec as P

HD = 128
BLK = 128
HEADS_DEV = 4
COLS = HEADS_DEV * BLK
WIN = 17
NEGATIVE = -1e30
SCALE = HD**-0.5
LOG2E = 1.4426950408889634
BF = jnp.bfloat16
F32 = jnp.float32


class Place:
    def __init__(self):
        self.ctx = lax.axis_index("ctx")
        self.tp = lax.axis_index("tp")
        self.x = self.ctx // 4
        self.ylo = (self.ctx // 2) % 2
        self.core = self.ctx % 2
        self.z = self.tp // 2
        self.yhi = self.tp % 2
        self.y = self.yhi * 2 + self.ylo

    def at(self, dx=0, dy=0, dc=0, dz=0):
        x = (self.x + dx + 4) % 4
        y = (self.y + dy + 4) % 4
        c = (self.core + dc) % 2
        z = (self.z + dz + 8) % 8
        return (x * 4 + (y % 2) * 2 + c, z * 2 + y // 2)

    def block(self, dx=0, dy=0, dc=0):
        return ((self.x + dx + 4) % 4) * 4 + ((self.ylo + dy) % 2) * 2 + (self.core + dc) % 2


class Mail:
    def __init__(self, send, recv):
        self.send, self.recv, self.used, self.out = send, recv, 0, []

    def post(self, src, dst, device):
        copy = pltpu.make_async_remote_copy(
            src_ref=src,
            dst_ref=dst,
            send_sem=self.send.at[self.used],
            recv_sem=self.recv.at[self.used],
            device_id=device,
            device_id_type=pl.DeviceIdType.MESH,
        )
        self.used += 1
        copy.start()
        self.out.append(copy)
        return copy

    def drain(self):
        for copy in self.out:
            copy.wait_send()
        self.out = []


def greet(devices):
    barrier = pltpu.get_barrier_semaphore()
    for device in devices:
        pl.semaphore_signal(
            barrier, inc=1, device_id=device, device_id_type=pl.DeviceIdType.MESH
        )
    pl.semaphore_wait(barrier, len(devices))


class Gather:
    def __init__(self, me, mail, src, buf, local_sem):
        self.me, self.mail, self.src, self.buf, self.local_sem = me, mail, src, buf, local_sem
        self.sib, self.far = [], []

    def whole(self, block):
        return self.buf.at[pl.ds(2 * block, 2)]

    def half(self, block, h):
        return self.buf.at[2 * block + h]

    def share(self, block, h=None):
        ref = self.whole(block) if h is None else self.half(block, h)
        self.sib.append(self.mail.post(ref, ref, self.me.at(dc=1)))

    def along_y(self, dx, h):
        ref = self.half(self.me.block(dx=dx), h)
        copy = self.mail.post(ref, ref, self.me.at(dy=1 - 2 * h))
        self.far.append((dx, h, copy))

    def own_x(self):
        me, own = self.me, self.me.block()
        self.local = pltpu.make_async_copy(self.src, self.whole(own), self.local_sem)
        self.local.start()
        self.xs = [
            (-d, self.mail.post(self.src, self.whole(own), me.at(dx=d))) for d in (1, -1, 2)
        ]

    def own_y(self):
        me, own = self.me, self.me.block()
        self.y0 = [
            self.mail.post(self.src.at[h], self.half(own, h), me.at(dy=1 - 2 * h))
            for h in range(2)
        ]
        self.sib.append(self.mail.post(self.src, self.whole(own), me.at(dc=1)))

    def from_x(self, i):
        dx, copy = self.xs[i]
        copy.wait_recv()
        for h in range(2):
            self.along_y(dx, h)
        self.share(self.me.block(dx=dx))

    def from_y(self):
        for h in range(2):
            self.y0[h].wait_recv()
        self.share(self.me.block(dy=1))

    def from_far(self, first, last):
        for i in range(first, last):
            dx, h, copy = self.far[i]
            copy.wait_recv()
            if h == 1:
                self.share(self.me.block(dx=dx, dy=1))

    def complete(self):
        self.local.wait()
        for copy in self.sib:
            copy.wait_recv()


CHUNKS = ((0, 6), (6, 12), (12, 17))


def prepare(span_ref, inv, w_scr):
    for j in range(32):
        found = jnp.int32(0)
        for s in range(32):
            found = jnp.where(span_ref[s] == j, s, found)
        inv[j] = found
    zero = jnp.zeros((BLK, HD), F32)
    for u in range(2):
        w_scr[u, WIN] = zero


def stack_heads(q_ref, do_ref, qs, ds_rows):
    for u in range(2):
        for h in range(HEADS_DEV):
            qs[u, pl.ds(h * BLK, BLK), :] = q_ref[pl.ds(u * BLK, BLK), pl.ds(h * HD, HD)]
            ds_rows[u, pl.ds(h * BLK, BLK), :] = do_ref[pl.ds(u * BLK, BLK), pl.ds(h * HD, HD)]


def window(ctx, u, span_ref, inv, buf, out):
    p = span_ref[2 * ctx + u]
    for t in range(WIN):
        out[u, pl.ds(t * BLK, BLK), :] = buf[inv[jnp.maximum(p - (WIN - 1) + t, 0)]]


def nt_dot(a, b):
    return lax.dot_general(a, b, (((1,), (1,)), ((), ())), preferred_element_type=F32)


def probs_of(ctx, u, span_ref, seg_ref, qs, ds_rows, qn, dn, kg, s_scr, p_scr):
    p = span_ref[2 * ctx + u]
    seg_all = seg_ref[...]
    counts = [jnp.sum(jnp.where(seg_all == v, 1.0, 0.0)) for v in range(3)]
    cols2 = lax.broadcasted_iota(jnp.int32, (BLK, 2 * BLK), 1) % BLK
    rows2 = lax.broadcasted_iota(jnp.int32, (BLK, 2 * BLK), 0)
    causal = rows2 <= cols2
    rows_f = rows2.astype(F32)
    seg_row = seg_ref[pl.ds(p, 1), :]
    start = jnp.zeros((1, BLK), F32)
    for v in range(3):
        start = start + jnp.where(seg_row > v, counts[v], 0.0)
    first = (p - (WIN - 1)) * BLK
    start = start - first.astype(F32)
    start2 = jnp.concatenate([start, start], axis=1)
    inv_norms = []
    for hp in range(2):
        wide = pl.ds(hp * 256, 256)
        q2 = qs[u, wide, :]
        top = jnp.full((8, 256), NEGATIVE, F32)
        for t0, t1 in CHUNKS:
            sc = nt_dot(kg[u, pl.ds(t0 * BLK, (t1 - t0) * BLK), :], q2)
            for t in range(t0, t1):
                tile = sc[(t - t0) * BLK : (t - t0 + 1) * BLK]
                ok = rows_f >= start2 - float(t * BLK)
                if t == WIN - 1:
                    ok = ok & causal
                tile = jnp.where(ok, tile * (SCALE * LOG2E), NEGATIVE)
                s_scr[u, pl.ds(t * BLK, BLK), wide] = tile
                top = jnp.maximum(top, jnp.max(tile.reshape(16, 8, 256), axis=0))
        top = jnp.max(top, axis=0, keepdims=True)
        norm = jnp.zeros((8, 256), F32)
        for t in range(WIN):
            tile = pl.ds(t * BLK, BLK)
            pt = jnp.exp2(s_scr[u, tile, wide] - top)
            s_scr[u, tile, wide] = pt
            p_scr[u, tile, wide] = pt.astype(BF)
            norm = norm + jnp.sum(pt.reshape(16, 8, 256), axis=0)
        inv_norm = 1.0 / jnp.sum(norm, axis=0, keepdims=True)
        for i in range(2):
            row = inv_norm[:, i * BLK : (i + 1) * BLK]
            by_row = jnp.broadcast_to(row, (BLK, BLK)).T
            part = pl.ds((2 * hp + i) * BLK, BLK)
            qn[u, part, :] = (qs[u, part, :].astype(F32) * by_row).astype(BF)
            dn[u, part, :] = (ds_rows[u, part, :].astype(F32) * by_row).astype(BF)
        inv_norms.append(inv_norm)
    return inv_norms


def dscores_of(u, inv_norms, ds_rows, vg, s_scr, dp_scr, ds_scr):
    for hp in range(2):
        wide = pl.ds(hp * 256, 256)
        do2 = ds_rows[u, wide, :]
        mixed = jnp.zeros((8, 256), F32)
        for t0, t1 in CHUNKS:
            dp = nt_dot(vg[u, pl.ds(t0 * BLK, (t1 - t0) * BLK), :], do2)
            for t in range(t0, t1):
                tile = pl.ds(t * BLK, BLK)
                dpt = dp[(t - t0) * BLK : (t - t0 + 1) * BLK]
                dp_scr[tile, wide] = dpt
                mixed = mixed + jnp.sum(
                    (s_scr[u, tile, wide] * dpt).reshape(16, 8, 256), axis=0
                )
        delta = jnp.sum(mixed, axis=0, keepdims=True) * inv_norms[hp]
        for t in range(WIN):
            tile = pl.ds(t * BLK, BLK)
            ds_scr[u, tile, wide] = (s_scr[u, tile, wide] * (dp_scr[tile, wide] - delta)).astype(BF)


def query_grads(dq_ref, kg, ds_scr, norms):
    for u in range(2):
        for hp in range(2):
            dqt = lax.dot_general(
                kg[u], ds_scr[u, :, pl.ds(hp * 256, 256)],
                (((0,), (0,)), ((), ())), preferred_element_type=F32,
            ) * (norms[u][hp] * SCALE)
            for i in range(2):
                piece = dqt[:, i * BLK : (i + 1) * BLK].T
                dq_ref[pl.ds(u * BLK, BLK), pl.ds((2 * hp + i) * HD, HD)] = piece.astype(BF)


def window_terms(u, source, weights, w_scr):
    for t0, t1 in CHUNKS:
        part = jnp.dot(
            source[u, pl.ds(t0 * BLK, (t1 - t0) * BLK), :], weights[u], preferred_element_type=F32
        )
        w_scr[u, pl.ds(t0, t1 - t0)] = part.reshape(t1 - t0, BLK, HD)


def assemble(ctx, span_ref, kind, core, w_scr, terms, part):
    base = [span_ref[2 * ctx + u] - (WIN - 1) for u in range(2)]
    for i in range(8 * part, 8 * part + 8):
        xx, lo, h = i // 4, (i // 2) % 2, i % 2
        where = span_ref[xx * 8 + lo * 4 + core * 2 + h]
        total = None
        for u in range(2):
            t = where - base[u]
            piece = w_scr[u, jnp.where((t >= 0) & (t < WIN), t, WIN)]
            total = piece if total is None else total + piece
        if kind == 0:
            total = total * SCALE
        terms[xx, lo, h] = total.astype(BF)


class Stream:
    def __init__(self, me, mail, kind, theirs, mine, r0, a1, b1, a2, b2, own, sem, result):
        self.me, self.mail, self.kind = me, mail, kind
        self.theirs, self.mine, self.r0 = theirs, mine, r0
        self.a1, self.b1, self.a2, self.b2 = a1, b1, a2, b2
        self.own, self.sem, self.result = own, sem, result

    def to_sibling(self, part):
        xs = pl.ds(2 * part, 2)
        copy = self.mail.post(self.theirs.at[xs], self.r0.at[xs], self.me.at(dc=1))
        self.halves = [copy] if part == 0 else self.halves + [copy]

    def first_leg(self):
        me, mine = self.me, self.mine
        for xx in range(4):
            if xx % 2 == 0:
                self.halves[xx // 2].wait_recv()
            mine[xx] = (mine[xx].astype(F32) + self.r0[xx].astype(F32)).astype(BF)
        self.leg1 = []
        for i, d in enumerate((1, -1, 2)):
            x = (me.x + d + 4) % 4
            y = (me.y + d + 4) % 4
            self.leg1.append(
                self.mail.post(mine.at[x, :, :, pl.ds(0, 64)], self.a1.at[i], me.at(dx=d))
            )
            self.leg1.append(
                self.mail.post(mine.at[:, y % 2, y // 2, pl.ds(64, 64)], self.b1.at[i], me.at(dy=d))
            )

    def second_leg(self):
        me, mine = self.me, self.mine
        for copy in self.leg1:
            copy.wait_recv()
        own_a = mine.at[me.x, :, :, pl.ds(0, 64)]
        own_b = mine.at[:, me.ylo, me.yhi, pl.ds(64, 64)]
        for own, got in ((own_a, self.a1), (own_b, self.b1)):
            total = own[...].astype(F32)
            for i in range(3):
                total = total + got[i].astype(F32)
            own[...] = total.astype(BF)
        self.leg2 = []
        for i, d in enumerate((1, -1, 2)):
            x = (me.x + d + 4) % 4
            y = (me.y + d + 4) % 4
            self.leg2.append(
                self.mail.post(
                    mine.at[me.x, y % 2, y // 2, pl.ds(0, 64)], self.a2.at[i], me.at(dy=d)
                )
            )
            self.leg2.append(
                self.mail.post(
                    mine.at[x, me.ylo, me.yhi, pl.ds(64, 64)], self.b2.at[i], me.at(dx=d)
                )
            )

    def spot(self, k, dz):
        half = self.me.yhi if k == 0 else 1 - self.me.yhi
        return self.result.at[self.kind, (self.me.z + dz + 8) % 8, half]

    def over(self, dz):
        return self.mail.post(self.spot(0, dz), self.spot(0, dz), self.me.at(dy=2))

    def finish(self):
        me, mine = self.me, self.mine
        for copy in self.leg2:
            copy.wait_recv()
        for rows, got in ((pl.ds(0, 64), self.a2), (pl.ds(64, 64), self.b2)):
            total = mine[me.x, me.ylo, me.yhi, rows].astype(F32)
            for i in range(3):
                total = total + got[i].astype(F32)
            self.own[rows] = total.astype(BF)
        self.kept = pltpu.make_async_copy(self.own, self.spot(0, 0), self.sem)
        self.kept.start()
        self.swaps = [self.mail.post(self.own, self.spot(0, 0), me.at(dy=2))]
        self.direct = [
            (-dz, self.mail.post(self.own, self.spot(0, 0), me.at(dz=dz)))
            for dz in (4, 3, -3, 2, -2, 1, -1)
        ]

    def swapped(self):
        self.swaps[0].wait_recv()
        self.near = [
            self.mail.post(self.spot(1, 0), self.spot(1, 0), self.me.at(dz=dz)) for dz in (1, -1)
        ]

    def spread(self):
        for dz, copy in self.direct:
            copy.wait_recv()
            if abs(dz) != 1:
                self.swaps.append(self.over(dz))

    def last(self):
        self.kept.wait()
        for copy in self.swaps[1:] + self.near:
            copy.wait_recv()


VMEM = pl.BlockSpec(memory_space=pltpu.VMEM)
SMEM = pl.BlockSpec(memory_space=pltpu.SMEM)
ANY = pl.BlockSpec(memory_space=pl.ANY)
LIMIT = 56 * 2**20


def kernel(
    q_ref, k_ref, v_ref, do_ref, span_ref, seg_ref, dq_ref, result,
    send, recv, local_sem, q_rows, do_rows, dq_rows, kbuf, vbuf, inv, qs, ds_rows, qn, dn, kg, vg,
    s_scr, dp_scr, p_scr, ds_scr, w_scr, theirs, mine, r0, a1, b1, a2, b2, own,
):
    me = Place()
    greet(
        [me.at(dx=1), me.at(dx=-1), me.at(dx=2), me.at(dy=1), me.at(dy=-1), me.at(dy=2)]
        + [me.at(dc=1)]
        + [me.at(dz=dz) for dz in (1, -1, 2, -2, 3, -3, 4)]
    )
    mail = Mail(send, recv)
    gk = Gather(me, mail, k_ref.at[me.z], kbuf, local_sem.at[0])
    gv = Gather(me, mail, v_ref.at[me.z], vbuf, local_sem.at[1])
    gk.own_x()
    gk.own_y()
    gv.own_x()
    loads = [
        pltpu.make_async_copy(q_ref, q_rows, local_sem.at[2]),
        pltpu.make_async_copy(do_ref, do_rows, local_sem.at[3]),
    ]
    for load in loads:
        load.start()
    gk.from_x(0)
    gk.from_x(1)
    gv.own_y()
    gk.from_y()
    gk.from_x(2)
    gv.from_x(0)
    gv.from_x(1)
    prepare(span_ref, inv, w_scr)
    gk.from_far(0, 4)
    gv.from_y()
    gv.from_x(2)
    for load in loads:
        load.wait()
    stack_heads(q_rows, do_rows, qs, ds_rows)
    gk.from_far(4, 6)
    gk.complete()
    ctx = me.ctx
    window(ctx, 0, span_ref, inv, kbuf, kg)
    norms = [probs_of(ctx, 0, span_ref, seg_ref, qs, ds_rows, qn, dn, kg, s_scr, p_scr)]
    gv.from_far(0, 6)
    window_terms(0, p_scr, dn, w_scr)
    window(ctx, 1, span_ref, inv, kbuf, kg)
    norms.append(probs_of(ctx, 1, span_ref, seg_ref, qs, ds_rows, qn, dn, kg, s_scr, p_scr))
    window_terms(1, p_scr, dn, w_scr)
    dk, dv = (
        Stream(
            me, mail, kind, theirs.at[kind], mine.at[kind], r0.at[kind], a1.at[kind],
            b1.at[kind], a2.at[kind], b2.at[kind], own.at[kind], local_sem.at[4 + kind], result,
        )
        for kind in range(2)
    )
    for part in range(2):
        assemble(ctx, span_ref, 1, 1 - me.core, w_scr, dv.theirs, part)
        dv.to_sibling(part)
    for part in range(2):
        assemble(ctx, span_ref, 1, me.core, w_scr, dv.mine, part)
    gv.complete()
    window(ctx, 0, span_ref, inv, vbuf, vg)
    dscores_of(0, norms[0], ds_rows, vg, s_scr, dp_scr, ds_scr)
    dv.first_leg()
    window_terms(0, ds_scr, qn, w_scr)
    window(ctx, 1, span_ref, inv, vbuf, vg)
    dscores_of(1, norms[1], ds_rows, vg, s_scr, dp_scr, ds_scr)
    window_terms(1, ds_scr, qn, w_scr)
    for part in range(2):
        assemble(ctx, span_ref, 0, 1 - me.core, w_scr, dk.theirs, part)
        dk.to_sibling(part)
    for part in range(2):
        assemble(ctx, span_ref, 0, me.core, w_scr, dk.mine, part)
    dv.second_leg()
    dk.first_leg()
    query_grads(dq_rows, kg, ds_scr, norms)
    leave = pltpu.make_async_copy(dq_rows, dq_ref, local_sem.at[6])
    leave.start()
    dv.finish()
    dk.second_leg()
    dv.swapped()
    dk.finish()
    dv.spread()
    dk.swapped()
    dk.spread()
    dv.last()
    dk.last()
    leave.wait()
    mail.drain()


def cast_kernel(result, dq_in, dk, dv, dq_out, narrow, wide, passing, sem_in, sem_out):
    outs = (dk, dv)
    loads, stores = [], []
    for i in range(8):
        part = pl.ds(2 * (i % 4), 2)
        copy = pltpu.make_async_copy(
            result.at[i // 4, part], narrow.at[i // 4, part], sem_in.at[i]
        )
        copy.start()
        loads.append(copy)
    inward = pltpu.make_async_copy(dq_in, passing, sem_in.at[8])
    inward.start()
    for i in range(8):
        part = pl.ds(2 * (i % 4), 2)
        loads[i].wait()
        wide[i // 4, part] = narrow[i // 4, part].astype(F32)
        copy = pltpu.make_async_copy(wide.at[i // 4, part], outs[i // 4].at[part], sem_out.at[i])
        copy.start()
        stores.append(copy)
    inward.wait()
    outward = pltpu.make_async_copy(passing, dq_out, sem_out.at[8])
    outward.start()
    for copy in stores:
        copy.wait()
    outward.wait()


def per_device(queries, keys, values, d_out, span_order, segments):
    keys = keys.reshape(8, 2, BLK, HD)
    values = values.reshape(8, 2, BLK, HD)
    dq, result = pl.pallas_call(
        kernel,
        out_shape=[
            jax.ShapeDtypeStruct((256, 512), BF),
            jax.ShapeDtypeStruct((2, 8, 2, BLK, HD), BF),
        ],
        in_specs=[ANY, ANY, ANY, ANY, SMEM, VMEM],
        out_specs=[ANY, ANY],
        scratch_shapes=[
            pltpu.SemaphoreType.DMA((112,)),
            pltpu.SemaphoreType.DMA((112,)),
            pltpu.SemaphoreType.DMA((7,)),
            pltpu.VMEM((256, 512), BF),
            pltpu.VMEM((256, 512), BF),
            pltpu.VMEM((256, 512), BF),
            pltpu.VMEM((32, BLK, HD), BF),
            pltpu.VMEM((32, BLK, HD), BF),
            pltpu.SMEM((32,), jnp.int32),
            pltpu.VMEM((2, COLS, HD), BF),
            pltpu.VMEM((2, COLS, HD), BF),
            pltpu.VMEM((2, COLS, HD), BF),
            pltpu.VMEM((2, COLS, HD), BF),
            pltpu.VMEM((2, WIN * BLK, HD), BF),
            pltpu.VMEM((2, WIN * BLK, HD), BF),
            pltpu.VMEM((2, WIN * BLK, COLS), F32),
            pltpu.VMEM((WIN * BLK, COLS), F32),
            pltpu.VMEM((2, WIN * BLK, COLS), BF),
            pltpu.VMEM((2, WIN * BLK, COLS), BF),
            pltpu.VMEM((2, WIN + 1, BLK, HD), F32),
            pltpu.VMEM((2, 4, 2, 2, BLK, HD), BF),
            pltpu.VMEM((2, 4, 2, 2, BLK, HD), BF),
            pltpu.VMEM((2, 4, 2, 2, BLK, HD), BF),
            pltpu.VMEM((2, 3, 2, 2, 64, HD), BF),
            pltpu.VMEM((2, 3, 4, 64, HD), BF),
            pltpu.VMEM((2, 3, 64, HD), BF),
            pltpu.VMEM((2, 3, 64, HD), BF),
            pltpu.VMEM((2, BLK, HD), BF),
        ],
        compiler_params=pltpu.CompilerParams(
            collective_id=0, has_side_effects=True, vmem_limit_bytes=LIMIT
        ),
        name="backward",
    )(queries, keys, values, d_out, span_order, segments.reshape(32, BLK))
    dk, dv, dq = pl.pallas_call(
        cast_kernel,
        out_shape=[
            jax.ShapeDtypeStruct((8, 2, BLK, HD), F32),
            jax.ShapeDtypeStruct((8, 2, BLK, HD), F32),
            jax.ShapeDtypeStruct((256, 512), BF),
        ],
        in_specs=[ANY, ANY],
        out_specs=[ANY, ANY, ANY],
        scratch_shapes=[
            pltpu.VMEM((2, 8, 2, BLK, HD), BF),
            pltpu.VMEM((2, 8, 2, BLK, HD), F32),
            pltpu.VMEM((256, 512), BF),
            pltpu.SemaphoreType.DMA((9,)),
            pltpu.SemaphoreType.DMA((9,)),
        ],
        compiler_params=pltpu.CompilerParams(vmem_limit_bytes=LIMIT),
        name="widen",
    )(result, dq)
    return (dq, dk.reshape(8, 256, HD), dv.reshape(8, 256, HD))


def solution(mesh):
    return jax.shard_map(
        per_device,
        mesh=mesh,
        in_specs=(
            P("ctx", "tp"),
            P(None, "ctx", None),
            P(None, "ctx", None),
            P("ctx", "tp"),
            P(),
            P(),
        ),
        out_specs=(P("ctx", "tp"), P(None, "ctx", None), P(None, "ctx", None)),
        check_vma=False,
    )
```

```python
import functools

import jax
import jax.numpy as jnp
from jax import lax
from jax.experimental import pallas as pl
from jax.experimental.pallas import tpu as pltpu
from jax.sharding import PartitionSpec as P

HD = 128
BLK = 128
HEADS_DEV = 4
COLS = HEADS_DEV * BLK
WIN = 17
NEGATIVE = -1e30
SCALE = HD**-0.5
LOG2E = 1.4426950408889634
BF = jnp.bfloat16
F32 = jnp.float32


class Place:
    def __init__(self):
        self.ctx = lax.axis_index("ctx")
        self.tp = lax.axis_index("tp")
        self.x = self.ctx // 4
        self.ylo = (self.ctx // 2) % 2
        self.core = self.ctx % 2
        self.z = self.tp // 2
        self.yhi = self.tp % 2
        self.y = self.yhi * 2 + self.ylo

    def at(self, dx=0, dy=0, dc=0, dz=0):
        x = (self.x + dx + 4) % 4
        y = (self.y + dy + 4) % 4
        c = (self.core + dc) % 2
        z = (self.z + dz + 8) % 8
        return (x * 4 + (y % 2) * 2 + c, z * 2 + y // 2)

    def block(self, dx=0, dy=0, dc=0):
        return ((self.x + dx + 4) % 4) * 4 + ((self.ylo + dy) % 2) * 2 + (self.core + dc) % 2


class Mail:
    def __init__(self, send, recv):
        self.send, self.recv, self.used, self.out = send, recv, 0, []

    def post(self, src, dst, device):
        copy = pltpu.make_async_remote_copy(
            src_ref=src,
            dst_ref=dst,
            send_sem=self.send.at[self.used],
            recv_sem=self.recv.at[self.used],
            device_id=device,
            device_id_type=pl.DeviceIdType.MESH,
        )
        self.used += 1
        copy.start()
        self.out.append(copy)
        return copy

    def drain(self):
        for copy in self.out:
            copy.wait_send()
        self.out = []


def greet(devices):
    barrier = pltpu.get_barrier_semaphore()
    for device in devices:
        pl.semaphore_signal(
            barrier, inc=1, device_id=device, device_id_type=pl.DeviceIdType.MESH
        )
    pl.semaphore_wait(barrier, len(devices))


class Gather:
    def __init__(self, me, mail, src, buf, local_sem):
        self.me, self.mail, self.src, self.buf, self.local_sem = me, mail, src, buf, local_sem
        self.sib, self.far = [], []

    def whole(self, block):
        return self.buf.at[pl.ds(2 * block, 2)]

    def half(self, block, h):
        return self.buf.at[2 * block + h]

    def share(self, block, h=None):
        ref = self.whole(block) if h is None else self.half(block, h)
        self.sib.append(self.mail.post(ref, ref, self.me.at(dc=1)))

    def along_y(self, dx, h):
        ref = self.half(self.me.block(dx=dx), h)
        copy = self.mail.post(ref, ref, self.me.at(dy=1 - 2 * h))
        self.far.append((dx, h, copy))

    def own_x(self):
        me, own = self.me, self.me.block()
        self.local = pltpu.make_async_copy(self.src, self.whole(own), self.local_sem)
        self.local.start()
        self.xs = [
            (-d, self.mail.post(self.src, self.whole(own), me.at(dx=d))) for d in (2, 1, -1)
        ]

    def own_y(self):
        me, own = self.me, self.me.block()
        self.y0 = [
            self.mail.post(self.src.at[h], self.half(own, h), me.at(dy=1 - 2 * h))
            for h in range(2)
        ]
        self.sib.append(self.mail.post(self.src, self.whole(own), me.at(dc=1)))

    def from_x(self, i):
        dx, copy = self.xs[i]
        copy.wait_recv()
        for h in range(2):
            self.along_y(dx, h)
        self.share(self.me.block(dx=dx))

    def from_y(self):
        for h in range(2):
            self.y0[h].wait_recv()
        self.share(self.me.block(dy=1))

    def from_far(self, first, last):
        for i in range(first, last):
            dx, h, copy = self.far[i]
            copy.wait_recv()
            if h == 1:
                self.share(self.me.block(dx=dx, dy=1))

    def complete(self):
        self.local.wait()
        for copy in self.sib:
            copy.wait_recv()


CHUNKS = ((0, 6), (6, 12), (12, 17))


def prepare(span_ref, inv, w_scr):
    for j in range(32):
        found = jnp.int32(0)
        for s in range(32):
            found = jnp.where(span_ref[s] == j, s, found)
        inv[j] = found
    zero = jnp.zeros((BLK, HD), F32)
    for u in range(2):
        w_scr[u, WIN] = zero


def stack_heads(q_ref, do_ref, qs, ds_rows):
    for u in range(2):
        for h in range(HEADS_DEV):
            qs[u, pl.ds(h * BLK, BLK), :] = q_ref[pl.ds(u * BLK, BLK), pl.ds(h * HD, HD)]
            ds_rows[u, pl.ds(h * BLK, BLK), :] = do_ref[pl.ds(u * BLK, BLK), pl.ds(h * HD, HD)]


def window(ctx, u, span_ref, inv, buf, out):
    p = span_ref[2 * ctx + u]
    for t in range(WIN):
        out[u, pl.ds(t * BLK, BLK), :] = buf[inv[jnp.maximum(p - (WIN - 1) + t, 0)]]


def nt_dot(a, b):
    return lax.dot_general(a, b, (((1,), (1,)), ((), ())), preferred_element_type=F32)


def probs_of(ctx, u, span_ref, seg_ref, qs, ds_rows, qn, dn, kg, s_scr, p_scr):
    p = span_ref[2 * ctx + u]
    seg_all = seg_ref[...]
    counts = [jnp.sum(jnp.where(seg_all == v, 1.0, 0.0)) for v in range(3)]
    cols2 = lax.broadcasted_iota(jnp.int32, (BLK, 2 * BLK), 1) % BLK
    rows2 = lax.broadcasted_iota(jnp.int32, (BLK, 2 * BLK), 0)
    causal = rows2 <= cols2
    rows_f = rows2.astype(F32)
    seg_row = seg_ref[pl.ds(p, 1), :]
    start = jnp.zeros((1, BLK), F32)
    for v in range(3):
        start = start + jnp.where(seg_row > v, counts[v], 0.0)
    first = (p - (WIN - 1)) * BLK
    start = start - first.astype(F32)
    start2 = jnp.concatenate([start, start], axis=1)
    inv_norms = []
    for hp in range(2):
        wide = pl.ds(hp * 256, 256)
        q2 = qs[u, wide, :]
        top = jnp.full((8, 256), NEGATIVE, F32)
        for t0, t1 in CHUNKS:
            sc = nt_dot(kg[u, pl.ds(t0 * BLK, (t1 - t0) * BLK), :], q2)
            for t in range(t0, t1):
                tile = sc[(t - t0) * BLK : (t - t0 + 1) * BLK]
                ok = rows_f >= start2 - float(t * BLK)
                if t == WIN - 1:
                    ok = ok & causal
                tile = jnp.where(ok, tile * (SCALE * LOG2E), NEGATIVE)
                s_scr[u, pl.ds(t * BLK, BLK), wide] = tile
                top = jnp.maximum(top, jnp.max(tile.reshape(16, 8, 256), axis=0))
        top = jnp.max(top, axis=0, keepdims=True)
        norm = jnp.zeros((8, 256), F32)
        for t in range(WIN):
            tile = pl.ds(t * BLK, BLK)
            pt = jnp.exp2(s_scr[u, tile, wide] - top)
            s_scr[u, tile, wide] = pt
            p_scr[u, tile, wide] = pt.astype(BF)
            norm = norm + jnp.sum(pt.reshape(16, 8, 256), axis=0)
        inv_norm = 1.0 / jnp.sum(norm, axis=0, keepdims=True)
        for i in range(2):
            row = inv_norm[:, i * BLK : (i + 1) * BLK]
            by_row = jnp.broadcast_to(row, (BLK, BLK)).T
            part = pl.ds((2 * hp + i) * BLK, BLK)
            qn[u, part, :] = (qs[u, part, :].astype(F32) * by_row).astype(BF)
            dn[u, part, :] = (ds_rows[u, part, :].astype(F32) * by_row).astype(BF)
        inv_norms.append(inv_norm)
    return inv_norms


def dscores_of(u, inv_norms, ds_rows, vg, s_scr, dp_scr, ds_scr):
    for hp in range(2):
        wide = pl.ds(hp * 256, 256)
        do2 = ds_rows[u, wide, :]
        mixed = jnp.zeros((8, 256), F32)
        for t0, t1 in CHUNKS:
            dp = nt_dot(vg[u, pl.ds(t0 * BLK, (t1 - t0) * BLK), :], do2)
            for t in range(t0, t1):
                tile = pl.ds(t * BLK, BLK)
                dpt = dp[(t - t0) * BLK : (t - t0 + 1) * BLK]
                dp_scr[tile, wide] = dpt
                mixed = mixed + jnp.sum(
                    (s_scr[u, tile, wide] * dpt).reshape(16, 8, 256), axis=0
                )
        delta = jnp.sum(mixed, axis=0, keepdims=True) * inv_norms[hp]
        for t in range(WIN):
            tile = pl.ds(t * BLK, BLK)
            ds_scr[u, tile, wide] = (s_scr[u, tile, wide] * (dp_scr[tile, wide] - delta)).astype(BF)


def query_grads(dq_ref, kg, ds_scr, norms):
    for u in range(2):
        for hp in range(2):
            dqt = lax.dot_general(
                kg[u], ds_scr[u, :, pl.ds(hp * 256, 256)],
                (((0,), (0,)), ((), ())), preferred_element_type=F32,
            ) * (norms[u][hp] * SCALE)
            for i in range(2):
                piece = dqt[:, i * BLK : (i + 1) * BLK].T
                dq_ref[pl.ds(u * BLK, BLK), pl.ds((2 * hp + i) * HD, HD)] = piece.astype(BF)


def window_terms(u, source, weights, w_scr):
    for t0, t1 in CHUNKS:
        part = jnp.dot(
            source[u, pl.ds(t0 * BLK, (t1 - t0) * BLK), :], weights[u], preferred_element_type=F32
        )
        w_scr[u, pl.ds(t0, t1 - t0)] = part.reshape(t1 - t0, BLK, HD)


def assemble(ctx, span_ref, kind, core, w_scr, terms, part):
    base = [span_ref[2 * ctx + u] - (WIN - 1) for u in range(2)]
    for i in range(8 * part, 8 * part + 8):
        xx, lo, h = i // 4, (i // 2) % 2, i % 2
        where = span_ref[xx * 8 + lo * 4 + core * 2 + h]
        total = None
        for u in range(2):
            t = where - base[u]
            piece = w_scr[u, jnp.where((t >= 0) & (t < WIN), t, WIN)]
            total = piece if total is None else total + piece
        if kind == 0:
            total = total * SCALE
        terms[xx, lo, h] = total.astype(BF)


class Stream:
    def __init__(self, me, mail, kind, theirs, mine, r0, a1, b1, a2, b2, own, sem, result):
        self.me, self.mail, self.kind = me, mail, kind
        self.theirs, self.mine, self.r0 = theirs, mine, r0
        self.a1, self.b1, self.a2, self.b2 = a1, b1, a2, b2
        self.own, self.sem, self.result = own, sem, result

    def to_sibling(self, part):
        xs = pl.ds(2 * part, 2)
        copy = self.mail.post(self.theirs.at[xs], self.r0.at[xs], self.me.at(dc=1))
        self.halves = [copy] if part == 0 else self.halves + [copy]

    def first_leg(self):
        me, mine = self.me, self.mine
        for xx in range(4):
            if xx % 2 == 0:
                self.halves[xx // 2].wait_recv()
            mine[xx] = (mine[xx].astype(F32) + self.r0[xx].astype(F32)).astype(BF)
        self.leg1 = []
        for i, d in enumerate((2, 1, -1)):
            x = (me.x + d + 4) % 4
            y = (me.y + d + 4) % 4
            self.leg1.append(
                self.mail.post(mine.at[x, :, :, pl.ds(0, 64)], self.a1.at[i], me.at(dx=d))
            )
            self.leg1.append(
                self.mail.post(mine.at[:, y % 2, y // 2, pl.ds(64, 64)], self.b1.at[i], me.at(dy=d))
            )

    def second_leg(self):
        me, mine = self.me, self.mine
        for copy in self.leg1:
            copy.wait_recv()
        own_a = mine.at[me.x, :, :, pl.ds(0, 64)]
        own_b = mine.at[:, me.ylo, me.yhi, pl.ds(64, 64)]
        for own, got in ((own_a, self.a1), (own_b, self.b1)):
            total = own[...].astype(F32)
            for i in range(3):
                total = total + got[i].astype(F32)
            own[...] = total.astype(BF)
        self.leg2 = []
        for i, d in enumerate((2, 1, -1)):
            x = (me.x + d + 4) % 4
            y = (me.y + d + 4) % 4
            self.leg2.append(
                self.mail.post(
                    mine.at[me.x, y % 2, y // 2, pl.ds(0, 64)], self.a2.at[i], me.at(dy=d)
                )
            )
            self.leg2.append(
                self.mail.post(
                    mine.at[x, me.ylo, me.yhi, pl.ds(64, 64)], self.b2.at[i], me.at(dx=d)
                )
            )

    def spot(self, k, dz):
        half = self.me.yhi if k == 0 else 1 - self.me.yhi
        return self.result.at[self.kind, (self.me.z + dz + 8) % 8, half]

    def over(self, dz):
        return self.mail.post(self.spot(0, dz), self.spot(0, dz), self.me.at(dy=2))

    def finish(self):
        me, mine = self.me, self.mine
        for copy in self.leg2:
            copy.wait_recv()
        for rows, got in ((pl.ds(0, 64), self.a2), (pl.ds(64, 64), self.b2)):
            total = mine[me.x, me.ylo, me.yhi, rows].astype(F32)
            for i in range(3):
                total = total + got[i].astype(F32)
            self.own[rows] = total.astype(BF)
        self.kept = pltpu.make_async_copy(self.own, self.spot(0, 0), self.sem)
        self.kept.start()
        self.swaps = [self.mail.post(self.own, self.spot(0, 0), me.at(dy=2))]
        self.direct = [
            (-dz, self.mail.post(self.own, self.spot(0, 0), me.at(dz=dz)))
            for dz in (4, 3, -3, 2, -2, 1, -1)
        ]

    def swapped(self):
        self.swaps[0].wait_recv()
        self.near = [
            self.mail.post(self.spot(1, 0), self.spot(1, 0), self.me.at(dz=dz)) for dz in (1, -1)
        ]

    def spread(self):
        for dz, copy in self.direct:
            copy.wait_recv()
            if abs(dz) != 1:
                self.swaps.append(self.over(dz))

    def last(self):
        self.kept.wait()
        for copy in self.swaps[1:] + self.near:
            copy.wait_recv()


VMEM = pl.BlockSpec(memory_space=pltpu.VMEM)
SMEM = pl.BlockSpec(memory_space=pltpu.SMEM)
ANY = pl.BlockSpec(memory_space=pl.ANY)
LIMIT = 56 * 2**20


def kernel(
    q_ref, k_ref, v_ref, do_ref, span_ref, seg_ref, dq_ref, result,
    send, recv, local_sem, q_rows, do_rows, dq_rows, kbuf, vbuf, inv, qs, ds_rows, qn, dn, kg, vg,
    s_scr, dp_scr, p_scr, ds_scr, w_scr, theirs, mine, r0, a1, b1, a2, b2, own,
):
    me = Place()
    greet(
        [me.at(dx=1), me.at(dx=-1), me.at(dx=2), me.at(dy=1), me.at(dy=-1), me.at(dy=2)]
        + [me.at(dc=1)]
        + [me.at(dz=dz) for dz in (1, -1, 2, -2, 3, -3, 4)]
    )
    mail = Mail(send, recv)
    gk = Gather(me, mail, k_ref.at[me.z], kbuf, local_sem.at[0])
    gv = Gather(me, mail, v_ref.at[me.z], vbuf, local_sem.at[1])
    gk.own_x()
    gk.own_y()
    gv.own_x()
    loads = [
        pltpu.make_async_copy(q_ref, q_rows, local_sem.at[2]),
        pltpu.make_async_copy(do_ref, do_rows, local_sem.at[3]),
    ]
    for load in loads:
        load.start()
    gk.from_x(0)
    gk.from_x(1)
    gv.own_y()
    gk.from_y()
    gk.from_x(2)
    gv.from_x(0)
    gv.from_x(1)
    prepare(span_ref, inv, w_scr)
    gk.from_far(0, 4)
    gv.from_y()
    gv.from_x(2)
    for load in loads:
        load.wait()
    stack_heads(q_rows, do_rows, qs, ds_rows)
    gk.from_far(4, 6)
    gk.complete()
    ctx = me.ctx
    window(ctx, 0, span_ref, inv, kbuf, kg)
    norms = [probs_of(ctx, 0, span_ref, seg_ref, qs, ds_rows, qn, dn, kg, s_scr, p_scr)]
    gv.from_far(0, 6)
    window_terms(0, p_scr, dn, w_scr)
    window(ctx, 1, span_ref, inv, kbuf, kg)
    norms.append(probs_of(ctx, 1, span_ref, seg_ref, qs, ds_rows, qn, dn, kg, s_scr, p_scr))
    window_terms(1, p_scr, dn, w_scr)
    dk, dv = (
        Stream(
            me, mail, kind, theirs.at[kind], mine.at[kind], r0.at[kind], a1.at[kind],
            b1.at[kind], a2.at[kind], b2.at[kind], own.at[kind], local_sem.at[4 + kind], result,
        )
        for kind in range(2)
    )
    for part in range(2):
        assemble(ctx, span_ref, 1, 1 - me.core, w_scr, dv.theirs, part)
        dv.to_sibling(part)
    for part in range(2):
        assemble(ctx, span_ref, 1, me.core, w_scr, dv.mine, part)
    gv.complete()
    window(ctx, 0, span_ref, inv, vbuf, vg)
    dscores_of(0, norms[0], ds_rows, vg, s_scr, dp_scr, ds_scr)
    dv.first_leg()
    window_terms(0, ds_scr, qn, w_scr)
    window(ctx, 1, span_ref, inv, vbuf, vg)
    dscores_of(1, norms[1], ds_rows, vg, s_scr, dp_scr, ds_scr)
    window_terms(1, ds_scr, qn, w_scr)
    for part in range(2):
        assemble(ctx, span_ref, 0, 1 - me.core, w_scr, dk.theirs, part)
        dk.to_sibling(part)
    for part in range(2):
        assemble(ctx, span_ref, 0, me.core, w_scr, dk.mine, part)
    dv.second_leg()
    dk.first_leg()
    query_grads(dq_rows, kg, ds_scr, norms)
    leave = pltpu.make_async_copy(dq_rows, dq_ref, local_sem.at[6])
    leave.start()
    dv.finish()
    dk.second_leg()
    dv.swapped()
    dk.finish()
    dv.spread()
    dk.swapped()
    dk.spread()
    dv.last()
    dk.last()
    leave.wait()
    mail.drain()


def cast_kernel(result, dq_in, dk, dv, dq_out, narrow, wide, passing, sem_in, sem_out):
    outs = (dk, dv)
    loads, stores = [], []
    for i in range(8):
        part = pl.ds(2 * (i % 4), 2)
        copy = pltpu.make_async_copy(
            result.at[i // 4, part], narrow.at[i // 4, part], sem_in.at[i]
        )
        copy.start()
        loads.append(copy)
    inward = pltpu.make_async_copy(dq_in, passing, sem_in.at[8])
    inward.start()
    for i in range(8):
        part = pl.ds(2 * (i % 4), 2)
        loads[i].wait()
        wide[i // 4, part] = narrow[i // 4, part].astype(F32)
        copy = pltpu.make_async_copy(wide.at[i // 4, part], outs[i // 4].at[part], sem_out.at[i])
        copy.start()
        stores.append(copy)
    inward.wait()
    outward = pltpu.make_async_copy(passing, dq_out, sem_out.at[8])
    outward.start()
    for copy in stores:
        copy.wait()
    outward.wait()


def per_device(queries, keys, values, d_out, span_order, segments):
    keys = keys.reshape(8, 2, BLK, HD)
    values = values.reshape(8, 2, BLK, HD)
    dq, result = pl.pallas_call(
        kernel,
        out_shape=[
            jax.ShapeDtypeStruct((256, 512), BF),
            jax.ShapeDtypeStruct((2, 8, 2, BLK, HD), BF),
        ],
        in_specs=[ANY, ANY, ANY, ANY, SMEM, VMEM],
        out_specs=[ANY, ANY],
        scratch_shapes=[
            pltpu.SemaphoreType.DMA((112,)),
            pltpu.SemaphoreType.DMA((112,)),
            pltpu.SemaphoreType.DMA((7,)),
            pltpu.VMEM((256, 512), BF),
            pltpu.VMEM((256, 512), BF),
            pltpu.VMEM((256, 512), BF),
            pltpu.VMEM((32, BLK, HD), BF),
            pltpu.VMEM((32, BLK, HD), BF),
            pltpu.SMEM((32,), jnp.int32),
            pltpu.VMEM((2, COLS, HD), BF),
            pltpu.VMEM((2, COLS, HD), BF),
            pltpu.VMEM((2, COLS, HD), BF),
            pltpu.VMEM((2, COLS, HD), BF),
            pltpu.VMEM((2, WIN * BLK, HD), BF),
            pltpu.VMEM((2, WIN * BLK, HD), BF),
            pltpu.VMEM((2, WIN * BLK, COLS), F32),
            pltpu.VMEM((WIN * BLK, COLS), F32),
            pltpu.VMEM((2, WIN * BLK, COLS), BF),
            pltpu.VMEM((2, WIN * BLK, COLS), BF),
            pltpu.VMEM((2, WIN + 1, BLK, HD), F32),
            pltpu.VMEM((2, 4, 2, 2, BLK, HD), BF),
            pltpu.VMEM((2, 4, 2, 2, BLK, HD), BF),
            pltpu.VMEM((2, 4, 2, 2, BLK, HD), BF),
            pltpu.VMEM((2, 3, 2, 2, 64, HD), BF),
            pltpu.VMEM((2, 3, 4, 64, HD), BF),
            pltpu.VMEM((2, 3, 64, HD), BF),
            pltpu.VMEM((2, 3, 64, HD), BF),
            pltpu.VMEM((2, BLK, HD), BF),
        ],
        compiler_params=pltpu.CompilerParams(
            collective_id=0, has_side_effects=True, vmem_limit_bytes=LIMIT
        ),
        name="backward",
    )(queries, keys, values, d_out, span_order, segments.reshape(32, BLK))
    dk, dv, dq = pl.pallas_call(
        cast_kernel,
        out_shape=[
            jax.ShapeDtypeStruct((8, 2, BLK, HD), F32),
            jax.ShapeDtypeStruct((8, 2, BLK, HD), F32),
            jax.ShapeDtypeStruct((256, 512), BF),
        ],
        in_specs=[ANY, ANY],
        out_specs=[ANY, ANY, ANY],
        scratch_shapes=[
            pltpu.VMEM((2, 8, 2, BLK, HD), BF),
            pltpu.VMEM((2, 8, 2, BLK, HD), F32),
            pltpu.VMEM((256, 512), BF),
            pltpu.SemaphoreType.DMA((9,)),
            pltpu.SemaphoreType.DMA((9,)),
        ],
        compiler_params=pltpu.CompilerParams(vmem_limit_bytes=LIMIT),
        name="widen",
    )(result, dq)
    return (dq, dk.reshape(8, 256, HD), dv.reshape(8, 256, HD))


def solution(mesh):
    return jax.shard_map(
        per_device,
        mesh=mesh,
        in_specs=(
            P("ctx", "tp"),
            P(None, "ctx", None),
            P(None, "ctx", None),
            P("ctx", "tp"),
            P(),
            P(),
        ),
        out_specs=(P("ctx", "tp"), P(None, "ctx", None), P(None, "ctx", None)),
        check_vma=False,
    )
```

```python
import functools

import jax
import jax.numpy as jnp
from jax import lax
from jax.experimental import pallas as pl
from jax.experimental.pallas import tpu as pltpu
from jax.sharding import PartitionSpec as P

HD = 128
BLK = 128
HEADS_DEV = 4
COLS = HEADS_DEV * BLK
WIN = 17
NEGATIVE = -1e30
SCALE = HD**-0.5
LOG2E = 1.4426950408889634
BF = jnp.bfloat16
F32 = jnp.float32


class Place:
    def __init__(self):
        self.ctx = lax.axis_index("ctx")
        self.tp = lax.axis_index("tp")
        self.x = self.ctx // 4
        self.ylo = (self.ctx // 2) % 2
        self.core = self.ctx % 2
        self.z = self.tp // 2
        self.yhi = self.tp % 2
        self.y = self.yhi * 2 + self.ylo

    def at(self, dx=0, dy=0, dc=0, dz=0):
        x = (self.x + dx + 4) % 4
        y = (self.y + dy + 4) % 4
        c = (self.core + dc) % 2
        z = (self.z + dz + 8) % 8
        return (x * 4 + (y % 2) * 2 + c, z * 2 + y // 2)

    def block(self, dx=0, dy=0, dc=0):
        return ((self.x + dx + 4) % 4) * 4 + ((self.ylo + dy) % 2) * 2 + (self.core + dc) % 2


class Mail:
    def __init__(self, send, recv):
        self.send, self.recv, self.used, self.out = send, recv, 0, []

    def post(self, src, dst, device):
        copy = pltpu.make_async_remote_copy(
            src_ref=src,
            dst_ref=dst,
            send_sem=self.send.at[self.used],
            recv_sem=self.recv.at[self.used],
            device_id=device,
            device_id_type=pl.DeviceIdType.MESH,
        )
        self.used += 1
        copy.start()
        self.out.append(copy)
        return copy

    def drain(self):
        for copy in self.out:
            copy.wait_send()
        self.out = []


def greet(devices):
    barrier = pltpu.get_barrier_semaphore()
    for device in devices:
        pl.semaphore_signal(
            barrier, inc=1, device_id=device, device_id_type=pl.DeviceIdType.MESH
        )
    pl.semaphore_wait(barrier, len(devices))


class Gather:
    def __init__(self, me, mail, src, buf, local_sem):
        self.me, self.mail, self.src, self.buf, self.local_sem = me, mail, src, buf, local_sem
        self.sib, self.far = [], []

    def whole(self, block):
        return self.buf.at[pl.ds(2 * block, 2)]

    def half(self, block, h):
        return self.buf.at[2 * block + h]

    def share(self, block, h=None):
        ref = self.whole(block) if h is None else self.half(block, h)
        self.sib.append(self.mail.post(ref, ref, self.me.at(dc=1)))

    def along_y(self, dx, h):
        ref = self.half(self.me.block(dx=dx), h)
        copy = self.mail.post(ref, ref, self.me.at(dy=1 - 2 * h))
        self.far.append((dx, h, copy))

    def own_x(self):
        me, own = self.me, self.me.block()
        self.local = pltpu.make_async_copy(self.src, self.whole(own), self.local_sem)
        self.local.start()
        self.xs = [
            (-d, self.mail.post(self.src, self.whole(own), me.at(dx=d))) for d in (1, -1, 2)
        ]

    def own_y(self):
        me, own = self.me, self.me.block()
        self.y0 = [
            self.mail.post(self.src.at[h], self.half(own, h), me.at(dy=1 - 2 * h))
            for h in range(2)
        ]
        self.sib.append(self.mail.post(self.src, self.whole(own), me.at(dc=1)))

    def from_x(self, i):
        dx, copy = self.xs[i]
        copy.wait_recv()
        for h in range(2):
            self.along_y(dx, h)
        self.share(self.me.block(dx=dx))

    def from_y(self):
        for h in range(2):
            self.y0[h].wait_recv()
        self.share(self.me.block(dy=1))

    def from_far(self, first, last):
        for i in range(first, last):
            dx, h, copy = self.far[i]
            copy.wait_recv()
            if h == 1:
                self.share(self.me.block(dx=dx, dy=1))

    def complete(self):
        self.local.wait()
        for copy in self.sib:
            copy.wait_recv()


CHUNKS = ((0, 6), (6, 12), (12, 17))


def prepare(span_ref, inv, w_scr):
    for j in range(32):
        found = jnp.int32(0)
        for s in range(32):
            found = jnp.where(span_ref[s] == j, s, found)
        inv[j] = found
    zero = jnp.zeros((BLK, HD), F32)
    for u in range(2):
        w_scr[u, WIN] = zero


def stack_heads(q_ref, do_ref, qs, ds_rows):
    for u in range(2):
        for h in range(HEADS_DEV):
            qs[u, pl.ds(h * BLK, BLK), :] = q_ref[pl.ds(u * BLK, BLK), pl.ds(h * HD, HD)]
            ds_rows[u, pl.ds(h * BLK, BLK), :] = do_ref[pl.ds(u * BLK, BLK), pl.ds(h * HD, HD)]


def window(ctx, u, span_ref, inv, buf, out):
    p = span_ref[2 * ctx + u]
    for t in range(WIN):
        out[u, pl.ds(t * BLK, BLK), :] = buf[inv[jnp.maximum(p - (WIN - 1) + t, 0)]]


def nt_dot(a, b):
    return lax.dot_general(a, b, (((1,), (1,)), ((), ())), preferred_element_type=F32)


def probs_of(ctx, u, span_ref, seg_ref, qs, ds_rows, qn, dn, kg, s_scr, p_scr):
    p = span_ref[2 * ctx + u]
    seg_all = seg_ref[...]
    counts = [jnp.sum(jnp.where(seg_all == v, 1.0, 0.0)) for v in range(3)]
    cols2 = lax.broadcasted_iota(jnp.int32, (BLK, 2 * BLK), 1) % BLK
    rows2 = lax.broadcasted_iota(jnp.int32, (BLK, 2 * BLK), 0)
    causal = rows2 <= cols2
    rows_f = rows2.astype(F32)
    seg_row = seg_ref[pl.ds(p, 1), :]
    start = jnp.zeros((1, BLK), F32)
    for v in range(3):
        start = start + jnp.where(seg_row > v, counts[v], 0.0)
    first = (p - (WIN - 1)) * BLK
    start = start - first.astype(F32)
    start2 = jnp.concatenate([start, start], axis=1)
    inv_norms = []
    for hp in range(2):
        wide = pl.ds(hp * 256, 256)
        q2 = qs[u, wide, :]
        top = jnp.full((8, 256), NEGATIVE, F32)
        for t0, t1 in CHUNKS:
            sc = nt_dot(kg[u, pl.ds(t0 * BLK, (t1 - t0) * BLK), :], q2)
            for t in range(t0, t1):
                tile = sc[(t - t0) * BLK : (t - t0 + 1) * BLK]
                ok = rows_f >= start2 - float(t * BLK)
                if t == WIN - 1:
                    ok = ok & causal
                tile = jnp.where(ok, tile * (SCALE * LOG2E), NEGATIVE)
                s_scr[u, pl.ds(t * BLK, BLK), wide] = tile
                top = jnp.maximum(top, jnp.max(tile.reshape(16, 8, 256), axis=0))
        top = jnp.max(top, axis=0, keepdims=True)
        norm = jnp.zeros((8, 256), F32)
        for t in range(WIN):
            tile = pl.ds(t * BLK, BLK)
            pt = jnp.exp2(s_scr[u, tile, wide] - top)
            p_scr[u, tile, wide] = pt.astype(BF)
            norm = norm + jnp.sum(pt.reshape(16, 8, 256), axis=0)
        inv_norm = 1.0 / jnp.sum(norm, axis=0, keepdims=True)
        for i in range(2):
            row = inv_norm[:, i * BLK : (i + 1) * BLK]
            by_row = jnp.broadcast_to(row, (BLK, BLK)).T
            part = pl.ds((2 * hp + i) * BLK, BLK)
            qn[u, part, :] = (qs[u, part, :].astype(F32) * by_row).astype(BF)
            dn[u, part, :] = (ds_rows[u, part, :].astype(F32) * by_row).astype(BF)
        inv_norms.append(inv_norm)
    return inv_norms


def dscores_of(u, inv_norms, ds_rows, vg, p_scr, dp_scr, ds_scr):
    for hp in range(2):
        wide = pl.ds(hp * 256, 256)
        do2 = ds_rows[u, wide, :]
        mixed = jnp.zeros((8, 256), F32)
        for t0, t1 in CHUNKS:
            dp = nt_dot(vg[u, pl.ds(t0 * BLK, (t1 - t0) * BLK), :], do2)
            for t in range(t0, t1):
                tile = pl.ds(t * BLK, BLK)
                dpt = dp[(t - t0) * BLK : (t - t0 + 1) * BLK]
                dp_scr[tile, wide] = dpt
                mixed = mixed + jnp.sum(
                    (p_scr[u, tile, wide].astype(F32) * dpt).reshape(16, 8, 256), axis=0
                )
        delta = jnp.sum(mixed, axis=0, keepdims=True) * inv_norms[hp]
        for t in range(WIN):
            tile = pl.ds(t * BLK, BLK)
            prob = p_scr[u, tile, wide].astype(F32)
            ds_scr[u, tile, wide] = (prob * (dp_scr[tile, wide] - delta)).astype(BF)


def query_grads(dq_ref, kg, ds_scr, norms):
    for u in range(2):
        for hp in range(2):
            dqt = lax.dot_general(
                kg[u], ds_scr[u, :, pl.ds(hp * 256, 256)],
                (((0,), (0,)), ((), ())), preferred_element_type=F32,
            ) * (norms[u][hp] * SCALE)
            for i in range(2):
                piece = dqt[:, i * BLK : (i + 1) * BLK].T
                dq_ref[pl.ds(u * BLK, BLK), pl.ds((2 * hp + i) * HD, HD)] = piece.astype(BF)


def window_terms(u, source, weights, w_scr):
    for t0, t1 in CHUNKS:
        part = jnp.dot(
            source[u, pl.ds(t0 * BLK, (t1 - t0) * BLK), :], weights[u], preferred_element_type=F32
        )
        w_scr[u, pl.ds(t0, t1 - t0)] = part.reshape(t1 - t0, BLK, HD)


def assemble(ctx, span_ref, kind, core, w_scr, terms, part):
    base = [span_ref[2 * ctx + u] - (WIN - 1) for u in range(2)]
    for i in range(8 * part, 8 * part + 8):
        xx, lo, h = i // 4, (i // 2) % 2, i % 2
        where = span_ref[xx * 8 + lo * 4 + core * 2 + h]
        total = None
        for u in range(2):
            t = where - base[u]
            piece = w_scr[u, jnp.where((t >= 0) & (t < WIN), t, WIN)]
            total = piece if total is None else total + piece
        if kind == 0:
            total = total * SCALE
        terms[xx, lo, h] = total.astype(BF)


class Stream:
    def __init__(self, me, mail, kind, theirs, mine, r0, a1, b1, a2, b2, own, sem, result):
        self.me, self.mail, self.kind = me, mail, kind
        self.theirs, self.mine, self.r0 = theirs, mine, r0
        self.a1, self.b1, self.a2, self.b2 = a1, b1, a2, b2
        self.own, self.sem, self.result = own, sem, result

    def to_sibling(self, part):
        xs = pl.ds(2 * part, 2)
        copy = self.mail.post(self.theirs.at[xs], self.r0.at[xs], self.me.at(dc=1))
        self.halves = [copy] if part == 0 else self.halves + [copy]

    def first_leg(self):
        me, mine = self.me, self.mine
        for xx in range(4):
            if xx % 2 == 0:
                self.halves[xx // 2].wait_recv()
            mine[xx] = (mine[xx].astype(F32) + self.r0[xx].astype(F32)).astype(BF)
        self.leg1 = []
        for i, d in enumerate((1, -1, 2)):
            x = (me.x + d + 4) % 4
            y = (me.y + d + 4) % 4
            self.leg1.append(
                self.mail.post(mine.at[x, :, :, pl.ds(0, 64)], self.a1.at[i], me.at(dx=d))
            )
            self.leg1.append(
                self.mail.post(mine.at[:, y % 2, y // 2, pl.ds(64, 64)], self.b1.at[i], me.at(dy=d))
            )

    def second_leg(self):
        me, mine = self.me, self.mine
        for copy in self.leg1:
            copy.wait_recv()
        own_a = mine.at[me.x, :, :, pl.ds(0, 64)]
        own_b = mine.at[:, me.ylo, me.yhi, pl.ds(64, 64)]
        for own, got in ((own_a, self.a1), (own_b, self.b1)):
            total = own[...].astype(F32)
            for i in range(3):
                total = total + got[i].astype(F32)
            own[...] = total.astype(BF)
        self.leg2 = []
        for i, d in enumerate((1, -1, 2)):
            x = (me.x + d + 4) % 4
            y = (me.y + d + 4) % 4
            self.leg2.append(
                self.mail.post(
                    mine.at[me.x, y % 2, y // 2, pl.ds(0, 64)], self.a2.at[i], me.at(dy=d)
                )
            )
            self.leg2.append(
                self.mail.post(
                    mine.at[x, me.ylo, me.yhi, pl.ds(64, 64)], self.b2.at[i], me.at(dx=d)
                )
            )

    def spot(self, k, dz):
        half = self.me.yhi if k == 0 else 1 - self.me.yhi
        return self.result.at[self.kind, (self.me.z + dz + 8) % 8, half]

    def over(self, dz):
        return self.mail.post(self.spot(0, dz), self.spot(0, dz), self.me.at(dy=2))

    def finish(self):
        me, mine = self.me, self.mine
        for copy in self.leg2:
            copy.wait_recv()
        for rows, got in ((pl.ds(0, 64), self.a2), (pl.ds(64, 64), self.b2)):
            total = mine[me.x, me.ylo, me.yhi, rows].astype(F32)
            for i in range(3):
                total = total + got[i].astype(F32)
            self.own[rows] = total.astype(BF)
        self.kept = pltpu.make_async_copy(self.own, self.spot(0, 0), self.sem)
        self.kept.start()
        self.swaps = [self.mail.post(self.own, self.spot(0, 0), me.at(dy=2))]
        self.direct = [
            (-dz, self.mail.post(self.own, self.spot(0, 0), me.at(dz=dz)))
            for dz in (4, 3, -3, 2, -2, 1, -1)
        ]

    def swapped(self):
        self.swaps[0].wait_recv()
        self.near = [
            self.mail.post(self.spot(1, 0), self.spot(1, 0), self.me.at(dz=dz)) for dz in (1, -1)
        ]

    def spread(self):
        for dz, copy in self.direct:
            copy.wait_recv()
            if abs(dz) != 1:
                self.swaps.append(self.over(dz))

    def last(self):
        self.kept.wait()
        for copy in self.swaps[1:] + self.near:
            copy.wait_recv()


VMEM = pl.BlockSpec(memory_space=pltpu.VMEM)
SMEM = pl.BlockSpec(memory_space=pltpu.SMEM)
ANY = pl.BlockSpec(memory_space=pl.ANY)
LIMIT = 56 * 2**20


def kernel(
    q_ref, k_ref, v_ref, do_ref, span_ref, seg_ref, dq_ref, result,
    send, recv, local_sem, q_rows, do_rows, dq_rows, kbuf, vbuf, inv, qs, ds_rows, qn, dn, kg, vg,
    s_scr, dp_scr, p_scr, ds_scr, w_scr, theirs, mine, r0, a1, b1, a2, b2, own,
):
    me = Place()
    greet(
        [me.at(dx=1), me.at(dx=-1), me.at(dx=2), me.at(dy=1), me.at(dy=-1), me.at(dy=2)]
        + [me.at(dc=1)]
        + [me.at(dz=dz) for dz in (1, -1, 2, -2, 3, -3, 4)]
    )
    mail = Mail(send, recv)
    gk = Gather(me, mail, k_ref.at[me.z], kbuf, local_sem.at[0])
    gv = Gather(me, mail, v_ref.at[me.z], vbuf, local_sem.at[1])
    gk.own_x()
    gk.own_y()
    gv.own_x()
    loads = [
        pltpu.make_async_copy(q_ref, q_rows, local_sem.at[2]),
        pltpu.make_async_copy(do_ref, do_rows, local_sem.at[3]),
    ]
    for load in loads:
        load.start()
    gk.from_x(0)
    gk.from_x(1)
    gv.own_y()
    gk.from_y()
    gk.from_x(2)
    gv.from_x(0)
    gv.from_x(1)
    prepare(span_ref, inv, w_scr)
    gk.from_far(0, 4)
    gv.from_y()
    gv.from_x(2)
    for load in loads:
        load.wait()
    stack_heads(q_rows, do_rows, qs, ds_rows)
    gk.from_far(4, 6)
    gk.complete()
    ctx = me.ctx
    window(ctx, 0, span_ref, inv, kbuf, kg)
    norms = [probs_of(ctx, 0, span_ref, seg_ref, qs, ds_rows, qn, dn, kg, s_scr, p_scr)]
    gv.from_far(0, 6)
    window_terms(0, p_scr, dn, w_scr)
    window(ctx, 1, span_ref, inv, kbuf, kg)
    norms.append(probs_of(ctx, 1, span_ref, seg_ref, qs, ds_rows, qn, dn, kg, s_scr, p_scr))
    window_terms(1, p_scr, dn, w_scr)
    dk, dv = (
        Stream(
            me, mail, kind, theirs.at[kind], mine.at[kind], r0.at[kind], a1.at[kind],
            b1.at[kind], a2.at[kind], b2.at[kind], own.at[kind], local_sem.at[4 + kind], result,
        )
        for kind in range(2)
    )
    for part in range(2):
        assemble(ctx, span_ref, 1, 1 - me.core, w_scr, dv.theirs, part)
        dv.to_sibling(part)
    for part in range(2):
        assemble(ctx, span_ref, 1, me.core, w_scr, dv.mine, part)
    gv.complete()
    window(ctx, 0, span_ref, inv, vbuf, vg)
    dscores_of(0, norms[0], ds_rows, vg, p_scr, dp_scr, ds_scr)
    dv.first_leg()
    window_terms(0, ds_scr, qn, w_scr)
    window(ctx, 1, span_ref, inv, vbuf, vg)
    dscores_of(1, norms[1], ds_rows, vg, p_scr, dp_scr, ds_scr)
    window_terms(1, ds_scr, qn, w_scr)
    for part in range(2):
        assemble(ctx, span_ref, 0, 1 - me.core, w_scr, dk.theirs, part)
        dk.to_sibling(part)
    for part in range(2):
        assemble(ctx, span_ref, 0, me.core, w_scr, dk.mine, part)
    dv.second_leg()
    dk.first_leg()
    query_grads(dq_rows, kg, ds_scr, norms)
    leave = pltpu.make_async_copy(dq_rows, dq_ref, local_sem.at[6])
    leave.start()
    dv.finish()
    dk.second_leg()
    dv.swapped()
    dk.finish()
    dv.spread()
    dk.swapped()
    dk.spread()
    dv.last()
    dk.last()
    leave.wait()
    mail.drain()


def cast_kernel(result, dq_in, dk, dv, dq_out, narrow, wide, passing, sem_in, sem_out):
    outs = (dk, dv)
    loads, stores = [], []
    for i in range(8):
        part = pl.ds(2 * (i % 4), 2)
        copy = pltpu.make_async_copy(
            result.at[i // 4, part], narrow.at[i // 4, part], sem_in.at[i]
        )
        copy.start()
        loads.append(copy)
    inward = pltpu.make_async_copy(dq_in, passing, sem_in.at[8])
    inward.start()
    for i in range(8):
        part = pl.ds(2 * (i % 4), 2)
        loads[i].wait()
        wide[i // 4, part] = narrow[i // 4, part].astype(F32)
        copy = pltpu.make_async_copy(wide.at[i // 4, part], outs[i // 4].at[part], sem_out.at[i])
        copy.start()
        stores.append(copy)
    inward.wait()
    outward = pltpu.make_async_copy(passing, dq_out, sem_out.at[8])
    outward.start()
    for copy in stores:
        copy.wait()
    outward.wait()


def per_device(queries, keys, values, d_out, span_order, segments):
    keys = keys.reshape(8, 2, BLK, HD)
    values = values.reshape(8, 2, BLK, HD)
    dq, result = pl.pallas_call(
        kernel,
        out_shape=[
            jax.ShapeDtypeStruct((256, 512), BF),
            jax.ShapeDtypeStruct((2, 8, 2, BLK, HD), BF),
        ],
        in_specs=[ANY, ANY, ANY, ANY, SMEM, VMEM],
        out_specs=[ANY, ANY],
        scratch_shapes=[
            pltpu.SemaphoreType.DMA((112,)),
            pltpu.SemaphoreType.DMA((112,)),
            pltpu.SemaphoreType.DMA((7,)),
            pltpu.VMEM((256, 512), BF),
            pltpu.VMEM((256, 512), BF),
            pltpu.VMEM((256, 512), BF),
            pltpu.VMEM((32, BLK, HD), BF),
            pltpu.VMEM((32, BLK, HD), BF),
            pltpu.SMEM((32,), jnp.int32),
            pltpu.VMEM((2, COLS, HD), BF),
            pltpu.VMEM((2, COLS, HD), BF),
            pltpu.VMEM((2, COLS, HD), BF),
            pltpu.VMEM((2, COLS, HD), BF),
            pltpu.VMEM((2, WIN * BLK, HD), BF),
            pltpu.VMEM((2, WIN * BLK, HD), BF),
            pltpu.VMEM((2, WIN * BLK, COLS), F32),
            pltpu.VMEM((WIN * BLK, COLS), F32),
            pltpu.VMEM((2, WIN * BLK, COLS), BF),
            pltpu.VMEM((2, WIN * BLK, COLS), BF),
            pltpu.VMEM((2, WIN + 1, BLK, HD), F32),
            pltpu.VMEM((2, 4, 2, 2, BLK, HD), BF),
            pltpu.VMEM((2, 4, 2, 2, BLK, HD), BF),
            pltpu.VMEM((2, 4, 2, 2, BLK, HD), BF),
            pltpu.VMEM((2, 3, 2, 2, 64, HD), BF),
            pltpu.VMEM((2, 3, 4, 64, HD), BF),
            pltpu.VMEM((2, 3, 64, HD), BF),
            pltpu.VMEM((2, 3, 64, HD), BF),
            pltpu.VMEM((2, BLK, HD), BF),
        ],
        compiler_params=pltpu.CompilerParams(
            collective_id=0, has_side_effects=True, vmem_limit_bytes=LIMIT
        ),
        name="backward",
    )(queries, keys, values, d_out, span_order, segments.reshape(32, BLK))
    dk, dv, dq = pl.pallas_call(
        cast_kernel,
        out_shape=[
            jax.ShapeDtypeStruct((8, 2, BLK, HD), F32),
            jax.ShapeDtypeStruct((8, 2, BLK, HD), F32),
            jax.ShapeDtypeStruct((256, 512), BF),
        ],
        in_specs=[ANY, ANY],
        out_specs=[ANY, ANY, ANY],
        scratch_shapes=[
            pltpu.VMEM((2, 8, 2, BLK, HD), BF),
            pltpu.VMEM((2, 8, 2, BLK, HD), F32),
            pltpu.VMEM((256, 512), BF),
            pltpu.SemaphoreType.DMA((9,)),
            pltpu.SemaphoreType.DMA((9,)),
        ],
        compiler_params=pltpu.CompilerParams(vmem_limit_bytes=LIMIT),
        name="widen",
    )(result, dq)
    return (dq, dk.reshape(8, 256, HD), dv.reshape(8, 256, HD))


def solution(mesh):
    return jax.shard_map(
        per_device,
        mesh=mesh,
        in_specs=(
            P("ctx", "tp"),
            P(None, "ctx", None),
            P(None, "ctx", None),
            P("ctx", "tp"),
            P(),
            P(),
        ),
        out_specs=(P("ctx", "tp"), P(None, "ctx", None), P(None, "ctx", None)),
        check_vma=False,
    )
```

```python
import functools

import jax
import jax.numpy as jnp
from jax import lax
from jax.experimental import pallas as pl
from jax.experimental.pallas import tpu as pltpu
from jax.sharding import PartitionSpec as P

HD = 128
BLK = 128
HEADS_DEV = 4
COLS = HEADS_DEV * BLK
WIN = 17
NEGATIVE = -1e30
SCALE = HD**-0.5
LOG2E = 1.4426950408889634
BF = jnp.bfloat16
F32 = jnp.float32


class Place:
    def __init__(self):
        self.ctx = lax.axis_index("ctx")
        self.tp = lax.axis_index("tp")
        self.x = self.ctx // 4
        self.ylo = (self.ctx // 2) % 2
        self.core = self.ctx % 2
        self.z = self.tp // 2
        self.yhi = self.tp % 2
        self.y = self.yhi * 2 + self.ylo

    def at(self, dx=0, dy=0, dc=0, dz=0):
        x = (self.x + dx + 4) % 4
        y = (self.y + dy + 4) % 4
        c = (self.core + dc) % 2
        z = (self.z + dz + 8) % 8
        return (x * 4 + (y % 2) * 2 + c, z * 2 + y // 2)

    def block(self, dx=0, dy=0, dc=0):
        return ((self.x + dx + 4) % 4) * 4 + ((self.ylo + dy) % 2) * 2 + (self.core + dc) % 2


class Mail:
    def __init__(self, send, recv):
        self.send, self.recv, self.used, self.out = send, recv, 0, []

    def post(self, src, dst, device):
        copy = pltpu.make_async_remote_copy(
            src_ref=src,
            dst_ref=dst,
            send_sem=self.send.at[self.used],
            recv_sem=self.recv.at[self.used],
            device_id=device,
            device_id_type=pl.DeviceIdType.MESH,
        )
        self.used += 1
        copy.start()
        self.out.append(copy)
        return copy

    def drain(self):
        for copy in self.out:
            copy.wait_send()
        self.out = []


def greet(devices):
    barrier = pltpu.get_barrier_semaphore()
    for device in devices:
        pl.semaphore_signal(
            barrier, inc=1, device_id=device, device_id_type=pl.DeviceIdType.MESH
        )
    pl.semaphore_wait(barrier, len(devices))


class Gather:
    def __init__(self, me, mail, src, buf, local_sem):
        self.me, self.mail, self.src, self.buf, self.local_sem = me, mail, src, buf, local_sem
        self.sib, self.far = [], []

    def whole(self, block):
        return self.buf.at[pl.ds(2 * block, 2)]

    def half(self, block, h):
        return self.buf.at[2 * block + h]

    def share(self, block, h=None):
        ref = self.whole(block) if h is None else self.half(block, h)
        self.sib.append(self.mail.post(ref, ref, self.me.at(dc=1)))

    def along_y(self, dx, h):
        ref = self.half(self.me.block(dx=dx), h)
        copy = self.mail.post(ref, ref, self.me.at(dy=1 - 2 * h))
        self.far.append((dx, h, copy))

    def own_x(self):
        me, own = self.me, self.me.block()
        self.local = pltpu.make_async_copy(self.src, self.whole(own), self.local_sem)
        self.local.start()
        self.xs = [
            (-d, self.mail.post(self.src, self.whole(own), me.at(dx=d))) for d in (1, -1, 2)
        ]

    def own_y(self):
        me, own = self.me, self.me.block()
        self.y0 = [
            self.mail.post(self.src.at[h], self.half(own, h), me.at(dy=1 - 2 * h))
            for h in range(2)
        ]
        self.sib.append(self.mail.post(self.src, self.whole(own), me.at(dc=1)))

    def from_x(self, i):
        dx, copy = self.xs[i]
        copy.wait_recv()
        for h in range(2):
            self.along_y(dx, h)
        self.share(self.me.block(dx=dx))

    def from_y(self):
        for h in range(2):
            self.y0[h].wait_recv()
        self.share(self.me.block(dy=1))

    def from_far(self, first, last):
        for i in range(first, last):
            dx, h, copy = self.far[i]
            copy.wait_recv()
            if h == 1:
                self.share(self.me.block(dx=dx, dy=1))

    def complete(self):
        self.local.wait()
        for copy in self.sib:
            copy.wait_recv()


CHUNKS = ((0, 6), (6, 12), (12, 17))


def prepare(span_ref, inv, w_scr):
    for j in range(32):
        found = jnp.int32(0)
        for s in range(32):
            found = jnp.where(span_ref[s] == j, s, found)
        inv[j] = found
    zero = jnp.zeros((BLK, HD), F32)
    for u in range(2):
        w_scr[u, WIN] = zero


def stack_heads(q_ref, do_ref, qs, ds_rows):
    for u in range(2):
        for h in range(HEADS_DEV):
            qs[u, pl.ds(h * BLK, BLK), :] = q_ref[pl.ds(u * BLK, BLK), pl.ds(h * HD, HD)]
            ds_rows[u, pl.ds(h * BLK, BLK), :] = do_ref[pl.ds(u * BLK, BLK), pl.ds(h * HD, HD)]


def window(ctx, u, span_ref, inv, buf, out):
    p = span_ref[2 * ctx + u]
    for t in range(WIN):
        out[u, pl.ds(t * BLK, BLK), :] = buf[inv[jnp.maximum(p - (WIN - 1) + t, 0)]]


def nt_dot(a, b):
    return lax.dot_general(a, b, (((1,), (1,)), ((), ())), preferred_element_type=F32)


def probs_of(ctx, u, span_ref, seg_ref, qs, ds_rows, qn, dn, kg, s_scr, p_scr):
    p = span_ref[2 * ctx + u]
    seg_all = seg_ref[...]
    counts = [jnp.sum(jnp.where(seg_all == v, 1.0, 0.0)) for v in range(3)]
    cols2 = lax.broadcasted_iota(jnp.int32, (BLK, 2 * BLK), 1) % BLK
    rows2 = lax.broadcasted_iota(jnp.int32, (BLK, 2 * BLK), 0)
    causal = rows2 <= cols2
    rows_f = rows2.astype(F32)
    seg_row = seg_ref[pl.ds(p, 1), :]
    start = jnp.zeros((1, BLK), F32)
    for v in range(3):
        start = start + jnp.where(seg_row > v, counts[v], 0.0)
    first = (p - (WIN - 1)) * BLK
    start = start - first.astype(F32)
    start2 = jnp.concatenate([start, start], axis=1)
    inv_norms = []
    for hp in range(2):
        wide = pl.ds(hp * 256, 256)
        q2 = qs[u, wide, :]
        top = jnp.full((8, 256), NEGATIVE, F32)
        for t0, t1 in CHUNKS:
            sc = nt_dot(kg[u, pl.ds(t0 * BLK, (t1 - t0) * BLK), :], q2)
            for t in range(t0, t1):
                tile = sc[(t - t0) * BLK : (t - t0 + 1) * BLK]
                ok = rows_f >= start2 - float(t * BLK)
                if t == WIN - 1:
                    ok = ok & causal
                tile = jnp.where(ok, tile * (SCALE * LOG2E), NEGATIVE)
                s_scr[u, pl.ds(t * BLK, BLK), wide] = tile
                top = jnp.maximum(top, jnp.max(tile.reshape(16, 8, 256), axis=0))
        top = jnp.max(top, axis=0, keepdims=True)
        norm = jnp.zeros((8, 256), F32)
        for t in range(WIN):
            tile = pl.ds(t * BLK, BLK)
            pt = jnp.exp2(s_scr[u, tile, wide] - top)
            s_scr[u, tile, wide] = pt
            p_scr[u, tile, wide] = pt.astype(BF)
            norm = norm + jnp.sum(pt.reshape(16, 8, 256), axis=0)
        inv_norm = 1.0 / jnp.sum(norm, axis=0, keepdims=True)
        for i in range(2):
            row = inv_norm[:, i * BLK : (i + 1) * BLK]
            by_row = jnp.broadcast_to(row, (BLK, BLK)).T
            part = pl.ds((2 * hp + i) * BLK, BLK)
            qn[u, part, :] = (qs[u, part, :].astype(F32) * by_row).astype(BF)
            dn[u, part, :] = (ds_rows[u, part, :].astype(F32) * by_row).astype(BF)
        inv_norms.append(inv_norm)
    return inv_norms


def dscores_of(u, inv_norms, ds_rows, vg, s_scr, dp_scr, ds_scr):
    for hp in range(2):
        wide = pl.ds(hp * 256, 256)
        do2 = ds_rows[u, wide, :]
        mixed = jnp.zeros((8, 256), F32)
        for t0, t1 in CHUNKS:
            dp = nt_dot(vg[u, pl.ds(t0 * BLK, (t1 - t0) * BLK), :], do2)
            for t in range(t0, t1):
                tile = pl.ds(t * BLK, BLK)
                dpt = dp[(t - t0) * BLK : (t - t0 + 1) * BLK]
                dp_scr[tile, wide] = dpt
                mixed = mixed + jnp.sum(
                    (s_scr[u, tile, wide] * dpt).reshape(16, 8, 256), axis=0
                )
        delta = jnp.sum(mixed, axis=0, keepdims=True) * inv_norms[hp]
        for t in range(WIN):
            tile = pl.ds(t * BLK, BLK)
            ds_scr[u, tile, wide] = (s_scr[u, tile, wide] * (dp_scr[tile, wide] - delta)).astype(BF)


def query_grads(dq_ref, kg, ds_scr, norms):
    for u in range(2):
        for hp in range(2):
            dqt = lax.dot_general(
                kg[u], ds_scr[u, :, pl.ds(hp * 256, 256)],
                (((0,), (0,)), ((), ())), preferred_element_type=F32,
            ) * (norms[u][hp] * SCALE)
            for i in range(2):
                piece = dqt[:, i * BLK : (i + 1) * BLK].T
                dq_ref[pl.ds(u * BLK, BLK), pl.ds((2 * hp + i) * HD, HD)] = piece.astype(BF)


def window_terms(u, source, weights, w_scr):
    for t0, t1 in CHUNKS:
        part = jnp.dot(
            source[u, pl.ds(t0 * BLK, (t1 - t0) * BLK), :], weights[u], preferred_element_type=F32
        )
        w_scr[u, pl.ds(t0, t1 - t0)] = part.reshape(t1 - t0, BLK, HD)


def assemble(ctx, span_ref, kind, core, w_scr, terms):
    base = [span_ref[2 * ctx + u] - (WIN - 1) for u in range(2)]
    for i in range(16):
        xx, lo, h = i // 4, (i // 2) % 2, i % 2
        where = span_ref[xx * 8 + lo * 4 + core * 2 + h]
        total = None
        for u in range(2):
            t = where - base[u]
            piece = w_scr[u, jnp.where((t >= 0) & (t < WIN), t, WIN)]
            total = piece if total is None else total + piece
        if kind == 0:
            total = total * SCALE
        terms[xx, lo, h] = total.astype(BF)


class Stream:
    def __init__(self, me, mail, kind, theirs, mine, r0, a1, b1, a2, b2, own, sem, result):
        self.me, self.mail, self.kind = me, mail, kind
        self.theirs, self.mine, self.r0 = theirs, mine, r0
        self.a1, self.b1, self.a2, self.b2 = a1, b1, a2, b2
        self.own, self.sem, self.result = own, sem, result

    def to_sibling(self):
        self.half = self.mail.post(self.theirs, self.r0, self.me.at(dc=1))

    def first_leg(self):
        me, mine = self.me, self.mine
        self.half.wait_recv()
        for xx in range(4):
            mine[xx] = (mine[xx].astype(F32) + self.r0[xx].astype(F32)).astype(BF)
        self.leg1 = []
        for i, d in enumerate((2, 1, -1)):
            x = (me.x + d + 4) % 4
            y = (me.y + d + 4) % 4
            self.leg1.append(
                self.mail.post(mine.at[x, :, :, pl.ds(0, 64)], self.a1.at[i], me.at(dx=d))
            )
            self.leg1.append(
                self.mail.post(mine.at[:, y % 2, y // 2, pl.ds(64, 64)], self.b1.at[i], me.at(dy=d))
            )

    def second_leg(self):
        me, mine = self.me, self.mine
        for copy in self.leg1:
            copy.wait_recv()
        own_a = mine.at[me.x, :, :, pl.ds(0, 64)]
        own_b = mine.at[:, me.ylo, me.yhi, pl.ds(64, 64)]
        for own, got in ((own_a, self.a1), (own_b, self.b1)):
            total = own[...].astype(F32)
            for i in range(3):
                total = total + got[i].astype(F32)
            own[...] = total.astype(BF)
        self.leg2 = []
        for i, d in enumerate((2, 1, -1)):
            x = (me.x + d + 4) % 4
            y = (me.y + d + 4) % 4
            self.leg2.append(
                self.mail.post(
                    mine.at[me.x, y % 2, y // 2, pl.ds(0, 64)], self.a2.at[i], me.at(dy=d)
                )
            )
            self.leg2.append(
                self.mail.post(
                    mine.at[x, me.ylo, me.yhi, pl.ds(64, 64)], self.b2.at[i], me.at(dx=d)
                )
            )

    def spot(self, k, dz):
        half = self.me.yhi if k == 0 else 1 - self.me.yhi
        return self.result.at[self.kind, (self.me.z + dz + 8) % 8, half]

    def over(self, dz):
        return self.mail.post(self.spot(0, dz), self.spot(0, dz), self.me.at(dy=2))

    def finish(self):
        me, mine = self.me, self.mine
        for copy in self.leg2:
            copy.wait_recv()
        for rows, got in ((pl.ds(0, 64), self.a2), (pl.ds(64, 64), self.b2)):
            total = mine[me.x, me.ylo, me.yhi, rows].astype(F32)
            for i in range(3):
                total = total + got[i].astype(F32)
            self.own[rows] = total.astype(BF)
        self.kept = pltpu.make_async_copy(self.own, self.spot(0, 0), self.sem)
        self.kept.start()
        self.swaps = [self.mail.post(self.own, self.spot(0, 0), me.at(dy=2))]
        self.direct = [
            (-dz, self.mail.post(self.own, self.spot(0, 0), me.at(dz=dz)))
            for dz in (4, 3, -3, 2, -2, 1, -1)
        ]

    def swapped(self):
        self.swaps[0].wait_recv()
        self.near = [
            self.mail.post(self.spot(1, 0), self.spot(1, 0), self.me.at(dz=dz)) for dz in (1, -1)
        ]

    def spread(self):
        for dz, copy in self.direct:
            copy.wait_recv()
            if abs(dz) != 1:
                self.swaps.append(self.over(dz))

    def last(self):
        self.kept.wait()
        for copy in self.swaps[1:] + self.near:
            copy.wait_recv()


VMEM = pl.BlockSpec(memory_space=pltpu.VMEM)
SMEM = pl.BlockSpec(memory_space=pltpu.SMEM)
ANY = pl.BlockSpec(memory_space=pl.ANY)
LIMIT = 56 * 2**20


def kernel(
    q_ref, k_ref, v_ref, do_ref, span_ref, seg_ref, dq_ref, result,
    send, recv, local_sem, q_rows, do_rows, dq_rows, kbuf, vbuf, inv, qs, ds_rows, qn, dn, kg, vg,
    s_scr, dp_scr, p_scr, ds_scr, w_scr, theirs, mine, r0, a1, b1, a2, b2, own,
):
    me = Place()
    greet(
        [me.at(dx=1), me.at(dx=-1), me.at(dx=2), me.at(dy=1), me.at(dy=-1), me.at(dy=2)]
        + [me.at(dc=1)]
        + [me.at(dz=dz) for dz in (1, -1, 2, -2, 3, -3, 4)]
    )
    mail = Mail(send, recv)
    gk = Gather(me, mail, k_ref.at[me.z], kbuf, local_sem.at[0])
    gv = Gather(me, mail, v_ref.at[me.z], vbuf, local_sem.at[1])
    gk.own_x()
    gk.own_y()
    gv.own_x()
    loads = [
        pltpu.make_async_copy(q_ref, q_rows, local_sem.at[2]),
        pltpu.make_async_copy(do_ref, do_rows, local_sem.at[3]),
    ]
    for load in loads:
        load.start()
    prepare(span_ref, inv, w_scr)
    for load in loads:
        load.wait()
    stack_heads(q_rows, do_rows, qs, ds_rows)
    gk.from_x(0)
    gk.from_x(1)
    gv.own_y()
    gk.from_y()
    gk.from_x(2)
    gv.from_x(0)
    gv.from_x(1)
    gk.from_far(0, 4)
    gv.from_y()
    gv.from_x(2)
    gk.from_far(4, 6)
    gk.complete()
    ctx = me.ctx
    window(ctx, 0, span_ref, inv, kbuf, kg)
    norms = [probs_of(ctx, 0, span_ref, seg_ref, qs, ds_rows, qn, dn, kg, s_scr, p_scr)]
    gv.from_far(0, 6)
    window_terms(0, p_scr, dn, w_scr)
    window(ctx, 1, span_ref, inv, kbuf, kg)
    norms.append(probs_of(ctx, 1, span_ref, seg_ref, qs, ds_rows, qn, dn, kg, s_scr, p_scr))
    window_terms(1, p_scr, dn, w_scr)
    dk, dv = (
        Stream(
            me, mail, kind, theirs.at[kind], mine.at[kind], r0.at[kind], a1.at[kind],
            b1.at[kind], a2.at[kind], b2.at[kind], own.at[kind], local_sem.at[4 + kind], result,
        )
        for kind in range(2)
    )
    assemble(ctx, span_ref, 1, 1 - me.core, w_scr, dv.theirs)
    dv.to_sibling()
    assemble(ctx, span_ref, 1, me.core, w_scr, dv.mine)
    gv.complete()
    window(ctx, 0, span_ref, inv, vbuf, vg)
    dscores_of(0, norms[0], ds_rows, vg, s_scr, dp_scr, ds_scr)
    dv.first_leg()
    window_terms(0, ds_scr, qn, w_scr)
    window(ctx, 1, span_ref, inv, vbuf, vg)
    dscores_of(1, norms[1], ds_rows, vg, s_scr, dp_scr, ds_scr)
    window_terms(1, ds_scr, qn, w_scr)
    assemble(ctx, span_ref, 0, 1 - me.core, w_scr, dk.theirs)
    dk.to_sibling()
    assemble(ctx, span_ref, 0, me.core, w_scr, dk.mine)
    dv.second_leg()
    dk.first_leg()
    query_grads(dq_rows, kg, ds_scr, norms)
    leave = pltpu.make_async_copy(dq_rows, dq_ref, local_sem.at[6])
    leave.start()
    dv.finish()
    dk.second_leg()
    dv.swapped()
    dk.finish()
    dv.spread()
    dk.swapped()
    dk.spread()
    dv.last()
    dk.last()
    leave.wait()
    mail.drain()


def cast_kernel(result, dq_in, dk, dv, dq_out, narrow, wide, passing, sem_in, sem_out):
    outs = (dk, dv)
    loads, stores = [], []
    for i in range(8):
        part = pl.ds(2 * (i % 4), 2)
        copy = pltpu.make_async_copy(
            result.at[i // 4, part], narrow.at[i // 4, part], sem_in.at[i]
        )
        copy.start()
        loads.append(copy)
    inward = pltpu.make_async_copy(dq_in, passing, sem_in.at[8])
    inward.start()
    for i in range(8):
        part = pl.ds(2 * (i % 4), 2)
        loads[i].wait()
        wide[i // 4, part] = narrow[i // 4, part].astype(F32)
        copy = pltpu.make_async_copy(wide.at[i // 4, part], outs[i // 4].at[part], sem_out.at[i])
        copy.start()
        stores.append(copy)
    inward.wait()
    outward = pltpu.make_async_copy(passing, dq_out, sem_out.at[8])
    outward.start()
    for copy in stores:
        copy.wait()
    outward.wait()


def per_device(queries, keys, values, d_out, span_order, segments):
    keys = keys.reshape(8, 2, BLK, HD)
    values = values.reshape(8, 2, BLK, HD)
    dq, result = pl.pallas_call(
        kernel,
        out_shape=[
            jax.ShapeDtypeStruct((256, 512), BF),
            jax.ShapeDtypeStruct((2, 8, 2, BLK, HD), BF),
        ],
        in_specs=[ANY, ANY, ANY, ANY, SMEM, VMEM],
        out_specs=[ANY, ANY],
        scratch_shapes=[
            pltpu.SemaphoreType.DMA((112,)),
            pltpu.SemaphoreType.DMA((112,)),
            pltpu.SemaphoreType.DMA((7,)),
            pltpu.VMEM((256, 512), BF),
            pltpu.VMEM((256, 512), BF),
            pltpu.VMEM((256, 512), BF),
            pltpu.VMEM((32, BLK, HD), BF),
            pltpu.VMEM((32, BLK, HD), BF),
            pltpu.SMEM((32,), jnp.int32),
            pltpu.VMEM((2, COLS, HD), BF),
            pltpu.VMEM((2, COLS, HD), BF),
            pltpu.VMEM((2, COLS, HD), BF),
            pltpu.VMEM((2, COLS, HD), BF),
            pltpu.VMEM((2, WIN * BLK, HD), BF),
            pltpu.VMEM((2, WIN * BLK, HD), BF),
            pltpu.VMEM((2, WIN * BLK, COLS), F32),
            pltpu.VMEM((WIN * BLK, COLS), F32),
            pltpu.VMEM((2, WIN * BLK, COLS), BF),
            pltpu.VMEM((2, WIN * BLK, COLS), BF),
            pltpu.VMEM((2, WIN + 1, BLK, HD), F32),
            pltpu.VMEM((2, 4, 2, 2, BLK, HD), BF),
            pltpu.VMEM((2, 4, 2, 2, BLK, HD), BF),
            pltpu.VMEM((2, 4, 2, 2, BLK, HD), BF),
            pltpu.VMEM((2, 3, 2, 2, 64, HD), BF),
            pltpu.VMEM((2, 3, 4, 64, HD), BF),
            pltpu.VMEM((2, 3, 64, HD), BF),
            pltpu.VMEM((2, 3, 64, HD), BF),
            pltpu.VMEM((2, BLK, HD), BF),
        ],
        compiler_params=pltpu.CompilerParams(
            collective_id=0, has_side_effects=True, vmem_limit_bytes=LIMIT
        ),
        name="backward",
    )(queries, keys, values, d_out, span_order, segments.reshape(32, BLK))
    dk, dv, dq = pl.pallas_call(
        cast_kernel,
        out_shape=[
            jax.ShapeDtypeStruct((8, 2, BLK, HD), F32),
            jax.ShapeDtypeStruct((8, 2, BLK, HD), F32),
            jax.ShapeDtypeStruct((256, 512), BF),
        ],
        in_specs=[ANY, ANY],
        out_specs=[ANY, ANY, ANY],
        scratch_shapes=[
            pltpu.VMEM((2, 8, 2, BLK, HD), BF),
            pltpu.VMEM((2, 8, 2, BLK, HD), F32),
            pltpu.VMEM((256, 512), BF),
            pltpu.SemaphoreType.DMA((9,)),
            pltpu.SemaphoreType.DMA((9,)),
        ],
        compiler_params=pltpu.CompilerParams(vmem_limit_bytes=LIMIT),
        name="widen",
    )(result, dq)
    return (dq, dk.reshape(8, 256, HD), dv.reshape(8, 256, HD))


def solution(mesh):
    return jax.shard_map(
        per_device,
        mesh=mesh,
        in_specs=(
            P("ctx", "tp"),
            P(None, "ctx", None),
            P(None, "ctx", None),
            P("ctx", "tp"),
            P(),
            P(),
        ),
        out_specs=(P("ctx", "tp"), P(None, "ctx", None), P(None, "ctx", None)),
        check_vma=False,
    )
```
